32 devices in a mesh: seq: 8 (over z, x), tp: 4 (over y, core).
Axes of the slice: x: 2, y: 2, z: 4, core: 2. Of those that a mesh axis runs over, the one named last changes fastest.
Arguments:
- tokens: bfloat16 [16384, 1024], P(('seq', 'tp')), may hold values from -6 to 6
- segment_ids: int32 [32, 512], P('seq'), may hold values from 0 to 7, never falling along the last dimension, each value on 1 to 256 neighbouring positions
- qkv_weight: bfloat16 [3, 1024, 1024], P(None, None, 'tp'), may hold values from -0.1875 to 0.1875
- out_weight: bfloat16 [1024, 1024], P('tp'), may hold values from -1.5 to 1.5
- up_weight: bfloat16 [1024, 4096], P(None, 'tp'), may hold values from -0.1875 to 0.1875
- down_weight: bfloat16 [4096, 1024], P('tp'), may hold values from -0.09375 to 0.09375
- gain_attn: float32 [1024], replicated, may hold values from 0.5 to 1.5
- shift_attn: float32 [1024], replicated, may hold values from -3 to 3
- gain_ffn: float32 [1024], replicated, may hold values from 0.5 to 1.5
- shift_ffn: float32 [1024], replicated, may hold values from -3 to 3
- cotangent: bfloat16 [16384, 1024], P(('seq', 'tp')), may hold values from -6 to 6
Outputs:
- mixed: bfloat16 [16384, 1024], P(('seq', 'tp'))
- token_grad: float32 [16384, 1024], P(('seq', 'tp'))
- qkv_grad: float32 [3, 1024, 1024], P(None, 'seq', 'tp')
- out_grad: float32 [1024, 1024], P('tp', 'seq')
- up_grad: float32 [1024, 4096], P('seq', 'tp')
- down_grad: float32 [4096, 1024], P('tp', 'seq')
- norm_grads: float32 [4, 1024], P(None, ('seq', 'tp'))
The draws below stay inside these ranges and needn't reach their ends.
Inputs may be any that keep to these rules, and one draw needn't show every extreme that they name: `segment_ids`: in each packed row the ids never fall, each segment has 1 to 256 tokens, and some segment has exactly 256.
All inputs are finite; a program needn't handle non-finite values.
Results may differ from the reference program's by a relative error of at most 0.02.
Values may be sent and summed in bfloat16 or wider, within the bound.
No kernel may reach another device: no remote copies, remote signals or barrier semaphores. Data moves between devices by JAX's collectives and lax.ppermute only.
A program may use at most 256 MiB of HBM per device.

```python
import math
import jax
import jax.numpy as jnp
import numpy as np
from jax import lax

D = 1024
HEADS = 16
FF = 4096
PACK = 512
HDIM = 64
TOKENS = 16384
ROWS = 32
SEGS = 8


def with_spikes(values, rng, source, target, shards_of, factor):
    owner, partner = [(jnp.arange(values.shape[position]) // (values.shape[position] // shards_of)).reshape([-1 if axis == position else 1 for axis in range(values.ndim)]) for position in (source, target)]
    chosen = jax.random.permutation(rng, shards_of)[partner]
    strong = (owner == chosen) | (owner == (partner + shards_of // 2) % shards_of)
    return jnp.where(strong, factor * values, values)


def levels(stream_key, shape, shards, least, high):
    loudness, own = 1.0, jax.random.fold_in(stream_key, 6)
    for dim, blocks in shards:
        steps = jnp.exp(jax.random.uniform(jax.random.fold_in(own, dim), (blocks,), jnp.float32, least / len(shards), high / len(shards)))
        loudness = loudness * jnp.repeat(steps, shape[dim] // blocks).reshape([-1 if axis == dim else 1 for axis in range(len(shape))])
    return loudness


def profile(number_of, total, limit, slope):
    portions = [(1 << 20) // math.isqrt(grade ** slope) + 1 for grade in range(2, number_of + 1)]
    rest, given = total - limit - (number_of - 1), [1] * (number_of - 1)
    while rest > 0:
        movable = [i for i in range(number_of - 1) if given[i] < limit]
        mass, budget = sum([portions[i] for i in movable]), rest
        for i in movable:
            addition = min(limit - given[i], max(1, budget * portions[i] // mass), rest)
            given[i] = given[i] + addition
            rest = rest - addition
    return np.array([limit] + given)


def ragged_sizes(stream_key, number_of, total, limit, lean):
    if number_of == 2:
        one = jax.random.randint(stream_key, (), max(1, total - limit), min(limit, total - 1) + 1)
        return jnp.stack([one, total - one])
    sizes = jnp.asarray(profile(number_of, total, limit, lean), jnp.int32)
    couples = (number_of - 1) // 2
    donor, receiver = sizes[1:1 + 2 * couples:2], sizes[2:2 + 2 * couples:2]
    room = jnp.minimum(donor - 1, limit - receiver)
    moved = jax.random.randint(jax.random.fold_in(stream_key, 1), (couples,), 0, 1 << 20) % (room + 1)
    sizes = sizes.at[1:1 + 2 * couples:2].set(donor - moved).at[2:2 + 2 * couples:2].set(receiver + moved)
    return sizes[jax.random.permutation(jax.random.fold_in(stream_key, 2), number_of)]


def normal_values(rng, dims, deviation, most, shards=(), held_as=jnp.bfloat16):
    result = deviation * jax.random.normal(rng, dims, jnp.float32)
    if shards:
        result = result * levels(rng, dims, shards, -0.22, 0.18)
    return jnp.clip(result, -most, most).astype(held_as)


def heavy_noise(own_key, dims, scale, reach, pieces, heavy, dtype=jnp.bfloat16):
    entries = scale * jax.random.normal(own_key, dims, jnp.float32)
    if pieces:
        entries = entries * levels(own_key, dims, pieces, -0.22, 0.18)
    return jnp.clip(with_spikes(entries, jax.random.fold_in(own_key, 3), *heavy), -reach, reach).astype(dtype)


def setup_inputs(seed: int = 0) -> dict:
    splits = jax.random.split(jax.random.key(seed), 12)
    tokens = normal_values(splits[0], (TOKENS, D), 1.0, 6.0, ((0, 32),))
    segment_ids = jax.vmap(lambda own: jnp.searchsorted(jnp.cumsum(ragged_sizes(own, SEGS, PACK, PACK // 2, 2)), jnp.arange(PACK), side="right"))(jax.random.split(splits[1], ROWS)).reshape((ROWS, PACK)).astype(jnp.int32)
    qkv_weight = normal_values(splits[2], (3, D, D), D ** -0.5, 0.1875, ((2, 4),))
    out_weight = normal_values(splits[3], (D, D), (D // 64) ** -0.5, 1.5, ((0, 4),))
    up_weight = normal_values(splits[4], (D, FF), D ** -0.5, 0.1875, ((1, 4),))
    down_weight = normal_values(splits[5], (FF, D), FF ** -0.5, 0.09375, ((0, 4),))
    gain_attn = jnp.clip(1.0 + 0.1 * jax.random.normal(splits[6], (D,), jnp.float32), 0.5, 1.5)
    shift_attn = normal_values(splits[7], (D,), 0.5, 3.0, (), jnp.float32)
    gain_ffn = jnp.clip(1.0 + 0.1 * jax.random.normal(splits[8], (D,), jnp.float32), 0.5, 1.5)
    shift_ffn = normal_values(splits[9], (D,), 0.5, 3.0, (), jnp.float32)
    cotangent = heavy_noise(splits[10], (TOKENS, D), 1.0, 6.0, ((0, 32),), (0, 1, 32, 2.75))
    return {"tokens": tokens, "segment_ids": segment_ids, "qkv_weight": qkv_weight, "out_weight": out_weight, "up_weight": up_weight, "down_weight": down_weight, "gain_attn": gain_attn, "shift_attn": shift_attn, "gain_ffn": gain_ffn, "shift_ffn": shift_ffn, "cotangent": cotangent}


highest = lax.Precision.HIGHEST

@jax.custom_vjp
def low(v):
    return lax.optimization_barrier(v.astype(jnp.bfloat16)).astype(jnp.float32)

@jax.custom_vjp
def low_back(v):
    return v

def low_keep(v):
    return (low(v), None)

def low_pass(kept, grad):
    return (grad,)

def back_keep(v):
    return (v, None)

def back_low(kept, grad):
    return (low(grad),)
low.defvjp(low_keep, low_pass)
low_back.defvjp(back_keep, back_low)

def normalize(values, gain, shift):
    center = values - lax.optimization_barrier(jnp.mean(values, axis=-1, keepdims=True))
    spread = lax.optimization_barrier(jnp.mean(center * center, axis=-1, keepdims=True))
    return center * lax.rsqrt(spread + 1e-12) * gain + shift

def attend_row(items):
    queries, keys, values, seg_row = items
    scores = jnp.einsum('qhd,khd->hqk', queries, keys, precision=highest) * HDIM ** (-0.5)
    scores = low_back(scores)
    same = seg_row[:, None] == seg_row[None, :]
    scores = jnp.where(same[None], scores, -1000000000.0)
    probs = jax.nn.softmax(scores, axis=-1)
    return jnp.einsum('hqk,khd->qhd', low(probs), values, precision=highest)

def layer(inputs, seg_block, qkv_weight, out_weight, up_weight, down_weight, gain_attn, shift_attn, gain_ffn, shift_ffn):
    count = inputs.shape[0]
    blocks = count // PACK
    shaped = []
    for which in range(3):
        projected = low_back(low(jnp.dot(inputs, qkv_weight[which], precision=highest)))
        shaped.append(projected.reshape(blocks, PACK, HEADS, HDIM))
    context = lax.map(jax.checkpoint(attend_row), (shaped[0], shaped[1], shaped[2], seg_block))
    context = low_back(low(context.reshape(count, D)))
    attn = low_back(jnp.dot(context, out_weight, precision=highest))
    normed = normalize(inputs + attn, gain_attn, shift_attn)
    up_value = low_back(jnp.dot(low(normed), up_weight, precision=highest))
    active = low(jax.nn.gelu(up_value, approximate=False))
    ffn = low_back(jnp.dot(active, down_weight, precision=highest))
    return normalize(normed + ffn, gain_ffn, shift_ffn)

def reference(tokens, segment_ids, qkv_weight, out_weight, up_weight, down_weight, gain_attn, shift_attn, gain_ffn, shift_ffn, cotangent):
    per_step = math.gcd(ROWS, max(1, 4096 // PACK))
    groups = ROWS // per_step
    inputs_all = tokens.astype(jnp.float32).reshape(groups, per_step * PACK, D)
    segs_all = segment_ids.reshape(groups, per_step, PACK)
    cots_all = cotangent.astype(jnp.float32).reshape(groups, per_step * PACK, D)
    params = (qkv_weight.astype(jnp.float32), out_weight.astype(jnp.float32), up_weight.astype(jnp.float32), down_weight.astype(jnp.float32), gain_attn, shift_attn, gain_ffn, shift_ffn)

    def step(summed, items):
        inputs, seg_block, cot_block = items

        def apply(values, *weights):
            return layer(values, seg_block, *weights)
        output, pullback = jax.vjp(apply, inputs, *params)
        grads = pullback(cot_block)
        summed = tuple((first + second for first, second in zip(summed, grads[1:])))
        return (summed, (output.astype(jnp.bfloat16), grads[0]))
    starting = tuple((jnp.zeros_like(weight) for weight in params))
    summed, (outputs, input_grads) = lax.scan(step, starting, (inputs_all, segs_all, cots_all))
    norm_grads = jnp.stack([summed[4], summed[5], summed[6], summed[7]])
    return (outputs.reshape(TOKENS, D), input_grads.reshape(TOKENS, D), summed[0], summed[1], summed[2], summed[3], norm_grads)
```

```python
import functools

import jax
import jax.numpy as jnp
from jax import lax
from jax.experimental import pallas as pl
from jax.experimental.pallas import tpu as pltpu
from jax.sharding import PartitionSpec as P

HDIM = 64
LANE = 128
BF = jnp.bfloat16
F32 = jnp.float32
SCALE = HDIM ** (-0.5)
MASKED = -1000000000.0


def dot(left, right):
    return jnp.dot(left, right, preferred_element_type=F32)


def dot_nt(left, right):
    return lax.dot_general(left, right, (((1,), (1,)), ((), ())), preferred_element_type=F32)


def dot_tn(left, right):
    return lax.dot_general(left, right, (((0,), (0,)), ((), ())), preferred_element_type=F32)


def call(kernel, outs, smem, args, name):
    out_shape = [jax.ShapeDtypeStruct(shape, dtype) for shape, dtype in outs]
    specs = [pl.BlockSpec(memory_space=pltpu.SMEM)] * len(smem)
    specs += [pl.BlockSpec(memory_space=pltpu.VMEM)] * len(args)
    return pl.pallas_call(
        kernel,
        out_shape=out_shape,
        in_specs=specs,
        out_specs=[pl.BlockSpec(memory_space=pltpu.VMEM)] * len(outs),
        compiler_params=pltpu.CompilerParams(vmem_limit_bytes=50 * 1024 * 1024),
        name=name,
    )(*smem, *args)


def store_turned(pos_ref, out_ref, values):
    for block in range(values.shape[1] // LANE):
        start = pl.multiple_of(pos_ref[block] * LANE, LANE)
        out_ref[pl.ds(start, LANE), :] = values[:, block * LANE : (block + 1) * LANE].T


def turn_kernel(pos_ref, x_ref, out_ref):
    store_turned(pos_ref, out_ref, x_ref[...])


def mean_of(values):
    return jnp.mean(values, axis=-1, keepdims=True)


def bias_of(seg_col, seg_row):
    return jnp.where(seg_col == seg_row, 0.0, MASKED)


def attn_fwd_kernel(units, first, last, pos_ref, *refs):
    refs = list(refs)
    tokens_ref, col_ref, row_ref = refs[:3]
    del refs[:3]
    weights = [(refs.pop(0), refs.pop(0)) for _ in range(units)]
    acc_ref = None if first else refs.pop(0)
    if last:
        gain_ref, shift_ref = refs.pop(0), refs.pop(0)
    saved = [(refs.pop(0), refs.pop(0), refs.pop(0)) for _ in range(units)]
    tokens = tokens_ref[...]
    bias = bias_of(col_ref[...], row_ref[...])
    lane = lax.broadcasted_iota(jnp.int32, (1, LANE), 1)
    line = lax.broadcasted_iota(jnp.int32, (LANE, 1), 0)
    contexts = []
    for (wqkv_ref, wo_ref), (qkv_ref, ctx_ref, lse_ref) in zip(weights, saved):
        qkv = dot(tokens, wqkv_ref[...]).astype(BF)
        qkv_ref[...] = qkv
        query, key, value = (qkv[:, i * LANE : (i + 1) * LANE] for i in range(3))
        query = query * jnp.asarray(SCALE, BF)
        value_t = value.T
        parts = []
        for head in range(2):
            mine = lane >= HDIM if head else lane < HDIM
            scores = dot_nt(jnp.where(mine, key, jnp.zeros_like(key)), query) + bias
            peak = jnp.max(scores, axis=0, keepdims=True)
            raw = jnp.exp(scores - peak)
            summed = jnp.sum(raw, axis=0, keepdims=True)
            lse_ref[head : head + 1, :] = peak + jnp.log(summed)
            prob = (raw * (1.0 / summed)).astype(BF)
            parts.append(dot(value_t, prob))
        context = jnp.where(line < HDIM, parts[0], parts[1]).astype(BF).T
        ctx_ref[...] = context
        contexts.append(context)
    both = jnp.concatenate(contexts, axis=1)
    total = dot(both, jnp.concatenate([wo[...] for _, wo in weights], axis=0))
    if not first:
        total = total + acc_ref[...]
    if not last:
        refs[0][...] = total
        return
    hat_ref, inv_ref, low_ref, turned_ref = refs
    pre = tokens.astype(F32) + total
    center = pre - mean_of(pre)
    inv = lax.rsqrt(mean_of(center * center) + 1e-12)
    hat = center * inv
    hat_ref[...] = hat
    inv_ref[...] = jnp.broadcast_to(inv, inv_ref.shape)
    low = (hat * gain_ref[...] + shift_ref[...]).astype(BF)
    low_ref[...] = low
    store_turned(pos_ref, turned_ref, low)


def ffn_fwd_kernel(units, first, last, pos_ref, *refs):
    refs = list(refs)
    low_ref = refs.pop(0)
    weights = [(refs.pop(0), refs.pop(0)) for _ in range(units)]
    acc_ref = None if first else refs.pop(0)
    if last:
        hat_ref, gain1_ref, shift1_ref, gain2_ref, shift2_ref, cot_ref = refs[:6]
        del refs[:6]
    saved = [(refs.pop(0), refs.pop(0)) for _ in range(units)]
    low = low_ref[...]
    total = None
    for (wu_ref, wd_ref), (act_ref, slope_ref) in zip(weights, saved):
        up = dot(low, wu_ref[...])
        phi_big = 0.5 + 0.5 * lax.erf(up * (0.5 ** 0.5))
        phi_small = jnp.exp(up * up * -0.5) * 0.3989422804014327
        slope_ref[...] = phi_big + up * phi_small
        act = (up * phi_big).astype(BF)
        act_ref[...] = act
        part = dot(act, wd_ref[...])
        total = part if total is None else total + part
    if not first:
        total = total + acc_ref[...]
    if not last:
        refs[0][...] = total
        return
    mixed_ref, dpre_ref, dffn_ref, turned_ref, gg_ref, gs_ref = refs
    gain2 = gain2_ref[...]
    pre = hat_ref[...] * gain1_ref[...] + shift1_ref[...] + total
    center = pre - mean_of(pre)
    inv = lax.rsqrt(mean_of(center * center) + 1e-12)
    hat = center * inv
    mixed_ref[...] = (hat * gain2 + shift2_ref[...]).astype(BF)
    cot = cot_ref[...].astype(F32)
    gg_ref[...] = jnp.sum(cot * hat, axis=0, keepdims=True)
    gs_ref[...] = jnp.sum(cot, axis=0, keepdims=True)
    scaled = cot * gain2
    dpre = (scaled - mean_of(scaled) - hat * mean_of(scaled * hat)) * inv
    dpre_ref[...] = dpre
    dffn = dpre.astype(BF)
    dffn_ref[...] = dffn
    store_turned(pos_ref, turned_ref, dffn)


def ffn_bwd_kernel(has_recv, last, pos_ref, *refs):
    refs = list(refs)
    dffn_ref, dffn_t_ref, low_t_ref = refs[:3]
    del refs[:3]
    weights = [[refs.pop(0) for _ in range(4)] for _ in range(2)]
    acc_ref = refs.pop(0)
    recv = [[refs.pop(0) for _ in range(3)] for _ in range(2)] if has_recv else None
    if last:
        hat_ref, inv_ref, gain_ref = refs[:3]
        del refs[:3]
    outs = [[refs.pop(0) for _ in range(3)] for _ in range(2)]
    dffn, dffn_t, low_t = dffn_ref[...], dffn_t_ref[...], low_t_ref[...]
    half = low_t.shape[0] // 2
    total = acc_ref[...]
    for unit in range(2):
        wu_ref, wd_ref, act_ref, slope_ref = weights[unit]
        down_ref, lo_ref, hi_ref = outs[unit]
        d_up = (dot_nt(dffn, wd_ref[...]) * slope_ref[...]).astype(BF)
        total = total + dot_nt(d_up, wu_ref[...])
        down = dot(dffn_t, act_ref[...])
        up_hi = dot(low_t[half:], d_up)
        up_lo = dot(low_t[:half], d_up)
        if has_recv:
            down = down + recv[unit][0][...].astype(F32)
            up_lo = up_lo + recv[unit][1][...].astype(F32)
            up_hi = up_hi + recv[unit][2][...].astype(F32)
        down_ref[...] = down.astype(BF)
        lo_ref[...] = up_lo.astype(BF)
        hi_ref[...] = up_hi.astype(BF)
    if not last:
        refs[0][...] = total
        return
    dpre_ref, datt_ref, turned_ref, gg_ref, gs_ref = refs
    hat = hat_ref[...]
    gg_ref[...] = jnp.sum(total * hat, axis=0, keepdims=True)
    gs_ref[...] = jnp.sum(total, axis=0, keepdims=True)
    scaled = total * gain_ref[...]
    inv = inv_ref[:, :1]
    dpre = (scaled - mean_of(scaled) - hat * mean_of(scaled * hat)) * inv
    dpre_ref[...] = dpre
    datt = dpre.astype(BF)
    datt_ref[...] = datt
    store_turned(pos_ref, turned_ref, datt)


def attn_bwd_kernel(has_recv, *refs):
    refs = list(refs)
    datt_ref, datt_t_ref, tok_t_ref, col_ref, row_ref = refs[:5]
    del refs[:5]
    units = [[refs.pop(0) for _ in range(5)] for _ in range(2)]
    acc_ref = refs.pop(0)
    recv = [[refs.pop(0) for _ in range(3)] for _ in range(2)] if has_recv else None
    outs = [[refs.pop(0) for _ in range(3)] for _ in range(2)]
    out_acc_ref = refs.pop(0)
    datt, datt_t, tok_t = datt_ref[...], datt_t_ref[...], tok_t_ref[...]
    half = tok_t.shape[0] // 2
    bias = bias_of(col_ref[...], row_ref[...])
    lane = lax.broadcasted_iota(jnp.int32, (1, LANE), 1)
    line = lax.broadcasted_iota(jnp.int32, (LANE, 1), 0)
    wo = jnp.concatenate([unit[1][...] for unit in units], axis=0)
    dctx_all = dot_nt(datt, wo).astype(BF)
    grads = []
    for index, (wqkv_ref, wo_ref, qkv_ref, ctx_ref, lse_ref) in enumerate(units):
        dctx = dctx_all[:, index * LANE : (index + 1) * LANE]
        query, key, value = (qkv_ref[:, i * LANE : (i + 1) * LANE] for i in range(3))
        query = query * jnp.asarray(SCALE, BF)
        key_t = key.T
        parts = []
        for head in range(2):
            mine = lane >= HDIM if head else lane < HDIM
            scores = dot_nt(jnp.where(mine, key, jnp.zeros_like(key)), query) + bias
            prob = jnp.exp(scores - lse_ref[head : head + 1, :])
            d_prob = dot_nt(jnp.where(mine, value, jnp.zeros_like(value)), dctx)
            inner = jnp.sum(prob * d_prob, axis=0, keepdims=True)
            d_scores = (prob * (d_prob - inner)).astype(BF)
            parts.append(
                (dot(key_t, d_scores), dot(d_scores, query), dot(prob.astype(BF), dctx))
            )
        d_query = (jnp.where(line < HDIM, parts[0][0], parts[1][0]) * SCALE).astype(BF).T
        d_key = jnp.where(lane < HDIM, parts[0][1], parts[1][1]).astype(BF)
        d_value = jnp.where(lane < HDIM, parts[0][2], parts[1][2]).astype(BF)
        grads.append(jnp.concatenate([d_query, d_key, d_value], axis=1))
    both = jnp.concatenate(grads, axis=1)
    wqkv = jnp.concatenate([unit[0][...] for unit in units], axis=1)
    out_acc_ref[...] = acc_ref[...] + dot_nt(both, wqkv)
    ctx = jnp.concatenate([unit[3][...] for unit in units], axis=1)
    qkv_grad = dot(tok_t, both)
    out_grad = dot(datt_t, ctx)
    for unit in range(2):
        qk_ref, lo_ref, hi_ref = outs[unit]
        qk = qkv_grad[:, unit * 3 * LANE : (unit * 3 + 2) * LANE]
        vo = jnp.concatenate(
            [
                qkv_grad[:, (unit * 3 + 2) * LANE : (unit * 3 + 3) * LANE],
                out_grad[:, unit * LANE : (unit + 1) * LANE],
            ],
            axis=1,
        )
        lo, hi = vo[:half], vo[half:]
        if has_recv:
            qk = qk + recv[unit][0][...].astype(F32)
            lo = lo + recv[unit][1][...].astype(F32)
            hi = hi + recv[unit][2][...].astype(F32)
        qk_ref[...] = qk.astype(BF)
        lo_ref[...] = lo.astype(BF)
        hi_ref[...] = hi.astype(BF)


def swap(value, axis, bit):
    count = lax.axis_size(axis)
    return lax.ppermute(value, axis, [(i, i ^ bit) for i in range(count)])


def add(*values):
    total = values[0].astype(F32)
    for value in values[1:]:
        total = total + value.astype(F32)
    return total.astype(BF)


def body(
    tokens,
    segment_ids,
    qkv_weight,
    out_weight,
    up_weight,
    down_weight,
    gain_attn,
    shift_attn,
    gain_ffn,
    shift_ffn,
    cotangent,
):
    count, width = tokens.shape
    seq, tp = lax.axis_size("seq"), lax.axis_size("tp")
    me_seq, me_tp = lax.axis_index("seq"), lax.axis_index("tp")
    blocks = width // LANE
    fast = seq == blocks and seq == 8 and tp == 4 and qkv_weight.shape[2] == 2 * LANE
    hidden = up_weight.shape[1] * tp // blocks
    seg = lax.dynamic_slice_in_dim(segment_ids, me_tp, 1, axis=0)
    seg_col = seg.reshape(count, 1)
    gains = [g.reshape(1, width) for g in (gain_attn, shift_attn, gain_ffn, shift_ffn)]
    absolute = jnp.arange(blocks, dtype=jnp.int32)
    side = lax.rem(me_seq, 2)
    if fast:
        rel = absolute ^ me_seq
        pos = (rel & 1) * 4 + ((rel >> 1) & 1) * 2 + (rel >> 2)

        def cut(half):
            at = lax.rem(side + half, 2)
            qkv = lax.dynamic_slice_in_dim(qkv_weight, at * LANE, LANE, axis=2)
            return (
                jnp.concatenate([qkv[0], qkv[1], qkv[2]], axis=1),
                lax.dynamic_slice_in_dim(out_weight, at * LANE, LANE, axis=0),
                lax.dynamic_slice_in_dim(up_weight, at * hidden, hidden, axis=1),
                lax.dynamic_slice_in_dim(down_weight, at * hidden, hidden, axis=0),
            )

        units = {(0, 0): cut(0), (0, 1): cut(1)}
        units[2, 0] = tuple(swap(w, "tp", 2) for w in units[0, 0])
        units[1, 0] = tuple(swap(w, "tp", 1) for w in units[0, 0])
        units[1, 1] = tuple(swap(w, "tp", 1) for w in units[0, 1])
        units[2, 1] = tuple(swap(w, "seq", 1) for w in units[2, 0])
        units[3, 0] = tuple(swap(w, "tp", 1) for w in units[2, 0])
        units[3, 1] = tuple(swap(w, "tp", 1) for w in units[2, 1])
    else:
        pos = absolute
        qkv_all = lax.all_gather(qkv_weight, "tp", axis=2, tiled=True)
        out_all = lax.all_gather(out_weight, "tp", axis=0, tiled=True)
        up_all = lax.all_gather(up_weight, "tp", axis=1, tiled=True)
        down_all = lax.all_gather(down_weight, "tp", axis=0, tiled=True)
        units = {}
        for index in range(blocks):
            cols = slice(index * LANE, (index + 1) * LANE)
            hid = slice(index * hidden, (index + 1) * hidden)
            units[index // 2, index % 2] = (
                jnp.concatenate([qkv_all[i][:, cols] for i in range(3)], axis=1),
                out_all[cols],
                up_all[:, hid],
                down_all[hid],
            )
    pairs = blocks // 2
    if fast:
        groups = [[(0, 0), (0, 1)], [(1, 0), (1, 1)], [(2, 0), (3, 0)], [(2, 1), (3, 1)]]
    else:
        groups = [[(j, 0), (j, 1)] for j in range(pairs)]
    wide = (count, width)

    tok_t = call(turn_kernel, [((width, count), BF)], [pos], [tokens], "turn")[0]
    kept = {}
    total = None
    for number, group in enumerate(groups):
        first, last = number == 0, number == len(groups) - 1
        args = [tokens, seg_col, seg]
        for unit in group:
            args += units[unit][:2]
        if not first:
            args.append(total)
        if last:
            args += gains[:2]
        outs = []
        for unit in group:
            outs += [((count, 3 * LANE), BF), ((count, LANE), BF), ((2, count), F32)]
        if last:
            outs += [(wide, F32), ((count, LANE), F32), (wide, BF), ((width, count), BF)]
        else:
            outs.append((wide, F32))
        res = call(
            functools.partial(attn_fwd_kernel, len(group), first, last),
            outs, [pos], args, f"attn_fwd{number}",
        )
        for index, unit in enumerate(group):
            kept[unit] = tuple(res[index * 3 : index * 3 + 3])
        if last:
            hat, inv, low, low_t = res[-4:]
        else:
            total = res[-1]

    acts = {}
    for number, group in enumerate(groups):
        first, last = number == 0, number == len(groups) - 1
        args = [low]
        for unit in group:
            args += units[unit][2:]
        if not first:
            args.append(total)
        if last:
            args += [hat, *gains, cotangent]
        outs = []
        for unit in group:
            outs += [((count, hidden), BF), ((count, hidden), F32)]
        if last:
            outs += [
                (wide, BF), (wide, F32), (wide, BF), ((width, count), BF),
                ((1, width), F32), ((1, width), F32),
            ]
        else:
            outs.append((wide, F32))
        res = call(
            functools.partial(ffn_fwd_kernel, len(group), first, last),
            outs, [pos], args, f"ffn_fwd{number}",
        )
        for index, unit in enumerate(group):
            acts[unit] = tuple(res[index * 2 : index * 2 + 2])
        if last:
            mixed, d_pre, d_ffn, d_ffn_t, g_gain2, g_shift2 = res[-6:]
        else:
            total = res[-1]

    half = width // 2
    order = [3, 2, 1, 0] if fast else list(range(pairs))
    ffn_g, attn_g = {}, {}
    total = d_pre
    for number, j in enumerate(order):
        last = number == len(order) - 1
        args = [d_ffn, d_ffn_t, low_t]
        for h in range(2):
            args += [*units[j, h][2:], *acts[j, h]]
        args.append(total)
        recv = [swap(g, "tp", 1) for g in ffn_g[j + 1]] if fast and j % 2 == 0 else []
        args += recv
        outs = [((width, hidden), BF), ((half, hidden), BF), ((half, hidden), BF)] * 2
        if last:
            args += [hat, inv, gains[0]]
            outs = outs + [
                (wide, F32), (wide, BF), ((width, count), BF), ((1, width), F32), ((1, width), F32),
            ]
        else:
            outs = outs + [(wide, F32)]
        res = call(
            functools.partial(ffn_bwd_kernel, bool(recv), last), outs, [pos], args, f"ffn_bwd{j}"
        )
        ffn_g[j] = res[:6]
        if last:
            d_pre_one, d_att, d_att_t, g_gain1, g_shift1 = res[6:]
        else:
            total = res[6]

    norm_terms = jnp.concatenate([g_gain1, g_shift1, g_gain2, g_shift2], axis=0)
    norm_grads = lax.psum_scatter(norm_terms, ("seq", "tp"), scatter_dimension=1, tiled=True)

    total = d_pre_one
    for j in order:
        args = [d_att, d_att_t, tok_t, seg_col, seg]
        for h in range(2):
            args += [*units[j, h][:2], *kept[j, h]]
        args.append(total)
        recv = [swap(g, "tp", 1) for g in attn_g[j + 1]] if fast and j % 2 == 0 else []
        args += recv
        outs = [((width, 2 * LANE), BF), ((half, 2 * LANE), BF), ((half, 2 * LANE), BF)] * 2
        outs = outs + [(wide, F32)]
        res = call(
            functools.partial(attn_bwd_kernel, bool(recv)), outs, [], args, f"attn_bwd{j}"
        )
        attn_g[j], total = res[:6], res[6]
    token_grad = total

    if fast:
        quarter, eighth = half // 2, half // 4

        def finish(lo):
            lo = [add(g[:quarter], swap(g[quarter:], "seq", 2)) for g in lo]
            return [
                g[:eighth].astype(F32) + swap(g[eighth:], "seq", 4).astype(F32) for g in lo
            ]

        def reduced(far, near):
            first = [swap(far[i], "tp", 2) for i in (0, 3)]
            lo = [add(near[i][:half], r[:half]) for i, r in zip((0, 3), first)]
            hi = [swap(add(near[i][half:], r[half:]), "seq", 1) for i, r in zip((0, 3), first)]
            one = finish([add(lo[0], hi[1]), add(lo[1], hi[0])])
            far_hi = [swap(far[i], "seq", 1) for i in (2, 5)]
            near_hi = [swap(near[i], "seq", 1) for i in (2, 5)]
            far_lo = [add(far[1], far_hi[1]), add(far[4], far_hi[0])]
            far_lo = [swap(g, "tp", 2) for g in far_lo]
            two = finish(
                [add(near[1], near_hi[1], far_lo[0]), add(near[4], near_hi[0], far_lo[1])]
            )
            return one, two

        def ordered(a, b):
            return jnp.where(side == 0, jnp.concatenate([a, b], 1), jnp.concatenate([b, a], 1))

        down, up = reduced(ffn_g[2], ffn_g[0])
        qk, vo = reduced(attn_g[2], attn_g[0])
        down_grad = ordered(*down).T
        up_grad = ordered(*up)
        qkv_grad = jnp.stack(
            [
                ordered(qk[0][:, :LANE], qk[1][:, :LANE]),
                ordered(qk[0][:, LANE:], qk[1][:, LANE:]),
                ordered(vo[0][:, :LANE], vo[1][:, :LANE]),
            ]
        )
        out_grad = ordered(vo[0][:, LANE:], vo[1][:, LANE:]).T
    else:

        def joined(parts):
            return jnp.concatenate(parts, axis=1)

        def scattered(value, tp_dim, seq_dim):
            value = lax.psum_scatter(value, "tp", scatter_dimension=tp_dim, tiled=True)
            value = lax.psum_scatter(value, "seq", scatter_dimension=seq_dim, tiled=True)
            return value.astype(F32)

        both = [(j, h) for j in range(pairs) for h in (0, 3)]

        def whole(g, j, h):
            return jnp.concatenate([g[j][h + 1], g[j][h + 2]], axis=0)

        down_grad = scattered(joined([ffn_g[j][h] for j, h in both]), 1, 0).T
        up_grad = scattered(joined([whole(ffn_g, j, h) for j, h in both]), 1, 0)
        qk = [attn_g[j][h] for j, h in both]
        vo = [whole(attn_g, j, h) for j, h in both]
        qkv_grad = jnp.stack(
            [
                joined([g[:, :LANE] for g in qk]),
                joined([g[:, LANE:] for g in qk]),
                joined([g[:, :LANE] for g in vo]),
            ]
        )
        qkv_grad = scattered(qkv_grad, 2, 1)
        out_grad = scattered(joined([g[:, LANE:] for g in vo]), 1, 0).T
    return (mixed, token_grad, qkv_grad, out_grad, up_grad, down_grad, norm_grads)


def solution(mesh):
    return jax.shard_map(
        body,
        mesh=mesh,
        in_specs=(
            P(("seq", "tp"), None),
            P("seq", None),
            P(None, None, "tp"),
            P("tp", None),
            P(None, "tp"),
            P("tp", None),
            P(),
            P(),
            P(),
            P(),
            P(("seq", "tp"), None),
        ),
        out_specs=(
            P(("seq", "tp"), None),
            P(("seq", "tp"), None),
            P(None, "seq", "tp"),
            P("tp", "seq"),
            P("seq", "tp"),
            P("tp", "seq"),
            P(None, ("seq", "tp")),
        ),
        check_vma=False,
    )
```

```python
import functools

import jax
import jax.numpy as jnp
from jax import lax
from jax.experimental import pallas as pl
from jax.experimental.pallas import tpu as pltpu
from jax.sharding import PartitionSpec as P

HDIM = 64
LANE = 128
BF = jnp.bfloat16
F32 = jnp.float32
SCALE = HDIM ** (-0.5)
MASKED = -1000000000.0
SIDE = 8


def dot(left, right):
    return jnp.dot(left, right, preferred_element_type=F32)


def dot_nt(left, right):
    return lax.dot_general(left, right, (((1,), (1,)), ((), ())), preferred_element_type=F32)


def everything(ref, scal):
    return ref


class Need:
    def __init__(self, shape, dtype, *parts):
        self.shape, self.dtype, self.parts = tuple(shape), dtype, parts


def need(array):
    return Need(array.shape, array.dtype, (array, everything, everything))


class Loads:
    def __init__(self, needs, refs, bufs, sems, scal):
        self.bufs, self.copies, self.next = bufs, [], 0
        at = 0
        for item, buf in zip(needs, bufs):
            mine = []
            for index, source, target in item.parts:
                copy = pltpu.make_async_copy(
                    source(refs[index], scal), target(buf, scal), sems.at[at]
                )
                copy.start()
                mine.append(copy)
                at += 1
            self.copies.append(mine)

    def take(self):
        self.next += 1
        return self.next - 1

    def get(self, slot):
        for copy in self.copies[slot]:
            copy.wait()
        self.copies[slot] = []
        return self.bufs[slot]

    def pop(self):
        return self.get(self.take())

    def finish(self):
        for slot in range(len(self.copies)):
            self.get(slot)


class Stores:
    def __init__(self, refs, bufs, sems):
        self.refs, self.bufs, self.sems, self.copies = refs, bufs, sems, []
        self.next = 0

    def part(self, slot, value, *where):
        self.bufs[slot][where] = value

    def send(self, slot, *where):
        source, target = self.bufs[slot], self.refs[slot]
        if where:
            source, target = source.at[where], target.at[where]
        copy = pltpu.make_async_copy(source, target, self.sems.at[self.next])
        self.next += 1
        copy.start()
        self.copies.append(copy)

    def put(self, slot, value):
        self.bufs[slot][...] = value
        self.send(slot)

    def finish(self):
        for copy in self.copies:
            copy.wait()


def call(kernel, needs, outs, scal, small, name, flops, sends=None):
    arrays, parts = [], []
    for item in needs:
        fixed = []
        for array, source, target in item.parts:
            index = next((i for i, a in enumerate(arrays) if a is array), None)
            if index is None:
                index = len(arrays)
                arrays.append(array)
            fixed.append((index, source, target))
        parts.append(Need(item.shape, item.dtype, *fixed))
    copies = sum(len(item.parts) for item in parts)
    sends = len(outs) if sends is None else sends

    def run(*refs):
        refs = list(refs)
        scal_ref = refs.pop(0)
        small_refs = [refs.pop(0) for _ in small]
        in_refs = [refs.pop(0) for _ in arrays]
        out_refs = [refs.pop(0) for _ in outs]
        in_bufs = [refs.pop(0) for _ in parts]
        out_bufs = [refs.pop(0) for _ in outs]
        in_sems, out_sems = refs
        loads = Loads(parts, in_refs, in_bufs, in_sems, scal_ref)
        stores = Stores(out_refs, out_bufs, out_sems)
        kernel(scal_ref, small_refs, loads, stores)
        loads.finish()
        stores.finish()

    moved = sum(a.size * a.dtype.itemsize for a in arrays)
    return pl.pallas_call(
        run,
        out_shape=[jax.ShapeDtypeStruct(shape, dtype) for shape, dtype in outs],
        in_specs=[pl.BlockSpec(memory_space=pltpu.SMEM)]
        + [pl.BlockSpec(memory_space=pltpu.VMEM)] * len(small)
        + [pl.BlockSpec(memory_space=pl.ANY)] * len(arrays),
        out_specs=[pl.BlockSpec(memory_space=pl.ANY)] * len(outs),
        scratch_shapes=[pltpu.VMEM(item.shape, item.dtype) for item in parts]
        + [pltpu.VMEM(shape, dtype) for shape, dtype in outs]
        + [pltpu.SemaphoreType.DMA((copies,)), pltpu.SemaphoreType.DMA((max(1, sends),))],
        compiler_params=pltpu.CompilerParams(vmem_limit_bytes=48 * 1024 * 1024),
        cost_estimate=pl.CostEstimate(flops=flops, bytes_accessed=moved, transcendentals=0),
        name=name,
    )(scal, *small, *arrays)


def store_turned(scal, buf, values):
    for block in range(values.shape[1] // LANE):
        start = pl.multiple_of(scal[block] * LANE, LANE)
        buf[pl.ds(start, LANE), :] = values[:, block * LANE : (block + 1) * LANE].T


def block_of(scal, place):
    kind, value = place
    if kind == "side":
        return lax.rem(scal[SIDE] + value, 2)
    return value


def columns(place, size, *front):
    def take(ref, scal):
        start = pl.multiple_of(block_of(scal, place) * size, size)
        return ref.at[(*front, slice(None), pl.ds(start, size))]

    return take


def lines(place, size):
    def take(ref, scal):
        start = pl.multiple_of(block_of(scal, place) * size, size)
        return ref.at[pl.ds(start, size), :]

    return take


def lanes_at(start, size):
    return lambda ref, scal: ref.at[:, pl.ds(start, size)]


def attn_needs(unit):
    if unit[0] == "half":
        return [need(unit[1])]
    _, qkv, out, _, _, place = unit
    depth, width = qkv.shape[1], out.shape[1]
    return [
        Need(
            (depth, 3 * LANE), BF,
            *[(qkv, columns(place, LANE, i), lanes_at(i * LANE, LANE)) for i in range(3)],
        ),
        Need((LANE, width), BF, (out, lines(place, LANE), everything)),
    ]


def up_need(unit, hidden):
    if unit[0] == "half":
        return need(unit[2])
    return Need((unit[3].shape[0], hidden), BF, (unit[3], columns(unit[5], hidden), everything))


def down_need(unit, hidden):
    if unit[0] == "half":
        return need(unit[3])
    return Need((hidden, unit[4].shape[1]), BF, (unit[4], lines(unit[5], hidden), everything))


def mean_of(values):
    return jnp.mean(values, axis=-1, keepdims=True)


def bias_of(seg_col, seg_row):
    return jnp.where(seg_col == seg_row, 0.0, MASKED)


def qkv_part(kind, buf):
    return buf[:, : 3 * LANE] if kind == "half" else buf[...]


def cut_kernel(scal, small, loads, stores):
    qkv, out = loads.pop(), loads.pop()
    stores.part(0, out[...].T, slice(None), slice(3 * LANE, 4 * LANE))
    stores.part(0, qkv[...], slice(None), slice(0, 3 * LANE))
    stores.send(0)


def turn_kernel(scal, small, loads, stores):
    store_turned(scal, stores.bufs[0], loads.pop()[...])
    stores.send(0)


def attn_fwd_kernel(kinds, first, last, scal, small, loads, stores):
    col_ref, row_ref = small[:2]
    tokens = loads.pop()[...]
    bias = bias_of(col_ref[...], row_ref[...])
    lane = lax.broadcasted_iota(jnp.int32, (1, LANE), 1)
    line = lax.broadcasted_iota(jnp.int32, (LANE, 1), 0)
    contexts, outs = [], []
    for number, kind in enumerate(kinds):
        weight = loads.pop()
        outs.append(loads.take() if kind == "whole" else weight)
        qkv = dot(tokens, qkv_part(kind, weight)).astype(BF)
        stores.put(number * 3, qkv)
        query, key, value = (qkv[:, i * LANE : (i + 1) * LANE] for i in range(3))
        query = query * jnp.asarray(SCALE, BF)
        value_t = value.T
        parts = []
        for head in range(2):
            mine = lane >= HDIM if head else lane < HDIM
            scores = dot_nt(jnp.where(mine, key, jnp.zeros_like(key)), query) + bias
            peak = jnp.max(scores, axis=0, keepdims=True)
            raw = jnp.exp(scores - peak)
            summed = jnp.sum(raw, axis=0, keepdims=True)
            stores.part(number * 3 + 2, peak + jnp.log(summed), pl.ds(head, 1), slice(None))
            prob = (raw * (1.0 / summed)).astype(BF)
            parts.append(dot(value_t, prob))
        stores.send(number * 3 + 2)
        context = jnp.where(line < HDIM, parts[0], parts[1]).astype(BF).T
        stores.put(number * 3 + 1, context)
        contexts.append(context)
    both = jnp.concatenate(contexts, axis=1)
    if kinds[0] == "whole":
        total = dot(both, jnp.concatenate([loads.get(slot)[...] for slot in outs], axis=0))
    else:
        total = dot_nt(both, jnp.concatenate([w[:, 3 * LANE :] for w in outs], axis=1))
    if not first:
        total = total + loads.pop()[...]
    at = len(kinds) * 3
    if not last:
        stores.put(at, total)
        return
    gain_ref, shift_ref = small[2:]
    pre = tokens.astype(F32) + total
    center = pre - mean_of(pre)
    inv = lax.rsqrt(mean_of(center * center) + 1e-12)
    hat = center * inv
    low = (hat * gain_ref[...] + shift_ref[...]).astype(BF)
    stores.put(at + 2, low)
    stores.put(at, hat)
    stores.put(at + 1, jnp.broadcast_to(inv, (hat.shape[0], LANE)))
    store_turned(scal, stores.bufs[at + 3], low)
    stores.send(at + 3)


def ffn_fwd_kernel(units, first, last, scal, small, loads, stores):
    low = loads.pop()[...]
    total = None
    for number in range(units):
        up = dot(low, loads.pop()[...])
        phi_big = 0.5 + 0.5 * lax.erf(up * (0.5 ** 0.5))
        phi_small = jnp.exp(up * up * -0.5) * 0.3989422804014327
        act = (up * phi_big).astype(BF)
        stores.put(number * 2, act)
        stores.put(number * 2 + 1, (phi_big + up * phi_small).astype(BF))
        part = dot(act, loads.pop()[...])
        total = part if total is None else total + part
    if not first:
        total = total + loads.pop()[...]
    at = units * 2
    if not last:
        stores.put(at, total)
        return
    gain1_ref, shift1_ref, gain2_ref, shift2_ref = small
    gain2 = gain2_ref[...]
    pre = loads.pop()[...] * gain1_ref[...] + shift1_ref[...] + total
    center = pre - mean_of(pre)
    inv = lax.rsqrt(mean_of(center * center) + 1e-12)
    hat = center * inv
    cot = loads.pop()[...].astype(F32)
    scaled = cot * gain2
    dpre = (scaled - mean_of(scaled) - hat * mean_of(scaled * hat)) * inv
    dffn = dpre.astype(BF)
    stores.put(at + 2, dffn)
    stores.put(at + 1, dpre)
    store_turned(scal, stores.bufs[at + 3], dffn)
    stores.send(at + 3)
    stores.put(at, (hat * gain2 + shift2_ref[...]).astype(BF))
    stores.put(at + 4, jnp.sum(cot * hat, axis=0, keepdims=True))
    stores.put(at + 5, jnp.sum(cot, axis=0, keepdims=True))


def ffn_bwd_kernel(near, has_recv, last, scal, small, loads, stores):
    dffn = loads.pop()[...]
    total = None
    ups = []
    dffn_t = low_t = None
    for unit in range(2):
        wd, slope = loads.pop(), loads.pop()
        d_up = (dot_nt(dffn, wd[...]) * slope[...].astype(F32)).astype(BF)
        if unit == 0:
            low_t = loads.pop()[...]
        up = dot(low_t, d_up)
        half = up.shape[0] // 2
        if unit == 0:
            dffn_t = loads.pop()[...]
        act = loads.pop()
        down = dot(dffn_t, act[...])
        if has_recv:
            got = loads.pop()
            down = down + got[0].astype(F32)
            up = up + got[1].astype(F32)
        down, up = down.astype(BF), up.astype(BF)
        if near:
            stores.part(0, down, unit)
            stores.send(0, unit)
            stores.part(1, up[:half], unit)
            stores.send(1, unit)
            stores.part(2, up[half:], unit)
            stores.send(2, unit)
        else:
            stores.part(0, down, unit, 0)
            stores.part(0, up, unit, 1)
            stores.send(0, unit)
        part = dot_nt(d_up, loads.pop()[...])
        total = part if total is None else total + part
    total = total + loads.pop()[...]
    at = 3 if near else 1
    if not last:
        stores.put(at, total)
        return
    hat = loads.pop()[...]
    scaled = total * small[0][...]
    inv = loads.pop()[:, :1]
    dpre = (scaled - mean_of(scaled) - hat * mean_of(scaled * hat)) * inv
    datt = dpre.astype(BF)
    stores.put(at + 1, datt)
    stores.put(at, dpre)
    store_turned(scal, stores.bufs[at + 2], datt)
    stores.send(at + 2)
    stores.put(at + 3, jnp.sum(total * hat, axis=0, keepdims=True))
    stores.put(at + 4, jnp.sum(total, axis=0, keepdims=True))


def attn_bwd_kernel(kind, near, has_recv, scal, small, loads, stores):
    bias = bias_of(small[0][...], small[1][...])
    lane = lax.broadcasted_iota(jnp.int32, (1, LANE), 1)
    line = lax.broadcasted_iota(jnp.int32, (LANE, 1), 0)
    datt = loads.pop()[...]
    weights = []
    for _ in range(2):
        weights.append((loads.take(), loads.take() if kind == "whole" else None))
    if kind == "whole":
        wo = jnp.concatenate([loads.get(slot)[...] for _, slot in weights], axis=0)
        dctx_all = dot_nt(datt, wo).astype(BF)
    else:
        wo = jnp.concatenate([loads.get(slot)[:, 3 * LANE :] for slot, _ in weights], axis=1)
        dctx_all = dot(datt, wo).astype(BF)
    grads, contexts = [], []
    for index in range(2):
        qkv_ref, lse_ref = loads.pop(), loads.pop()
        dctx = dctx_all[:, index * LANE : (index + 1) * LANE]
        query, key, value = (qkv_ref[:, i * LANE : (i + 1) * LANE] for i in range(3))
        query = query * jnp.asarray(SCALE, BF)
        key_t = key.T
        parts = []
        for head in range(2):
            mine = lane >= HDIM if head else lane < HDIM
            scores = dot_nt(jnp.where(mine, key, jnp.zeros_like(key)), query) + bias
            prob = jnp.exp(scores - lse_ref[head : head + 1, :])
            d_prob = dot_nt(jnp.where(mine, value, jnp.zeros_like(value)), dctx)
            inner = jnp.sum(prob * d_prob, axis=0, keepdims=True)
            d_scores = (prob * (d_prob - inner)).astype(BF)
            parts.append(
                (dot(key_t, d_scores), dot(d_scores, query), dot(prob.astype(BF), dctx))
            )
        d_query = (jnp.where(line < HDIM, parts[0][0], parts[1][0]) * SCALE).astype(BF).T
        d_key = jnp.where(lane < HDIM, parts[0][1], parts[1][1]).astype(BF)
        d_value = jnp.where(lane < HDIM, parts[0][2], parts[1][2]).astype(BF)
        grads.append(jnp.concatenate([d_query, d_key, d_value], axis=1))
    both = jnp.concatenate(grads, axis=1)
    datt_t, tok_t = loads.pop()[...], loads.pop()[...]
    ctx = jnp.concatenate([loads.pop()[...] for _ in range(2)], axis=1)
    qkv_grad = dot(tok_t, both)
    out_grad = dot(datt_t, ctx)
    half = tok_t.shape[0] // 2
    for unit in range(2):
        full = jnp.concatenate(
            [
                qkv_grad[:, unit * 3 * LANE : (unit + 1) * 3 * LANE],
                out_grad[:, unit * LANE : (unit + 1) * LANE],
            ],
            axis=1,
        )
        if has_recv:
            full = full + loads.pop()[...].astype(F32)
        full = full.astype(BF)
        if near:
            stores.part(0, full[:, : 2 * LANE], unit)
            stores.send(0, unit)
            stores.part(1, full[:half, 2 * LANE :], unit)
            stores.send(1, unit)
            stores.part(2, full[half:, 2 * LANE :], unit)
            stores.send(2, unit)
        else:
            stores.part(0, full, unit)
            stores.send(0, unit)
    wqkv = jnp.concatenate([qkv_part(kind, loads.get(slot)) for slot, _ in weights], axis=1)
    stores.put(3 if near else 1, loads.pop()[...] + dot_nt(both, wqkv))


def swap(value, axis, bit):
    count = lax.axis_size(axis)
    return lax.ppermute(value, axis, [(i, i ^ bit) for i in range(count)])


def add(*values):
    total = values[0].astype(F32)
    for value in values[1:]:
        total = total + value.astype(F32)
    return total.astype(BF)


def crossed(value):
    return jnp.concatenate([value[1:], value[:1]], axis=0)


def body(
    tokens,
    segment_ids,
    qkv_weight,
    out_weight,
    up_weight,
    down_weight,
    gain_attn,
    shift_attn,
    gain_ffn,
    shift_ffn,
    cotangent,
):
    count, width = tokens.shape
    seq, tp = lax.axis_size("seq"), lax.axis_size("tp")
    me_seq, me_tp = lax.axis_index("seq"), lax.axis_index("tp")
    blocks = width // LANE
    fast = seq == blocks and seq == 8 and tp == 4 and qkv_weight.shape[2] == 2 * LANE
    hidden = up_weight.shape[1] * tp // blocks
    seg = lax.dynamic_slice_in_dim(segment_ids, me_tp, 1, axis=0)
    seg_col = seg.reshape(count, 1)
    gains = [g.reshape(1, width) for g in (gain_attn, shift_attn, gain_ffn, shift_ffn)]
    absolute = jnp.arange(blocks, dtype=jnp.int32)
    side = lax.rem(me_seq, 2)
    pairs = blocks // 2
    half = width // 2
    wide = (count, width)
    if fast:
        rel = absolute ^ me_seq
        pos = (rel & 1) * 4 + ((rel >> 1) & 1) * 2 + (rel >> 2)
        scal = jnp.concatenate([pos, side.reshape(1)]).astype(jnp.int32)
        whole = [qkv_weight, out_weight, up_weight, down_weight]
        near = [swap(w, "tp", 1) for w in whole]
        units = {(0, h): ("whole", *whole, ("side", h)) for h in range(2)}
        units.update({(1, h): ("whole", *near, ("side", h)) for h in range(2)})
        cut = call(
            cut_kernel, attn_needs(units[0, 0]), [((width, 4 * LANE), BF)], scal, [], "cut", 1
        )[0]
        mine = [
            cut,
            lax.dynamic_slice_in_dim(up_weight, side * hidden, hidden, axis=1),
            lax.dynamic_slice_in_dim(down_weight, side * hidden, hidden, axis=0),
        ]
        far_a = [swap(w, "tp", 2) for w in mine]
        far_b = [swap(w, "seq", 1) for w in far_a]
        units[2, 0], units[2, 1] = ("half", *far_a), ("half", *far_b)
        units[3, 0] = ("half", *[swap(w, "tp", 1) for w in far_a])
        units[3, 1] = ("half", *[swap(w, "tp", 1) for w in far_b])
        groups = [[(0, 0), (0, 1)], [(1, 0), (1, 1)], [(2, 0), (3, 0)], [(2, 1), (3, 1)]]
    else:
        scal = jnp.concatenate([absolute, jnp.zeros((max(1, SIDE + 1 - blocks),), jnp.int32)])
        whole = [
            lax.all_gather(qkv_weight, "tp", axis=2, tiled=True),
            lax.all_gather(out_weight, "tp", axis=0, tiled=True),
            lax.all_gather(up_weight, "tp", axis=1, tiled=True),
            lax.all_gather(down_weight, "tp", axis=0, tiled=True),
        ]
        units = {(k // 2, k % 2): ("whole", *whole, ("block", k)) for k in range(blocks)}
        groups = [[(j, 0), (j, 1)] for j in range(pairs)]
    work = 2 * count * width

    tok_t = call(turn_kernel, [need(tokens)], [((width, count), BF)], scal, [], "turn", 1)[0]
    kept = {}
    total = None
    for number, group in enumerate(groups):
        first, last = number == 0, number == len(groups) - 1
        needs = [need(tokens)]
        for unit in group:
            needs += attn_needs(units[unit])
        if not first:
            needs.append(need(total))
        outs = []
        for unit in group:
            outs += [((count, 3 * LANE), BF), ((count, LANE), BF), ((8, count), F32)]
        if last:
            outs += [(wide, F32), ((count, LANE), F32), (wide, BF), ((width, count), BF)]
        else:
            outs.append((wide, F32))
        small = [seg_col, seg] + (gains[:2] if last else [])
        kinds = [units[unit][0] for unit in group]
        res = call(
            functools.partial(attn_fwd_kernel, kinds, first, last),
            needs, outs, scal, small, f"attn_fwd{number}", 4 * work * LANE * 2,
        )
        for index, unit in enumerate(group):
            kept[unit] = tuple(res[index * 3 : index * 3 + 3])
        if last:
            hat, inv, low, low_t = res[-4:]
        else:
            total = res[-1]

    acts = {}
    for number, group in enumerate(groups):
        first, last = number == 0, number == len(groups) - 1
        needs = [need(low)]
        for unit in group:
            needs += [up_need(units[unit], hidden), down_need(units[unit], hidden)]
        if not first:
            needs.append(need(total))
        if last:
            needs += [need(hat), need(cotangent)]
        outs = []
        for unit in group:
            outs += [((count, hidden), BF), ((count, hidden), BF)]
        if last:
            outs += [
                (wide, BF), (wide, F32), (wide, BF), ((width, count), BF),
                ((1, width), F32), ((1, width), F32),
            ]
        else:
            outs.append((wide, F32))
        res = call(
            functools.partial(ffn_fwd_kernel, len(group), first, last),
            needs, outs, scal, gains if last else [], f"ffn_fwd{number}", 4 * work * hidden,
        )
        for index, unit in enumerate(group):
            acts[unit] = tuple(res[index * 2 : index * 2 + 2])
        if last:
            mixed, d_pre, d_ffn, d_ffn_t, g_gain2, g_shift2 = res[-6:]
        else:
            total = res[-1]

    order = [3, 1, 2, 0] if fast else list(range(pairs))
    ffn_g, attn_g = {}, {}
    total = d_pre
    for number, j in enumerate(order):
        last = number == len(order) - 1
        here = not fast or j % 2 == 0
        recv = swap(ffn_g[j + 1][0], "tp", 1) if fast and here else None
        needs = [need(d_ffn)]
        for h in range(2):
            unit = units[j, h]
            needs += [down_need(unit, hidden), need(acts[j, h][1])]
            if h == 0:
                needs.append(need(low_t))
                needs.append(need(d_ffn_t))
            needs.append(need(acts[j, h][0]))
            if recv is not None:
                needs.append(
                    Need(recv.shape[1:], BF, (recv, lambda ref, scal, h=h: ref.at[h], everything))
                )
            needs.append(up_need(unit, hidden))
        needs.append(need(total))
        if here:
            outs = [((2, width, hidden), BF), ((2, half, hidden), BF), ((2, half, hidden), BF)]
        else:
            outs = [((2, 2, width, hidden), BF)]
        used = 6 if here else 2
        if last:
            needs += [need(hat), need(inv)]
            outs = outs + [
                (wide, F32), (wide, BF), ((width, count), BF), ((1, width), F32), ((1, width), F32),
            ]
        else:
            outs = outs + [(wide, F32)]
        res = call(
            functools.partial(ffn_bwd_kernel, here, recv is not None, last),
            needs, outs, scal, [gains[0]] if last else [], f"ffn_bwd{j}", 8 * work * hidden,
            used + (5 if last else 1),
        )
        grads = 3 if here else 1
        ffn_g[j] = res[:grads]
        if last:
            d_pre_one, d_att, d_att_t, g_gain1, g_shift1 = res[grads:]
        else:
            total = res[grads]

    norm_grads = jnp.concatenate([g_gain1, g_shift1, g_gain2, g_shift2], axis=0)
    if fast:
        for axis, bit in (("tp", 1), ("tp", 2), ("seq", 1), ("seq", 2), ("seq", 4)):
            norm_grads = norm_grads + swap(norm_grads, axis, bit)
        share = width // (seq * tp)
        norm_grads = lax.dynamic_slice_in_dim(
            norm_grads, (me_seq * tp + me_tp) * share, share, axis=1
        )
    else:
        norm_grads = lax.psum_scatter(norm_grads, ("seq", "tp"), scatter_dimension=1, tiled=True)

    total = d_pre_one
    for j in order:
        here = not fast or j % 2 == 0
        recv = swap(attn_g[j + 1][0], "tp", 1) if fast and here else None
        needs = [need(d_att)]
        for h in range(2):
            needs += attn_needs(units[j, h])
        for h in range(2):
            needs += [need(kept[j, h][0]), need(kept[j, h][2])]
        needs += [need(d_att_t), need(tok_t)]
        needs += [need(kept[j, h][1]) for h in range(2)]
        if recv is not None:
            needs += [
                Need(recv.shape[1:], BF, (recv, lambda ref, scal, h=h: ref.at[h], everything))
                for h in range(2)
            ]
        needs.append(need(total))
        if here:
            outs = [
                ((2, width, 2 * LANE), BF), ((2, half, 2 * LANE), BF), ((2, half, 2 * LANE), BF),
            ]
        else:
            outs = [((2, width, 4 * LANE), BF)]
        used = 6 if here else 2
        res = call(
            functools.partial(attn_bwd_kernel, units[j, 0][0], here, recv is not None),
            needs, outs + [(wide, F32)], scal, [seg_col, seg], f"attn_bwd{j}",
            12 * work * LANE * 2, used + 1,
        )
        attn_g[j], total = res[:-1], res[-1]
    token_grad = total

    if fast:
        quarter, eighth = half // 2, half // 4

        def finish(lo):
            lo = add(lo[:, :quarter], swap(lo[:, quarter:], "seq", 2))
            return lo[:, :eighth].astype(F32) + swap(lo[:, eighth:], "seq", 4).astype(F32)

        def reduced(far, near):
            got = swap(far[0], "tp", 2)
            far_hi = swap(far[2], "seq", 1)
            near_hi = swap(near[2], "seq", 1)
            far_lo = swap(add(far[1], crossed(far_hi)), "tp", 2)
            one_hi = swap(add(near[0][:, half:], got[:, half:]), "seq", 1)
            one = finish(add(near[0][:, :half], got[:, :half], crossed(one_hi)))
            two = finish(add(near[1], crossed(near_hi), far_lo))
            return one, two

        def ordered(value):
            return jnp.where(
                side == 0,
                jnp.concatenate([value[0], value[1]], 1),
                jnp.concatenate([value[1], value[0]], 1),
            )

        down, up = reduced(ffn_g[2], ffn_g[0])
        qk, vo = reduced(attn_g[2], attn_g[0])
        down_grad = ordered(down).T
        up_grad = ordered(up)
        qkv_grad = jnp.stack(
            [ordered(qk[:, :, :LANE]), ordered(qk[:, :, LANE:]), ordered(vo[:, :, :LANE])]
        )
        out_grad = ordered(vo[:, :, LANE:]).T
    else:

        def scattered(value, tp_dim, seq_dim):
            value = lax.psum_scatter(value, "tp", scatter_dimension=tp_dim, tiled=True)
            value = lax.psum_scatter(value, "seq", scatter_dimension=seq_dim, tiled=True)
            return value.astype(F32)

        def joined(parts):
            return jnp.concatenate(parts, axis=1)

        both = [(j, h) for j in range(pairs) for h in range(2)]
        down = joined([ffn_g[j][0][h] for j, h in both])
        up = joined([jnp.concatenate([ffn_g[j][i][h] for i in (1, 2)], 0) for j, h in both])
        qk = [attn_g[j][0][h] for j, h in both]
        vo = [jnp.concatenate([attn_g[j][i][h] for i in (1, 2)], 0) for j, h in both]
        down_grad = scattered(down, 1, 0).T
        up_grad = scattered(up, 1, 0)
        qkv_grad = jnp.stack(
            [
                joined([g[:, :LANE] for g in qk]),
                joined([g[:, LANE:] for g in qk]),
                joined([g[:, :LANE] for g in vo]),
            ]
        )
        qkv_grad = scattered(qkv_grad, 2, 1)
        out_grad = scattered(joined([g[:, LANE:] for g in vo]), 1, 0).T
    return (mixed, token_grad, qkv_grad, out_grad, up_grad, down_grad, norm_grads)


def solution(mesh):
    return jax.shard_map(
        body,
        mesh=mesh,
        in_specs=(
            P(("seq", "tp"), None),
            P("seq", None),
            P(None, None, "tp"),
            P("tp", None),
            P(None, "tp"),
            P("tp", None),
            P(),
            P(),
            P(),
            P(),
            P(("seq", "tp"), None),
        ),
        out_specs=(
            P(("seq", "tp"), None),
            P(("seq", "tp"), None),
            P(None, "seq", "tp"),
            P("tp", "seq"),
            P("seq", "tp"),
            P("tp", "seq"),
            P(None, ("seq", "tp")),
        ),
        check_vma=False,
    )
```

```python
import functools

import jax
import jax.numpy as jnp
from jax import lax
from jax.experimental import pallas as pl
from jax.experimental.pallas import tpu as pltpu
from jax.sharding import PartitionSpec as P

HDIM = 64
LANE = 128
BF = jnp.bfloat16
F32 = jnp.float32
SCALE = HDIM ** (-0.5)
MASKED = -1000000000.0


def dot(left, right):
    return jnp.dot(left, right, preferred_element_type=F32)


def dot_nt(left, right):
    return lax.dot_general(left, right, (((1,), (1,)), ((), ())), preferred_element_type=F32)


def everything(ref, scal):
    return ref


class Need:
    def __init__(self, shape, dtype, *parts):
        self.shape, self.dtype, self.parts = tuple(shape), dtype, parts


def need(array):
    return Need(array.shape, array.dtype, (array, everything, everything))


class Loads:
    def __init__(self, needs, refs, bufs, sems, scal):
        self.bufs, self.copies, self.next = bufs, [], 0
        at = 0
        for item, buf in zip(needs, bufs):
            mine = []
            for index, source, target in item.parts:
                copy = pltpu.make_async_copy(
                    source(refs[index], scal), target(buf, scal), sems.at[at]
                )
                copy.start()
                mine.append(copy)
                at += 1
            self.copies.append(mine)

    def take(self):
        self.next += 1
        return self.next - 1

    def get(self, slot):
        for copy in self.copies[slot]:
            copy.wait()
        self.copies[slot] = []
        return self.bufs[slot]

    def pop(self):
        return self.get(self.take())

    def finish(self):
        for slot in range(len(self.copies)):
            self.get(slot)


class Stores:
    def __init__(self, refs, bufs, sems):
        self.refs, self.sems, self.copies = refs, sems, []
        self.bufs = [ref if buf is None else buf for ref, buf in zip(refs, bufs)]
        self.direct = [buf is None for buf in bufs]
        self.next = 0

    def part(self, slot, value, *where):
        self.bufs[slot][where] = value

    def send(self, slot, *where):
        if self.direct[slot]:
            return
        source, target = self.bufs[slot], self.refs[slot]
        if where:
            source, target = source.at[where], target.at[where]
        copy = pltpu.make_async_copy(source, target, self.sems.at[self.next])
        self.next += 1
        copy.start()
        self.copies.append(copy)

    def put(self, slot, value):
        self.bufs[slot][...] = value
        self.send(slot)

    def finish(self):
        for copy in self.copies:
            copy.wait()


def hot(shape, dtype):
    return (shape, dtype, True)


def call(kernel, needs, outs, scal, small, name, flops, sends=None):
    arrays, parts = [], []
    for item in needs:
        fixed = []
        for array, source, target in item.parts:
            index = next((i for i, a in enumerate(arrays) if a is array), None)
            if index is None:
                index = len(arrays)
                arrays.append(array)
            fixed.append((index, source, target))
        parts.append(Need(item.shape, item.dtype, *fixed))
    copies = max(1, sum(len(item.parts) for item in parts))
    sends = max(1, len(outs) if sends is None else sends)
    here = [len(out) == 3 for out in outs]

    def run(*refs):
        refs = list(refs)
        scal_ref = refs.pop(0)
        small_refs = [refs.pop(0) for _ in small]
        in_refs = [refs.pop(0) for _ in arrays]
        out_refs = [refs.pop(0) for _ in outs]
        in_bufs = [refs.pop(0) for _ in parts]
        out_bufs = [None if stays else refs.pop(0) for stays in here]
        in_sems, out_sems = refs
        loads = Loads(parts, in_refs, in_bufs, in_sems, scal_ref)
        stores = Stores(out_refs, out_bufs, out_sems)
        kernel(scal_ref, small_refs, loads, stores)
        loads.finish()
        stores.finish()

    return pl.pallas_call(
        run,
        out_shape=[
            jax.ShapeDtypeStruct(out[0], out[1]) if stays else pltpu.HBM(out[0], out[1])
            for out, stays in zip(outs, here)
        ],
        in_specs=[pl.BlockSpec(memory_space=pltpu.SMEM)]
        + [pl.BlockSpec(memory_space=pltpu.VMEM)] * len(small)
        + [pl.BlockSpec(memory_space=pltpu.HBM)] * len(arrays),
        out_specs=[
            pl.BlockSpec(memory_space=pltpu.VMEM if stays else pltpu.HBM) for stays in here
        ],
        scratch_shapes=[pltpu.VMEM(item.shape, item.dtype) for item in parts]
        + [pltpu.VMEM(out[0], out[1]) for out, stays in zip(outs, here) if not stays]
        + [pltpu.SemaphoreType.DMA((copies,)), pltpu.SemaphoreType.DMA((sends,))],
        compiler_params=pltpu.CompilerParams(vmem_limit_bytes=32 * 1024 * 1024),
        cost_estimate=pl.CostEstimate(flops=flops, bytes_accessed=0, transcendentals=0),
        name=name,
    )(scal, *small, *[pltpu.with_memory_space_constraint(a, pltpu.HBM) for a in arrays])


def store_turned(scal, buf, values):
    for block in range(values.shape[1] // LANE):
        start = pl.multiple_of(scal[block] * LANE, LANE)
        buf[pl.ds(start, LANE), :] = values[:, block * LANE : (block + 1) * LANE].T


def block_of(scal, place):
    kind, value = place
    return scal[value] if kind == "table" else value


def columns(place, size, *front):
    def take(ref, scal):
        start = pl.multiple_of(block_of(scal, place) * size, size)
        return ref.at[(*front, slice(None), pl.ds(start, size))]

    return take


def lines(place, size):
    def take(ref, scal):
        start = pl.multiple_of(block_of(scal, place) * size, size)
        return ref.at[pl.ds(start, size), :]

    return take


def lanes_at(start, size):
    return lambda ref, scal: ref.at[:, pl.ds(start, size)]


def lines_at(start, size):
    return lambda ref, scal: ref.at[pl.ds(start, size), :]


def slot_at(*where):
    return lambda ref, scal: ref.at[where]


def stacked_at(index, size):
    def take(ref, scal):
        ref = ref if len(ref.shape) == 2 else ref.at[1]
        return ref.at[pl.ds(index * size, size), :]

    return take


def block_at(row, column, size):
    return lambda ref, scal: ref.at[pl.ds(row * size, size), pl.ds(column * size, size)]


def first_of(ref, scal):
    return ref if len(ref.shape) == 2 else ref.at[0]


def attn_needs(unit):
    if unit[0] == "half":
        return [need(unit[1])]
    _, qkv, out, place = unit
    depth, width = qkv.shape[1], out.shape[1]
    return [
        Need(
            (depth, 3 * LANE), BF,
            *[(qkv, columns(place, LANE, i), lanes_at(i * LANE, LANE)) for i in range(3)],
        ),
        Need((LANE, width), BF, (out, lines(place, LANE), everything)),
    ]


def up_need(pieces, size):
    parts = []
    for number, piece in enumerate(pieces):
        target = lanes_at(number * size, size)
        if piece[0] == "packed":
            parts.append((piece[1], first_of, target))
        else:
            parts.append((piece[1], columns(piece[3], size), target))
    return Need((pieces[0][-1], len(pieces) * size), BF, *parts)


def down_need(pieces, size):
    parts = []
    for number, piece in enumerate(pieces):
        width = piece[-1]
        if piece[0] == "packed":
            for index in range(width // size):
                parts.append(
                    (piece[2], stacked_at(index, size), block_at(number, index, size))
                )
        else:
            parts.append((piece[2], lines(piece[3], size), lines_at(number * size, size)))
    return Need((len(pieces) * size, pieces[0][-1]), BF, *parts)


def saved_need(pieces, size):
    parts = [
        (array, lanes_at(index * size, size), lanes_at(number * size, size))
        for number, (array, index) in enumerate(pieces)
    ]
    return Need((pieces[0][0].shape[0], len(pieces) * size), BF, *parts)


def mean_of(values):
    return jnp.mean(values, axis=-1, keepdims=True)


def bias_of(seg_col, seg_row):
    return jnp.where(seg_col == seg_row, 0.0, MASKED)


def qkv_part(kind, buf):
    return buf[:, : 3 * LANE] if kind == "half" else buf[...]


def cut_kernel(scal, small, loads, stores):
    qkv, out = loads.pop(), loads.pop()
    stores.part(0, out[...].T, slice(None), slice(3 * LANE, 4 * LANE))
    stores.part(0, qkv[...], slice(None), slice(0, 3 * LANE))
    stores.send(0)


def pack_kernel(size, scal, small, loads, stores):
    up, down = loads.pop(), loads.pop()
    stores.part(0, up[...], 0)
    for index in range(down.shape[1] // size):
        block = down[:, index * size : (index + 1) * size]
        stores.part(0, block, 1, pl.ds(index * size, size))
    stores.send(0)


def turn_kernel(scal, small, loads, stores):
    store_turned(scal, stores.bufs[0], small[0][...])
    stores.send(0)


def attn_fwd_kernel(kinds, first, last, scal, small, loads, stores):
    col_ref, row_ref, tokens_ref = small[:3]
    tokens = tokens_ref[...]
    bias = bias_of(col_ref[...], row_ref[...])
    lane = lax.broadcasted_iota(jnp.int32, (1, LANE), 1)
    line = lax.broadcasted_iota(jnp.int32, (LANE, 1), 0)
    contexts, outs = [], []
    for number, kind in enumerate(kinds):
        weight = loads.pop()
        outs.append(loads.take() if kind == "whole" else weight)
        qkv = dot(tokens, qkv_part(kind, weight)).astype(BF)
        stores.put(number * 3, qkv)
        query, key, value = (qkv[:, i * LANE : (i + 1) * LANE] for i in range(3))
        query = query * jnp.asarray(SCALE, BF)
        value_t = value.T
        parts = []
        for head in range(2):
            mine = lane >= HDIM if head else lane < HDIM
            scores = dot_nt(jnp.where(mine, key, jnp.zeros_like(key)), query) + bias
            peak = jnp.max(scores, axis=0, keepdims=True)
            raw = jnp.exp(scores - peak)
            summed = jnp.sum(raw, axis=0, keepdims=True)
            stores.part(number * 3 + 2, peak + jnp.log(summed), pl.ds(head, 1), slice(None))
            prob = (raw * (1.0 / summed)).astype(BF)
            parts.append(dot(value_t, prob))
        stores.send(number * 3 + 2)
        context = jnp.where(line < HDIM, parts[0], parts[1]).astype(BF).T
        stores.put(number * 3 + 1, context)
        contexts.append(context)
    both = jnp.concatenate(contexts, axis=1)
    if kinds[0] == "whole":
        total = dot(both, jnp.concatenate([loads.get(slot)[...] for slot in outs], axis=0))
    else:
        total = dot_nt(both, jnp.concatenate([w[:, 3 * LANE :] for w in outs], axis=1))
    if not first:
        total = total + small[3][...]
    at = len(kinds) * 3
    if not last:
        stores.put(at, total)
        return
    gain_ref, shift_ref = small[-2:]
    pre = tokens.astype(F32) + total
    center = pre - mean_of(pre)
    inv = lax.rsqrt(mean_of(center * center) + 1e-12)
    hat = center * inv
    low = (hat * gain_ref[...] + shift_ref[...]).astype(BF)
    stores.put(at + 2, low)
    stores.put(at, hat)
    stores.put(at + 1, jnp.broadcast_to(inv, (hat.shape[0], LANE)))
    store_turned(scal, stores.bufs[at + 3], low)
    stores.send(at + 3)


def ffn_fwd_kernel(units, first, last, scal, small, loads, stores):
    low = small[0][...]
    total = None
    for number in range(units):
        up = dot(low, loads.pop()[...])
        phi_big = 0.5 + 0.5 * lax.erf(up * (0.5 ** 0.5))
        phi_small = jnp.exp(up * up * -0.5) * 0.3989422804014327
        act = (up * phi_big).astype(BF)
        stores.put(number * 2, act)
        stores.put(number * 2 + 1, (phi_big + up * phi_small).astype(BF))
        part = dot(act, loads.pop()[...])
        total = part if total is None else total + part
    if not first:
        total = total + small[1][...]
    at = units * 2
    if not last:
        stores.put(at, total)
        return
    hat_ref, gain1_ref, shift1_ref, gain2_ref, shift2_ref = small[-5:]
    gain2 = gain2_ref[...]
    pre = hat_ref[...] * gain1_ref[...] + shift1_ref[...] + total
    center = pre - mean_of(pre)
    inv = lax.rsqrt(mean_of(center * center) + 1e-12)
    hat = center * inv
    cot = loads.pop()[...].astype(F32)
    scaled = cot * gain2
    dpre = (scaled - mean_of(scaled) - hat * mean_of(scaled * hat)) * inv
    dffn = dpre.astype(BF)
    stores.put(at + 2, dffn)
    stores.put(at + 1, dpre)
    store_turned(scal, stores.bufs[at + 3], dffn)
    stores.send(at + 3)
    stores.put(at, (hat * gain2 + shift2_ref[...]).astype(BF))
    stores.put(at + 4, jnp.sum(cot * hat, axis=0, keepdims=True))
    stores.put(at + 5, jnp.sum(cot, axis=0, keepdims=True))


def split_rows(stores, low_slot, high_slot, index, value):
    step = value.shape[0] // 4
    for number in range(4):
        slot = high_slot if number % 2 else low_slot
        rows = pl.ds(number // 2 * step, step)
        stores.part(slot, value[number * step : (number + 1) * step], index, rows)


def ffn_bwd_kernel(near, has_recv, last, size, scal, small, loads, stores):
    dffn_ref, dffn_t_ref, low_t_ref, acc_ref = small[:4]
    wd, slope = loads.pop(), loads.pop()
    d_up = (dot_nt(dffn_ref[...], wd[...]) * slope[...].astype(F32)).astype(BF)
    up = dot(low_t_ref[...], d_up)
    if has_recv:
        got = loads.take()
        up = up + loads.get(got)[1].astype(F32)
    up = up.astype(BF)
    for index in range(2):
        value = up[:, index * size : (index + 1) * size]
        if near:
            split_rows(stores, 1, 2, index, value)
        else:
            stores.part(0, up, 1)
    if near:
        stores.send(1)
        stores.send(2)
    down = dot(dffn_t_ref[...], loads.pop()[...])
    if has_recv:
        down = down + loads.get(got)[0].astype(F32)
    down = down.astype(BF)
    if near:
        for index in range(2):
            stores.part(0, down[:, index * size : (index + 1) * size], index)
    else:
        stores.part(0, down, 0)
    stores.send(0)
    total = acc_ref[...] + dot_nt(d_up, loads.pop()[...])
    at = 3 if near else 1
    if not last:
        stores.put(at, total)
        return
    hat_ref, inv_ref, gain_ref = small[4:]
    hat = hat_ref[...]
    scaled = total * gain_ref[...]
    inv = inv_ref[:, :1]
    dpre = (scaled - mean_of(scaled) - hat * mean_of(scaled * hat)) * inv
    datt = dpre.astype(BF)
    stores.put(at + 1, datt)
    stores.put(at, dpre)
    store_turned(scal, stores.bufs[at + 2], datt)
    stores.send(at + 2)
    stores.put(at + 3, jnp.sum(total * hat, axis=0, keepdims=True))
    stores.put(at + 4, jnp.sum(total, axis=0, keepdims=True))


def attn_bwd_kernel(kind, near, has_recv, scal, small, loads, stores):
    col_ref, row_ref, datt_ref, datt_t_ref, tok_t_ref, acc_ref = small
    bias = bias_of(col_ref[...], row_ref[...])
    lane = lax.broadcasted_iota(jnp.int32, (1, LANE), 1)
    line = lax.broadcasted_iota(jnp.int32, (LANE, 1), 0)
    datt = datt_ref[...]
    weights = []
    for _ in range(2):
        weights.append((loads.take(), loads.take() if kind == "whole" else None))
    if kind == "whole":
        wo = jnp.concatenate([loads.get(slot)[...] for _, slot in weights], axis=0)
        dctx_all = dot_nt(datt, wo).astype(BF)
    else:
        wo = jnp.concatenate([loads.get(slot)[:, 3 * LANE :] for slot, _ in weights], axis=1)
        dctx_all = dot(datt, wo).astype(BF)
    grads = []
    for index in range(2):
        qkv_ref, lse_ref = loads.pop(), loads.pop()
        dctx = dctx_all[:, index * LANE : (index + 1) * LANE]
        query, key, value = (qkv_ref[:, i * LANE : (i + 1) * LANE] for i in range(3))
        query = query * jnp.asarray(SCALE, BF)
        key_t = key.T
        parts = []
        for head in range(2):
            mine = lane >= HDIM if head else lane < HDIM
            scores = dot_nt(jnp.where(mine, key, jnp.zeros_like(key)), query) + bias
            prob = jnp.exp(scores - lse_ref[head : head + 1, :])
            d_prob = dot_nt(jnp.where(mine, value, jnp.zeros_like(value)), dctx)
            inner = jnp.sum(prob * d_prob, axis=0, keepdims=True)
            d_scores = (prob * (d_prob - inner)).astype(BF)
            parts.append(
                (dot(key_t, d_scores), dot(d_scores, query), dot(prob.astype(BF), dctx))
            )
        d_query = (jnp.where(line < HDIM, parts[0][0], parts[1][0]) * SCALE).astype(BF).T
        d_key = jnp.where(lane < HDIM, parts[0][1], parts[1][1]).astype(BF)
        d_value = jnp.where(lane < HDIM, parts[0][2], parts[1][2]).astype(BF)
        grads.append(jnp.concatenate([d_query, d_key, d_value], axis=1))
    both = jnp.concatenate(grads, axis=1)
    ctx = jnp.concatenate([loads.pop()[...] for _ in range(2)], axis=1)
    qkv_grad = dot(tok_t_ref[...], both)
    out_grad = dot(datt_t_ref[...], ctx)
    for unit in range(2):
        full = jnp.concatenate(
            [
                qkv_grad[:, unit * 3 * LANE : (unit + 1) * 3 * LANE],
                out_grad[:, unit * LANE : (unit + 1) * LANE],
            ],
            axis=1,
        )
        if has_recv:
            full = full + loads.pop()[...].astype(F32)
        full = full.astype(BF)
        if near:
            stores.part(0, full[:, : 2 * LANE], unit)
            stores.send(0, unit)
            split_rows(stores, 1, 2, unit, full[:, 2 * LANE :])
            stores.send(1, unit)
            stores.send(2, unit)
        else:
            stores.part(0, full, unit)
            stores.send(0, unit)
    wqkv = jnp.concatenate([qkv_part(kind, loads.get(slot)) for slot, _ in weights], axis=1)
    stores.put(3 if near else 1, acc_ref[...] + dot_nt(both, wqkv))


def swap(value, axis, bit):
    count = lax.axis_size(axis)
    return lax.ppermute(value, axis, [(i, i ^ bit) for i in range(count)])


def add(*values):
    total = values[0].astype(F32)
    for value in values[1:]:
        total = total + value.astype(F32)
    return total.astype(BF)


def tie(values, *after):
    return list(lax.optimization_barrier((tuple(values), after))[0])


def join(values, axis=0):
    return jnp.concatenate(values, axis=axis)


def body(
    tokens,
    segment_ids,
    qkv_weight,
    out_weight,
    up_weight,
    down_weight,
    gain_attn,
    shift_attn,
    gain_ffn,
    shift_ffn,
    cotangent,
):
    count, width = tokens.shape
    seq, tp = lax.axis_size("seq"), lax.axis_size("tp")
    me_seq, me_tp = lax.axis_index("seq"), lax.axis_index("tp")
    blocks = width // LANE
    pairs = blocks // 2
    size = up_weight.shape[1] * tp // (4 * pairs)
    fast = seq == blocks and seq == 8 and tp == 4 and qkv_weight.shape[2] == 2 * LANE
    seg = lax.dynamic_slice_in_dim(segment_ids, me_tp, 1, axis=0)
    seg_col = seg.reshape(count, 1)
    gains = [g.reshape(1, width) for g in (gain_attn, shift_attn, gain_ffn, shift_ffn)]
    absolute = jnp.arange(blocks, dtype=jnp.int32)
    half, quarter, eighth = width // 2, width // 4, width // 8
    wide = (count, width)
    work = 2 * count * width
    bit_x, bit_z = me_seq & 1, (me_seq >> 1) & 1

    def over_x(value):
        return swap(value, "seq", 1)

    def over_z(value):
        return swap(value, "seq", 2)

    def over_y(value):
        return swap(value, "tp", 2)

    def over_core(value):
        return swap(value, "tp", 1)

    if fast:
        rel = absolute ^ me_seq
        pos = ((rel >> 1) & 1) * 4 + (rel & 1) * 2 + (rel >> 2)
        mine = me_seq & 3
        scal = jnp.stack(
            [pos[i] for i in range(blocks)] + [mine ^ r for r in range(4)] + [bit_z, 1 - bit_z]
        ).astype(jnp.int32)
        table = [("table", blocks + r) for r in range(6)]
        cut = call(
            cut_kernel, attn_needs(("whole", qkv_weight, out_weight, table[4])),
            [((width, 4 * LANE), BF)], scal, [], "cut", 1,
        )[0]
        head_a = over_y(cut)
        own = ("whole", up_weight, down_weight, table[0], width)
        pack = call(
            functools.partial(pack_kernel, size), [up_need([own], size), down_need([own], size)],
            [((2, width, size), BF)], scal, [], "pack", 1,
        )[0]
        ffn_a = over_y(pack)
        near = [over_core(w) for w in (qkv_weight, out_weight, up_weight, down_weight)]
    else:
        scal = jnp.concatenate([absolute, jnp.zeros((6,), jnp.int32)])
        qkv_all = lax.all_gather(qkv_weight, "tp", axis=2, tiled=True)
        out_all = lax.all_gather(out_weight, "tp", axis=0, tiled=True)
        up_all = lax.all_gather(up_weight, "tp", axis=1, tiled=True)
        down_all = lax.all_gather(down_weight, "tp", axis=0, tiled=True)

    kept, acts = {}, {}

    def attn_fwd(number, group, total, last):
        needs, outs = [], []
        for unit in group:
            needs += attn_needs(heads[unit])
            outs += [((count, 3 * LANE), BF), ((count, LANE), BF), ((8, count), F32)]
        if last:
            outs += [
                hot(wide, F32), hot((count, LANE), F32), hot(wide, BF), hot((width, count), BF),
            ]
        else:
            outs.append(hot(wide, F32))
        first = total is None
        small = [seg_col, seg, tokens] + ([] if first else [total]) + (gains[:2] if last else [])
        kinds = [heads[unit][0] for unit in group]
        res = call(
            functools.partial(attn_fwd_kernel, kinds, first, last),
            needs, outs, scal, small, f"attn_fwd{number}", 4 * work * LANE * 2,
        )
        for index, unit in enumerate(group):
            kept[unit] = tuple(res[index * 3 : index * 3 + 3])
        return res[len(group) * 3 :]

    def ffn_fwd(number, group, total, last):
        needs, outs = [], []
        for unit in group:
            pieces = [hidden[piece] for piece in unit]
            needs += [up_need(pieces, size), down_need(pieces, size)]
            outs += [((count, len(unit) * size), BF)] * 2
        first = total is None
        small = [low] + ([] if first else [total])
        if last:
            needs.append(need(cotangent))
            small += [hat, *gains]
            outs += [
                (wide, BF), hot(wide, F32), hot(wide, BF), hot((width, count), BF),
                hot((1, width), F32), hot((1, width), F32),
            ]
        else:
            outs.append(hot(wide, F32))
        res = call(
            functools.partial(ffn_fwd_kernel, len(group), first, last),
            needs, outs, scal, small, f"ffn_fwd{number}", 8 * work * size * len(group),
        )
        for index, unit in enumerate(group):
            for place, piece in enumerate(unit):
                acts[piece] = [(array, place) for array in res[index * 2 : index * 2 + 2]]
        return res[len(group) * 2 :]

    if fast:
        heads, hidden = {}, {}
        for h in range(2):
            heads[0, h] = ("whole", qkv_weight, out_weight, table[4 + h])
            heads[1, h] = ("whole", *near[:2], table[4 + h])
        for r in range(4):
            hidden[0, r] = ("whole", up_weight, down_weight, table[r], width)
            hidden[1, r] = ("whole", *near[2:], table[r], width)

        def packed(r, up, down):
            hidden[2, r] = ("packed", up, down, width)
            if up is down:
                other = over_core(up)
                hidden[3, r] = ("packed", other, other, width)
            else:
                hidden[3, r] = ("packed", over_core(up), over_core(down), width)

        (total,) = attn_fwd(0, [(0, 0), (0, 1)], None, False)
        (total,) = attn_fwd(1, [(1, 0), (1, 1)], total, False)
        (head_a,) = tie([head_a], total)
        head_b = over_z(head_a)
        heads[2, 0], heads[3, 0] = ("half", head_a), ("half", over_core(head_a))
        (total,) = attn_fwd(2, [(2, 0)], total, False)
        (total,) = attn_fwd(3, [(3, 0)], total, False)
        tok_t = call(
            turn_kernel, [], [hot((width, count), BF)], scal, tie([tokens], total), "turn", 1
        )[0]
        ffn_a, head_b = tie([ffn_a, head_b], tok_t)
        heads[2, 1], heads[3, 1] = ("half", head_b), ("half", over_core(head_b))
        ffn_b, ffn_c = over_x(ffn_a), over_z(ffn_a)
        packed(0, ffn_a, ffn_a)
        (total,) = attn_fwd(4, [(2, 1)], total, False)
        hat, inv, low, low_t = attn_fwd(5, [(3, 1)], total, True)
        (total,) = ffn_fwd(0, [[(0, 0), (0, 1)], [(0, 2), (0, 3)]], None, False)
        (total,) = ffn_fwd(1, [[(1, 0), (1, 1)], [(1, 2), (1, 3)]], total, False)
        ffn_b, ffn_c = tie([ffn_b, ffn_c], total)
        up_d, down_d = over_x(ffn_c[0]), over_z(ffn_b[1])
        packed(1, ffn_b, ffn_b)
        packed(2, ffn_c, ffn_c)
        (total,) = ffn_fwd(2, [[(2, 0), (3, 0)]], total, False)
        (total,) = ffn_fwd(3, [[(2, 1), (2, 2)], [(3, 1), (3, 2)]], total, False)
        packed(3, *tie([up_d, down_d], total))
        res = ffn_fwd(4, [[(2, 3), (3, 3)]], total, True)
    else:
        heads = {
            (k // 2, k % 2): ("whole", qkv_all, out_all, ("block", k)) for k in range(blocks)
        }
        hidden = {
            (k // 4, k % 4): ("whole", up_all, down_all, ("block", k), width)
            for k in range(4 * pairs)
        }
        tok_t = call(
            turn_kernel, [], [hot((width, count), BF)], scal, [tokens], "turn", 1
        )[0]
        total = None
        for j in range(pairs):
            res = attn_fwd(j, [(j, 0), (j, 1)], total, j == pairs - 1)
            total = res[0]
        hat, inv, low, low_t = res
        total = None
        for j in range(pairs):
            res = ffn_fwd(j, [[(j, 0), (j, 1)], [(j, 2), (j, 3)]], total, j == pairs - 1)
            total = res[0]
    mixed, d_pre, d_ffn, d_ffn_t, g_gain2, g_shift2 = res

    order = [3, 1, 2, 0] if fast else list(range(pairs))
    ffn_g, attn_g, ffn_got, attn_got = {}, {}, {}, {}
    total = d_pre
    for u in range(2):
        for j in order:
            last = j == order[-1] and u == 1
            here = not fast or j % 2 == 0
            recv = ffn_got.get((j, u))
            pieces = [hidden[j, 2 * u + i] for i in range(2)]
            saved = [acts[j, 2 * u + i] for i in range(2)]
            needs = [down_need(pieces, size), saved_need([s[1] for s in saved], size)]
            if recv is not None:
                needs.append(need(recv))
            needs += [saved_need([s[0] for s in saved], size), up_need(pieces, size)]
            small = [d_ffn, d_ffn_t, low_t, total]
            if here:
                outs = [((2, width, size), BF), ((2, half, size), BF), ((2, half, size), BF)]
            else:
                outs = [((2, width, 2 * size), BF)]
            grads = len(outs)
            if last:
                small += [hat, inv, gains[0]]
                outs = outs + [
                    hot(wide, F32), hot(wide, BF), hot((width, count), BF),
                    hot((1, width), F32), hot((1, width), F32),
                ]
            else:
                outs = outs + [hot(wide, F32)]
            res = call(
                functools.partial(ffn_bwd_kernel, here, recv is not None, last, size),
                needs, outs, scal, small, f"ffn_bwd{j}{u}", 16 * work * size,
            )
            ffn_g[j, u] = res[:grads]
            if not here:
                ffn_got[j - 1, u] = over_core(res[0])
            total = res[grads]
    d_pre_one, d_att, d_att_t, g_gain1, g_shift1 = res[grads:]

    total = d_pre_one
    done = []
    for j in order:
        here = not fast or j % 2 == 0
        recv = attn_got.get(j)
        needs = []
        for h in range(2):
            needs += attn_needs(heads[j, h])
        for h in range(2):
            needs += [need(kept[j, h][0]), need(kept[j, h][2])]
        needs += [need(kept[j, h][1]) for h in range(2)]
        if recv is not None:
            needs += [Need(recv.shape[1:], BF, (recv, slot_at(h), everything)) for h in range(2)]
        if here:
            outs = [
                ((2, width, 2 * LANE), BF), ((2, half, 2 * LANE), BF), ((2, half, 2 * LANE), BF),
            ]
        else:
            outs = [((2, width, 4 * LANE), BF)]
        res = call(
            functools.partial(attn_bwd_kernel, heads[j, 0][0], here, recv is not None),
            needs, outs + [hot(wide, F32)], scal, [seg_col, seg, d_att, d_att_t, tok_t, total],
            f"attn_bwd{j}", 12 * work * LANE * 2, 2 * len(outs) + 1,
        )
        attn_g[j], total = res[:-1], res[-1]
        done.append(total)
        if not here:
            attn_got[j - 1] = over_core(res[0])
    token_grad = total

    norm_grads = join([g_gain1, g_shift1, g_gain2, g_shift2])
    if fast:
        for axis, bit in (("tp", 1), ("tp", 2), ("seq", 1), ("seq", 2), ("seq", 4)):
            norm_grads = norm_grads + swap(norm_grads, axis, bit)
        share = width // (seq * tp)
        norm_grads = lax.dynamic_slice_in_dim(
            norm_grads, (me_seq * tp + me_tp) * share, share, axis=1
        )

        def flip(value):
            return join([value[1:], value[:1]])

        def turn_halves(value):
            return join([value[2:], value[:2]])

        def last_step(value):
            return value[:, :eighth].astype(F32) + swap(value[:, eighth:], "seq", 4).astype(F32)

        far_y = [over_y(ffn_g[2, u][0]) for u in range(2)]
        far_x = [over_x(ffn_g[2, u][2]) for u in range(2)]
        far_x = tie(far_x, done[0])
        far = join([add(ffn_g[2, u][1], flip(far_x[u])) for u in range(2)])
        far_z = over_z(far[:, quarter:])
        near_x = tie([over_x(ffn_g[0, u][2]) for u in range(2)], done[1])
        near = join([add(ffn_g[0, u][1], flip(near_x[u])) for u in range(2)])
        near_z = over_z(near[:, quarter:])
        (far_z,) = tie([far_z], done[1])
        up_y = over_y(add(far[:, :quarter], turn_halves(far_z)))
        far_y = tie(far_y, done[1])
        down_z = [over_z(add(ffn_g[0, u][0][:, half:], far_y[u][:, half:])) for u in range(2)]

        def flip_pairs(value):
            return join([value[1:2], value[:1], value[3:], value[2:3]])

        qk_y = over_y(attn_g[2][0])
        vo_x = over_x(attn_g[2][2])
        vo_far = add(attn_g[2][1], vo_x)
        vo_z = over_z(vo_far[:, quarter:])
        vo_near_x = over_x(attn_g[0][2])
        down_z = tie(down_z, done[2])
        down = join(
            [
                add(ffn_g[0, u][0][:, :half], far_y[u][:, :half], down_z[1 - u])
                for u in range(2)
            ]
        )
        down_x = over_x(down[:, quarter:])
        (near_z,) = tie([near_z], done[2])
        up = add(near[:, :quarter], turn_halves(near_z), up_y)
        up = last_step(up)
        vo_y = over_y(add(vo_far[:, :quarter], flip(vo_z)))
        down = last_step(add(down[:, :quarter], flip_pairs(down_x)))
        vo_near = add(attn_g[0][1], vo_near_x)
        vo_near_z = over_z(vo_near[:, quarter:])
        qk_z = over_z(add(attn_g[0][0][:, half:], qk_y[:, half:]))
        vo = last_step(add(vo_near[:, :quarter], flip(vo_near_z), vo_y))
        qk = add(attn_g[0][0][:, :half], qk_y[:, :half], flip(qk_z))
        qk = last_step(add(qk[:, :quarter], over_x(qk[:, quarter:])))

        def ordered(value):
            flipped = jnp.where(bit_z == 0, value, flip(value))
            return join([flipped[0], flipped[1]], 1)

        def ordered_four(value):
            value = jnp.where(bit_x == 0, value, flip_pairs(value))
            value = jnp.where(bit_z == 0, value, turn_halves(value))
            return join([value[r] for r in range(4)], 1)

        down_grad = ordered_four(down).T
        up_grad = ordered_four(up)
        qkv_grad = jnp.stack(
            [ordered(qk[:, :, :LANE]), ordered(qk[:, :, LANE:]), ordered(vo[:, :, :LANE])]
        )
        out_grad = ordered(vo[:, :, LANE:]).T
    else:
        norm_grads = lax.psum_scatter(norm_grads, ("seq", "tp"), scatter_dimension=1, tiled=True)

        def scattered(value, tp_dim, seq_dim):
            value = lax.psum_scatter(value, "tp", scatter_dimension=tp_dim, tiled=True)
            value = lax.psum_scatter(value, "seq", scatter_dimension=seq_dim, tiled=True)
            return value.astype(F32)

        def rows_of(low_part, high_part):
            parts = [low_part[:quarter], high_part[:quarter], low_part[quarter:], high_part[quarter:]]
            return join(parts)

        both = [(j, u) for j in range(pairs) for u in range(2)]
        down = join([ffn_g[k][0][i] for k in both for i in range(2)], 1)
        up = join([rows_of(ffn_g[k][1][i], ffn_g[k][2][i]) for k in both for i in range(2)], 1)
        qk = [attn_g[j][0][h] for j, h in both]
        vo = [rows_of(attn_g[j][1][h], attn_g[j][2][h]) for j, h in both]
        down_grad = scattered(down, 1, 0).T
        up_grad = scattered(up, 1, 0)
        qkv_grad = jnp.stack(
            [
                join([g[:, :LANE] for g in qk], 1),
                join([g[:, LANE:] for g in qk], 1),
                join([g[:, :LANE] for g in vo], 1),
            ]
        )
        qkv_grad = scattered(qkv_grad, 2, 1)
        out_grad = scattered(join([g[:, LANE:] for g in vo], 1), 1, 0).T
    return (mixed, token_grad, qkv_grad, out_grad, up_grad, down_grad, norm_grads)


def solution(mesh):
    return jax.shard_map(
        body,
        mesh=mesh,
        in_specs=(
            P(("seq", "tp"), None),
            P("seq", None),
            P(None, None, "tp"),
            P("tp", None),
            P(None, "tp"),
            P("tp", None),
            P(),
            P(),
            P(),
            P(),
            P(("seq", "tp"), None),
        ),
        out_specs=(
            P(("seq", "tp"), None),
            P(("seq", "tp"), None),
            P(None, "seq", "tp"),
            P("tp", "seq"),
            P("seq", "tp"),
            P("tp", "seq"),
            P(None, ("seq", "tp")),
        ),
        check_vma=False,
    )
```

```python
import functools

import jax
import jax.numpy as jnp
from jax import lax
from jax.experimental import pallas as pl
from jax.experimental.pallas import tpu as pltpu
from jax.sharding import PartitionSpec as P

HDIM = 64
LANE = 128
BF = jnp.bfloat16
F32 = jnp.float32
SCALE = HDIM ** (-0.5)
MASKED = -1000000000.0
SPLIT = (1, 1)


def dot(left, right):
    return jnp.dot(left, right, preferred_element_type=F32)


def dot_nt(left, right):
    return lax.dot_general(left, right, (((1,), (1,)), ((), ())), preferred_element_type=F32)


def everything(ref, scal):
    return ref


class Need:
    def __init__(self, shape, dtype, *parts, pinned=True):
        self.shape, self.dtype, self.parts, self.pinned = tuple(shape), dtype, parts, pinned


def need(array, pinned=True):
    return Need(array.shape, array.dtype, (array, everything, everything), pinned=pinned)


class Loads:
    def __init__(self, needs, refs, bufs, sems, scal):
        self.bufs, self.copies, self.next = bufs, [], 0
        at = 0
        for item, buf in zip(needs, bufs):
            mine = []
            for index, source, target in item.parts:
                copy = pltpu.make_async_copy(
                    source(refs[index], scal), target(buf, scal), sems.at[at]
                )
                copy.start()
                mine.append(copy)
                at += 1
            self.copies.append(mine)

    def take(self):
        self.next += 1
        return self.next - 1

    def get(self, slot):
        for copy in self.copies[slot]:
            copy.wait()
        self.copies[slot] = []
        return self.bufs[slot]

    def pop(self):
        return self.get(self.take())

    def finish(self):
        for slot in range(len(self.copies)):
            self.get(slot)


class Stores:
    def __init__(self, refs, bufs, sems):
        self.refs, self.sems, self.copies = refs, sems, []
        self.bufs = [ref if buf is None else buf for ref, buf in zip(refs, bufs)]
        self.direct = [buf is None for buf in bufs]
        self.next = 0

    def part(self, slot, value, *where):
        self.bufs[slot][where] = value

    def send(self, slot, *where):
        if self.direct[slot]:
            return
        source, target = self.bufs[slot], self.refs[slot]
        if where:
            source, target = source.at[where], target.at[where]
        copy = pltpu.make_async_copy(source, target, self.sems.at[self.next])
        self.next += 1
        copy.start()
        self.copies.append(copy)

    def put(self, slot, value):
        self.bufs[slot][...] = value
        self.send(slot)

    def finish(self):
        for copy in self.copies:
            copy.wait()


def hot(shape, dtype):
    return (shape, dtype, True)


def call(kernel, needs, outs, scal, small, name, flops, sends=None):
    arrays, parts, pinned = [], [], []
    for item in needs:
        fixed = []
        for array, source, target in item.parts:
            index = next((i for i, a in enumerate(arrays) if a is array), None)
            if index is None:
                index = len(arrays)
                arrays.append(array)
                pinned.append(item.pinned)
            fixed.append((index, source, target))
        parts.append(Need(item.shape, item.dtype, *fixed))
    copies = max(1, sum(len(item.parts) for item in parts))
    sends = max(1, len(outs) if sends is None else sends)
    here = [len(out) == 3 for out in outs]

    def run(*refs):
        refs = list(refs)
        scal_ref = refs.pop(0)
        small_refs = [refs.pop(0) for _ in small]
        in_refs = [refs.pop(0) for _ in arrays]
        out_refs = [refs.pop(0) for _ in outs]
        in_bufs = [refs.pop(0) for _ in parts]
        out_bufs = [None if stays else refs.pop(0) for stays in here]
        in_sems, out_sems = refs
        loads = Loads(parts, in_refs, in_bufs, in_sems, scal_ref)
        stores = Stores(out_refs, out_bufs, out_sems)
        kernel(scal_ref, small_refs, loads, stores)
        loads.finish()
        stores.finish()

    return pl.pallas_call(
        run,
        out_shape=[
            jax.ShapeDtypeStruct(out[0], out[1]) if stays else pltpu.HBM(out[0], out[1])
            for out, stays in zip(outs, here)
        ],
        in_specs=[pl.BlockSpec(memory_space=pltpu.SMEM)]
        + [pl.BlockSpec(memory_space=pltpu.VMEM)] * len(small)
        + [pl.BlockSpec(memory_space=pltpu.HBM if p else pl.ANY) for p in pinned],
        out_specs=[
            pl.BlockSpec(memory_space=pltpu.VMEM if stays else pltpu.HBM) for stays in here
        ],
        scratch_shapes=[pltpu.VMEM(item.shape, item.dtype) for item in parts]
        + [pltpu.VMEM(out[0], out[1]) for out, stays in zip(outs, here) if not stays]
        + [pltpu.SemaphoreType.DMA((copies,)), pltpu.SemaphoreType.DMA((sends,))],
        compiler_params=pltpu.CompilerParams(vmem_limit_bytes=32 * 1024 * 1024),
        cost_estimate=pl.CostEstimate(flops=flops, bytes_accessed=0, transcendentals=0),
        name=name,
    )(
        scal,
        *small,
        *[
            pltpu.with_memory_space_constraint(a, pltpu.HBM) if p else a
            for a, p in zip(arrays, pinned)
        ],
    )


def store_turned(scal, buf, values):
    for block in range(values.shape[1] // LANE):
        start = pl.multiple_of(scal[block] * LANE, LANE)
        buf[pl.ds(start, LANE), :] = values[:, block * LANE : (block + 1) * LANE].T


def block_of(scal, place):
    kind, value = place
    return scal[value] if kind == "table" else value


def columns(place, size, *front):
    def take(ref, scal):
        start = pl.multiple_of(block_of(scal, place) * size, size)
        return ref.at[(*front, slice(None), pl.ds(start, size))]

    return take


def lines(place, size):
    def take(ref, scal):
        start = pl.multiple_of(block_of(scal, place) * size, size)
        return ref.at[pl.ds(start, size), :]

    return take


def lanes_at(start, size):
    return lambda ref, scal: ref.at[:, pl.ds(start, size)]


def lines_at(start, size):
    return lambda ref, scal: ref.at[pl.ds(start, size), :]


def slot_at(*where):
    return lambda ref, scal: ref.at[where]


def stacked_at(index, size):
    def take(ref, scal):
        ref = ref if len(ref.shape) == 2 else ref.at[1]
        return ref.at[pl.ds(index * size, size), :]

    return take


def block_at(row, column, size):
    return lambda ref, scal: ref.at[pl.ds(row * size, size), pl.ds(column * size, size)]


def first_of(ref, scal):
    return ref if len(ref.shape) == 2 else ref.at[0]


def attn_needs(unit):
    if unit[0] == "half":
        return [need(unit[1])]
    _, qkv, out, place = unit
    depth, width = qkv.shape[1], out.shape[1]
    return [
        Need(
            (depth, 3 * LANE), BF,
            *[(qkv, columns(place, LANE, i), lanes_at(i * LANE, LANE)) for i in range(3)],
        ),
        Need((LANE, width), BF, (out, lines(place, LANE), everything)),
    ]


def up_need(pieces, size):
    parts = []
    for number, piece in enumerate(pieces):
        target = lanes_at(number * size, size)
        if piece[0] == "packed":
            parts.append((piece[1], first_of, target))
        else:
            parts.append((piece[1], columns(piece[3], size), target))
    return Need((pieces[0][-1], len(pieces) * size), BF, *parts)


def down_need(pieces, size):
    parts = []
    for number, piece in enumerate(pieces):
        width = piece[-1]
        if piece[0] == "packed":
            for index in range(width // size):
                parts.append(
                    (piece[2], stacked_at(index, size), block_at(number, index, size))
                )
        else:
            parts.append((piece[2], lines(piece[3], size), lines_at(number * size, size)))
    return Need((len(pieces) * size, pieces[0][-1]), BF, *parts)


def saved_need(pieces, size):
    parts = [
        (array, lanes_at(index * size, size), lanes_at(number * size, size))
        for number, (array, index) in enumerate(pieces)
    ]
    return Need((pieces[0][0].shape[0], len(pieces) * size), BF, *parts)


def mean_of(values):
    return jnp.mean(values, axis=-1, keepdims=True)


def bias_of(seg_col, seg_row):
    return jnp.where(seg_col == seg_row, 0.0, MASKED)


def qkv_part(kind, buf):
    return buf[:, : 3 * LANE] if kind == "half" else buf[...]


def cut_kernel(scal, small, loads, stores):
    qkv, out = loads.pop(), loads.pop()
    stores.part(0, out[...].T, slice(None), slice(3 * LANE, 4 * LANE))
    stores.part(0, qkv[...], slice(None), slice(0, 3 * LANE))
    stores.send(0)


def pack_kernel(size, scal, small, loads, stores):
    for slot in range(2):
        up, down = loads.pop(), loads.pop()
        stores.part(slot, up[...], 0)
        for index in range(down.shape[1] // size):
            block = down[:, index * size : (index + 1) * size]
            stores.part(slot, block, 1, pl.ds(index * size, size))
        stores.send(slot)


def turn_kernel(scal, small, loads, stores):
    store_turned(scal, stores.bufs[0], small[0][...])
    stores.send(0)


def attn_fwd_kernel(kinds, first, last, scal, small, loads, stores):
    col_ref, row_ref, tokens_ref = small[:3]
    tokens = tokens_ref[...]
    bias = bias_of(col_ref[...], row_ref[...])
    lane = lax.broadcasted_iota(jnp.int32, (1, LANE), 1)
    line = lax.broadcasted_iota(jnp.int32, (LANE, 1), 0)
    contexts, outs = [], []
    for number, kind in enumerate(kinds):
        weight = loads.pop()
        outs.append(loads.take() if kind == "whole" else weight)
        qkv = dot(tokens, qkv_part(kind, weight)).astype(BF)
        stores.put(number * 3, qkv)
        query, key, value = (qkv[:, i * LANE : (i + 1) * LANE] for i in range(3))
        query = query * jnp.asarray(SCALE, BF)
        value_t = value.T
        parts = []
        for head in range(2):
            mine = lane >= HDIM if head else lane < HDIM
            scores = dot_nt(jnp.where(mine, key, jnp.zeros_like(key)), query) + bias
            peak = jnp.max(scores, axis=0, keepdims=True)
            raw = jnp.exp(scores - peak)
            summed = jnp.sum(raw, axis=0, keepdims=True)
            stores.part(number * 3 + 2, peak + jnp.log(summed), pl.ds(head, 1), slice(None))
            prob = (raw * (1.0 / summed)).astype(BF)
            parts.append(dot(value_t, prob))
        stores.send(number * 3 + 2)
        context = jnp.where(line < HDIM, parts[0], parts[1]).astype(BF).T
        stores.put(number * 3 + 1, context)
        contexts.append(context)
    both = jnp.concatenate(contexts, axis=1)
    if kinds[0] == "whole":
        total = dot(both, jnp.concatenate([loads.get(slot)[...] for slot in outs], axis=0))
    else:
        total = dot_nt(both, jnp.concatenate([w[:, 3 * LANE :] for w in outs], axis=1))
    if not first:
        total = total + small[3][...]
    at = len(kinds) * 3
    if not last:
        stores.put(at, total)
        return
    gain_ref, shift_ref = small[-2:]
    pre = tokens.astype(F32) + total
    center = pre - mean_of(pre)
    inv = lax.rsqrt(mean_of(center * center) + 1e-12)
    hat = center * inv
    low = (hat * gain_ref[...] + shift_ref[...]).astype(BF)
    stores.put(at + 2, low)
    stores.put(at, hat)
    stores.put(at + 1, jnp.broadcast_to(inv, (hat.shape[0], LANE)))
    store_turned(scal, stores.bufs[at + 3], low)
    stores.send(at + 3)


def ffn_fwd_kernel(units, first, last, scal, small, loads, stores):
    low = small[0][...]
    total = None
    for number in range(units):
        up = dot(low, loads.pop()[...])
        phi_big = 0.5 + 0.5 * lax.erf(up * (0.5 ** 0.5))
        phi_small = jnp.exp(up * up * -0.5) * 0.3989422804014327
        act = (up * phi_big).astype(BF)
        stores.put(number * 2, act)
        stores.put(number * 2 + 1, (phi_big + up * phi_small).astype(BF))
        part = dot(act, loads.pop()[...])
        total = part if total is None else total + part
    if not first:
        total = total + small[1][...]
    at = units * 2
    if not last:
        stores.put(at, total)
        return
    hat_ref, gain1_ref, shift1_ref, gain2_ref, shift2_ref = small[-5:]
    gain2 = gain2_ref[...]
    pre = hat_ref[...] * gain1_ref[...] + shift1_ref[...] + total
    center = pre - mean_of(pre)
    inv = lax.rsqrt(mean_of(center * center) + 1e-12)
    hat = center * inv
    cot = loads.pop()[...].astype(F32)
    scaled = cot * gain2
    dpre = (scaled - mean_of(scaled) - hat * mean_of(scaled * hat)) * inv
    dffn = dpre.astype(BF)
    stores.put(at + 2, dffn)
    stores.put(at + 1, dpre)
    store_turned(scal, stores.bufs[at + 3], dffn)
    stores.send(at + 3)
    stores.put(at, (hat * gain2 + shift2_ref[...]).astype(BF))
    stores.put(at + 4, jnp.sum(cot * hat, axis=0, keepdims=True))
    stores.put(at + 5, jnp.sum(cot, axis=0, keepdims=True))


def split_rows(stores, low_slot, high_slot, index, value):
    step = value.shape[0] // 4
    for number in range(4):
        slot = high_slot if number % 2 else low_slot
        rows = pl.ds(number // 2 * step, step)
        stores.part(slot, value[number * step : (number + 1) * step], index, rows)


def received(value, pieces, loads):
    if not pieces:
        return value
    rows = value.shape[0] // pieces
    parts = [
        value[i * rows : (i + 1) * rows] + loads.pop()[...].astype(F32) for i in range(pieces)
    ]
    return jnp.concatenate(parts, axis=0)


def put_rows(stores, pieces, which, value):
    rows = value.shape[0] // pieces
    for i in range(pieces):
        stores.put(which * pieces + i, value[i * rows : (i + 1) * rows])


def ffn_bwd_kernel(near, pieces, last, size, scal, small, loads, stores):
    dffn_ref, dffn_t_ref, low_t_ref, acc_ref = small[:4]
    wd, slope = loads.pop(), loads.pop()
    d_up = (dot_nt(dffn_ref[...], wd[...]) * slope[...].astype(F32)).astype(BF)
    up = dot(low_t_ref[...], d_up)
    up = received(up, pieces if near else 0, loads).astype(BF)
    if near:
        for index in range(2):
            split_rows(stores, 1, 2, index, up[:, index * size : (index + 1) * size])
        stores.send(1)
        stores.send(2)
    else:
        put_rows(stores, pieces, 0, up)
    down = dot(dffn_t_ref[...], loads.pop()[...])
    down = received(down, pieces if near else 0, loads).astype(BF)
    if near:
        for index in range(2):
            stores.part(0, down[:, index * size : (index + 1) * size], index)
        stores.send(0)
    else:
        put_rows(stores, pieces, 1, down)
    total = acc_ref[...] + dot_nt(d_up, loads.pop()[...])
    at = 3 if near else 2 * pieces
    if not last:
        stores.put(at, total)
        return
    hat_ref, inv_ref, gain_ref = small[4:]
    hat = hat_ref[...]
    scaled = total * gain_ref[...]
    inv = inv_ref[:, :1]
    dpre = (scaled - mean_of(scaled) - hat * mean_of(scaled * hat)) * inv
    datt = dpre.astype(BF)
    stores.put(at + 1, datt)
    stores.put(at, dpre)
    store_turned(scal, stores.bufs[at + 2], datt)
    stores.send(at + 2)
    stores.put(at + 3, jnp.sum(total * hat, axis=0, keepdims=True))
    stores.put(at + 4, jnp.sum(total, axis=0, keepdims=True))


def attn_bwd_kernel(kind, near, has_recv, scal, small, loads, stores):
    col_ref, row_ref, datt_ref, datt_t_ref, tok_t_ref, acc_ref = small
    bias = bias_of(col_ref[...], row_ref[...])
    lane = lax.broadcasted_iota(jnp.int32, (1, LANE), 1)
    line = lax.broadcasted_iota(jnp.int32, (LANE, 1), 0)
    datt = datt_ref[...]
    weights = []
    for _ in range(2):
        weights.append((loads.take(), loads.take() if kind == "whole" else None))
    if kind == "whole":
        wo = jnp.concatenate([loads.get(slot)[...] for _, slot in weights], axis=0)
        dctx_all = dot_nt(datt, wo).astype(BF)
    else:
        wo = jnp.concatenate([loads.get(slot)[:, 3 * LANE :] for slot, _ in weights], axis=1)
        dctx_all = dot(datt, wo).astype(BF)
    grads = []
    for index in range(2):
        qkv_ref, lse_ref = loads.pop(), loads.pop()
        dctx = dctx_all[:, index * LANE : (index + 1) * LANE]
        query, key, value = (qkv_ref[:, i * LANE : (i + 1) * LANE] for i in range(3))
        query = query * jnp.asarray(SCALE, BF)
        key_t = key.T
        parts = []
        for head in range(2):
            mine = lane >= HDIM if head else lane < HDIM
            scores = dot_nt(jnp.where(mine, key, jnp.zeros_like(key)), query) + bias
            prob = jnp.exp(scores - lse_ref[head : head + 1, :])
            d_prob = dot_nt(jnp.where(mine, value, jnp.zeros_like(value)), dctx)
            inner = jnp.sum(prob * d_prob, axis=0, keepdims=True)
            d_scores = (prob * (d_prob - inner)).astype(BF)
            parts.append(
                (dot(key_t, d_scores), dot(d_scores, query), dot(prob.astype(BF), dctx))
            )
        d_query = (jnp.where(line < HDIM, parts[0][0], parts[1][0]) * SCALE).astype(BF).T
        d_key = jnp.where(lane < HDIM, parts[0][1], parts[1][1]).astype(BF)
        d_value = jnp.where(lane < HDIM, parts[0][2], parts[1][2]).astype(BF)
        grads.append(jnp.concatenate([d_query, d_key, d_value], axis=1))
    both = jnp.concatenate(grads, axis=1)
    ctx = jnp.concatenate([loads.pop()[...] for _ in range(2)], axis=1)
    qkv_grad = dot(tok_t_ref[...], both)
    out_grad = dot(datt_t_ref[...], ctx)
    for unit in range(2):
        full = jnp.concatenate(
            [
                qkv_grad[:, unit * 3 * LANE : (unit + 1) * 3 * LANE],
                out_grad[:, unit * LANE : (unit + 1) * LANE],
            ],
            axis=1,
        )
        if has_recv:
            full = full + loads.pop()[...].astype(F32)
        full = full.astype(BF)
        if near:
            stores.part(0, full[:, : 2 * LANE], unit)
            stores.send(0, unit)
            split_rows(stores, 1, 2, unit, full[:, 2 * LANE :])
            stores.send(1, unit)
            stores.send(2, unit)
        else:
            stores.part(0, full, unit)
            stores.send(0, unit)
    wqkv = jnp.concatenate([qkv_part(kind, loads.get(slot)) for slot, _ in weights], axis=1)
    stores.put(3 if near else 1, acc_ref[...] + dot_nt(both, wqkv))


def swap(value, axis, bit):
    count = lax.axis_size(axis)
    return lax.ppermute(value, axis, [(i, i ^ bit) for i in range(count)])


def add(*values):
    total = values[0].astype(F32)
    for value in values[1:]:
        total = total + value.astype(F32)
    return total.astype(BF)


def tie(values, *after):
    return list(lax.optimization_barrier((tuple(values), after))[0])


def sync(values, arrived):
    return lax.optimization_barrier((*values, *arrived))


def join(values, axis=0):
    return jnp.concatenate(values, axis=axis)


def body(
    tokens,
    segment_ids,
    qkv_weight,
    out_weight,
    up_weight,
    down_weight,
    gain_attn,
    shift_attn,
    gain_ffn,
    shift_ffn,
    cotangent,
):
    count, width = tokens.shape
    seq, tp = lax.axis_size("seq"), lax.axis_size("tp")
    me_seq, me_tp = lax.axis_index("seq"), lax.axis_index("tp")
    blocks = width // LANE
    pairs = blocks // 2
    size = up_weight.shape[1] * tp // (4 * pairs)
    fast = seq == blocks and seq == 8 and tp == 4 and qkv_weight.shape[2] == 2 * LANE
    seg = lax.dynamic_slice_in_dim(segment_ids, me_tp, 1, axis=0)
    seg_col = seg.reshape(count, 1)
    gains = [g.reshape(1, width) for g in (gain_attn, shift_attn, gain_ffn, shift_ffn)]
    absolute = jnp.arange(blocks, dtype=jnp.int32)
    half, quarter, eighth = width // 2, width // 4, width // 8
    wide = (count, width)
    work = 2 * count * width
    bit_x, bit_z = me_seq & 1, (me_seq >> 1) & 1

    def over_x(value):
        return swap(value, "seq", 1)

    def over_z(value):
        return swap(value, "seq", 2)

    def over_y(value):
        return swap(value, "tp", 2)

    def over_core(value):
        return swap(value, "tp", 1)

    if fast:
        rel = absolute ^ me_seq
        pos = ((rel >> 1) & 1) * 4 + (rel & 1) * 2 + (rel >> 2)
        mine = me_seq & 3
        scal = jnp.stack(
            [pos[i] for i in range(blocks)] + [mine ^ r for r in range(4)] + [bit_z, 1 - bit_z]
        ).astype(jnp.int32)
        table = [("table", blocks + r) for r in range(6)]
        cut = call(
            cut_kernel, attn_needs(("whole", qkv_weight, out_weight, table[4])),
            [((width, 4 * LANE), BF)], scal, [], "cut", 1,
        )[0]
        head_a = over_y(cut)
        needs = []
        for r in (0, 3):
            own = [("whole", up_weight, down_weight, table[r], width)]
            needs += [up_need(own, size), down_need(own, size)]
        packs = call(
            functools.partial(pack_kernel, size), needs,
            [((2, width, size), BF)] * 2, scal, [], "pack", 1,
        )
        ffn_a, ffn_d = over_y(packs[0]), over_y(packs[1])
        (tokens_late,) = tie([tokens], packs[1])
        near = [over_core(w) for w in (qkv_weight, out_weight, up_weight, down_weight)]
    else:
        scal = jnp.concatenate([absolute, jnp.zeros((6,), jnp.int32)])
        qkv_all = lax.all_gather(qkv_weight, "tp", axis=2, tiled=True)
        out_all = lax.all_gather(out_weight, "tp", axis=0, tiled=True)
        up_all = lax.all_gather(up_weight, "tp", axis=1, tiled=True)
        down_all = lax.all_gather(down_weight, "tp", axis=0, tiled=True)

    kept, acts = {}, {}
    early = tokens_late if fast else tokens

    def attn_fwd(number, group, total, last):
        needs, outs = [], []
        for unit in group:
            needs += attn_needs(heads[unit])
            outs += [((count, 3 * LANE), BF), ((count, LANE), BF), ((8, count), F32)]
        if last:
            outs += [
                hot(wide, F32), hot((count, LANE), F32), hot(wide, BF), hot((width, count), BF),
            ]
        else:
            outs.append(hot(wide, F32))
        first = total is None
        small = [seg_col, seg, early] + ([] if first else [total]) + (gains[:2] if last else [])
        kinds = [heads[unit][0] for unit in group]
        res = call(
            functools.partial(attn_fwd_kernel, kinds, first, last),
            needs, outs, scal, small, f"attn_fwd{number}", 4 * work * LANE * 2,
        )
        for index, unit in enumerate(group):
            kept[unit] = tuple(res[index * 3 : index * 3 + 3])
        return res[len(group) * 3 :]

    def ffn_fwd(number, group, total, last):
        needs, outs = [], []
        for unit in group:
            pieces = [hidden[piece] for piece in unit]
            needs += [up_need(pieces, size), down_need(pieces, size)]
            outs += [((count, len(unit) * size), BF)] * 2
        first = total is None
        small = [low] + ([] if first else [total])
        if last:
            needs.append(need(cotangent))
            small += [hat, *gains]
            outs += [
                (wide, BF), hot(wide, F32), hot(wide, BF), hot((width, count), BF),
                hot((1, width), F32), hot((1, width), F32),
            ]
        else:
            outs.append(hot(wide, F32))
        res = call(
            functools.partial(ffn_fwd_kernel, len(group), first, last),
            needs, outs, scal, small, f"ffn_fwd{number}", 8 * work * size * len(group),
        )
        for index, unit in enumerate(group):
            for place, piece in enumerate(unit):
                acts[piece] = [(array, place) for array in res[index * 2 : index * 2 + 2]]
        return res[len(group) * 2 :]

    if fast:
        heads, hidden = {}, {}
        for h in range(2):
            heads[0, h] = ("whole", qkv_weight, out_weight, table[4 + h])
            heads[1, h] = ("whole", *near[:2], table[4 + h])
        for r in range(4):
            hidden[0, r] = ("whole", up_weight, down_weight, table[r], width)
            hidden[1, r] = ("whole", *near[2:], table[r], width)

        def packed(r, both):
            hidden[2, r] = ("packed", both, both, width)
            other = over_core(both)
            hidden[3, r] = ("packed", other, other, width)

        (total,) = attn_fwd(0, [(0, 0), (0, 1)], None, False)
        (total,) = attn_fwd(1, [(1, 0), (1, 1)], total, False)
        (head_a,) = tie([head_a], total)
        head_b = over_z(head_a)
        heads[2, 0], heads[3, 0] = ("half", head_a), ("half", over_core(head_a))
        (total,) = attn_fwd(2, [(2, 0)], total, False)
        (total,) = attn_fwd(3, [(3, 0)], total, False)
        tok_t = call(
            turn_kernel, [], [hot((width, count), BF)], scal, tie([tokens], total), "turn", 1
        )[0]
        ffn_a, head_b = tie([ffn_a, head_b], tok_t)
        heads[2, 1], heads[3, 1] = ("half", head_b), ("half", over_core(head_b))
        ffn_b, ffn_c = over_x(ffn_a), over_z(ffn_a)
        packed(0, ffn_a)
        (total,) = attn_fwd(4, [(2, 1)], total, False)
        hat, inv, low, low_t = attn_fwd(5, [(3, 1)], total, True)
        (total,) = ffn_fwd(0, [[(0, 0), (0, 1)], [(0, 2), (0, 3)]], None, False)
        (total,) = ffn_fwd(1, [[(1, 0), (1, 1)], [(1, 2), (1, 3)]], total, False)
        for r, both in zip((1, 2, 3), tie([ffn_b, ffn_c, ffn_d], total)):
            packed(r, both)
        (total,) = ffn_fwd(2, [[(2, 0), (3, 0)]], total, False)
        (total,) = ffn_fwd(3, [[(2, 1), (2, 2)], [(3, 1), (3, 2)]], total, False)
        res = ffn_fwd(4, [[(2, 3), (3, 3)]], total, True)
    else:
        heads = {
            (k // 2, k % 2): ("whole", qkv_all, out_all, ("block", k)) for k in range(blocks)
        }
        hidden = {
            (k // 4, k % 4): ("whole", up_all, down_all, ("block", k), width)
            for k in range(4 * pairs)
        }
        tok_t = call(
            turn_kernel, [], [hot((width, count), BF)], scal, [tokens], "turn", 1
        )[0]
        total = None
        for j in range(pairs):
            res = attn_fwd(j, [(j, 0), (j, 1)], total, j == pairs - 1)
            total = res[0]
        hat, inv, low, low_t = res
        total = None
        for j in range(pairs):
            res = ffn_fwd(j, [[(j, 0), (j, 1)], [(j, 2), (j, 3)]], total, j == pairs - 1)
            total = res[0]
    mixed, d_pre, d_ffn, d_ffn_t, g_gain2, g_shift2 = res

    order = [3, 1, 2, 0] if fast else list(range(pairs))
    ffn_g, attn_g, ffn_got, attn_got = {}, {}, {}, {}
    total = d_pre
    for u in range(2):
        for j in order:
            last = j == order[-1] and u == 1
            here = not fast or j % 2 == 0
            recv = ffn_got.get((j, u))
            pieces = [hidden[j, 2 * u + i] for i in range(2)]
            saved = [acts[j, 2 * u + i] for i in range(2)]
            needs = [down_need(pieces, size), saved_need([s[1] for s in saved], size)]
            split = SPLIT[u] if fast else 0
            if recv is not None:
                needs += [need(g, False) for g in recv[:split]]
            needs.append(saved_need([s[0] for s in saved], size))
            if recv is not None:
                needs += [need(g, False) for g in recv[split:]]
            needs.append(up_need(pieces, size))
            small = [d_ffn, d_ffn_t, low_t, total]
            if here:
                outs = [((2, width, size), BF), ((2, half, size), BF), ((2, half, size), BF)]
            else:
                outs = [((width // split, 2 * size), BF)] * (2 * split)
            grads = len(outs)
            if last:
                small += [hat, inv, gains[0]]
                outs = outs + [
                    hot(wide, F32), hot(wide, BF), hot((width, count), BF),
                    hot((1, width), F32), hot((1, width), F32),
                ]
            else:
                outs = outs + [hot(wide, F32)]
            res = call(
                functools.partial(ffn_bwd_kernel, here, split, last, size),
                needs, outs, scal, small, f"ffn_bwd{j}{u}", 16 * work * size,
            )
            ffn_g[j, u] = res[:grads]
            if not here:
                ffn_got[j - 1, u] = [over_core(g) for g in res[:grads]]
            total = res[grads]
            if fast and (j, u) == (2, 0):
                far_y = {0: over_y(ffn_g[2, 0][0])}
            if fast and (j, u) == (0, 0):
                first_x = over_x(join([ffn_g[2, 0][2], ffn_g[0, 0][2]]))
            if fast and (j, u) == (2, 1):
                far_y[1] = over_y(ffn_g[2, 1][0])
                far_x = {1: over_x(ffn_g[2, 1][2])}
    d_pre_one, d_att, d_att_t, g_gain1, g_shift1 = res[grads:]

    norm_grads = join([g_gain1, g_shift1, g_gain2, g_shift2])

    def flip(value):
        return join([value[1:], value[:1]])

    def turn_halves(value):
        return join([value[2:], value[:2]])

    def flip_pairs(value):
        return join([value[1:2], value[:1], value[3:], value[2:3]])

    def last_step(value):
        return value[:, :eighth].astype(F32) + swap(value[:, eighth:], "seq", 4).astype(F32)

    total = d_pre_one
    for number, j in enumerate(order):
        here = not fast or j % 2 == 0
        recv = attn_got.get(j)
        if fast:
            if number == 0:
                near_x = {1: over_x(ffn_g[0, 1][2])}
                total, far_y[0], first_x = sync([total], [far_y[0], first_x])
                far_x[0], near_x[0] = first_x[:2], first_x[2:]
                down_z = {0: over_z(add(ffn_g[0, 0][0][:, half:], far_y[0][:, half:]))}
                far = {0: add(ffn_g[2, 0][1], flip(far_x[0]))}
                near = {0: add(ffn_g[0, 0][1], flip(near_x[0]))}
            if number == 1:
                total, far_x[1] = sync([total], [far_x[1]])
                far[1] = add(ffn_g[2, 1][1], flip(far_x[1]))
                far = join([far[0], far[1]])
                far_z = over_z(far[:, quarter:])
            if number == 2:
                total, far_y[1], near_x[1], far_z = sync([total], [far_y[1], near_x[1], far_z])
                down_z[1] = over_z(add(ffn_g[0, 1][0][:, half:], far_y[1][:, half:]))
                up_y = over_y(add(far[:, :quarter], turn_halves(far_z)))
                near[1] = add(ffn_g[0, 1][1], flip(near_x[1]))
                near = join([near[0], near[1]])
                near_z = over_z(near[:, quarter:])
            if number == 3:
                qk_y = over_y(attn_g[2][0])
                vo_x = over_x(attn_g[2][2])
                total, down_z[0], down_z[1] = sync([total], [down_z[0], down_z[1]])
                down = join(
                    [
                        add(ffn_g[0, u][0][:, :half], far_y[u][:, :half], down_z[1 - u])
                        for u in range(2)
                    ]
                )
                down_x = over_x(down[:, quarter:])
        needs = []
        for h in range(2):
            needs += attn_needs(heads[j, h])
        for h in range(2):
            needs += [need(kept[j, h][0]), need(kept[j, h][2])]
        needs += [need(kept[j, h][1]) for h in range(2)]
        if recv is not None:
            needs += [
                Need(recv.shape[1:], BF, (recv, slot_at(h), everything), pinned=False)
                for h in range(2)
            ]
        if here:
            outs = [
                ((2, width, 2 * LANE), BF), ((2, half, 2 * LANE), BF), ((2, half, 2 * LANE), BF),
            ]
        else:
            outs = [((2, width, 4 * LANE), BF)]
        res = call(
            functools.partial(attn_bwd_kernel, heads[j, 0][0], here, recv is not None),
            needs, outs + [hot(wide, F32)], scal, [seg_col, seg, d_att, d_att_t, tok_t, total],
            f"attn_bwd{j}", 12 * work * LANE * 2, 2 * len(outs) + 1,
        )
        attn_g[j], total = res[:-1], res[-1]
        if not here:
            attn_got[j - 1] = over_core(res[0])
    token_grad = total

    if fast:
        vo_near_x = over_x(attn_g[0][2])
        vo_far = add(attn_g[2][1], vo_x)
        vo_z = over_z(vo_far[:, quarter:])
        down_x, near_z, up_y, norm_grads = tie([down_x, near_z, up_y, norm_grads], total)
        down = last_step(add(down[:, :quarter], flip_pairs(down_x)))
        up = last_step(add(near[:, :quarter], turn_halves(near_z), up_y))
        vo_y = over_y(add(vo_far[:, :quarter], flip(vo_z)))
        for axis, bit in (("tp", 1), ("tp", 2), ("seq", 1), ("seq", 2), ("seq", 4)):
            norm_grads = norm_grads + swap(norm_grads, axis, bit)
        share = width // (seq * tp)
        norm_grads = lax.dynamic_slice_in_dim(
            norm_grads, (me_seq * tp + me_tp) * share, share, axis=1
        )
        vo_near = add(attn_g[0][1], vo_near_x)
        vo_near_z = over_z(vo_near[:, quarter:])
        qk_z = over_z(add(attn_g[0][0][:, half:], qk_y[:, half:]))
        vo = last_step(add(vo_near[:, :quarter], flip(vo_near_z), vo_y))
        qk = add(attn_g[0][0][:, :half], qk_y[:, :half], flip(qk_z))
        qk = last_step(add(qk[:, :quarter], over_x(qk[:, quarter:])))

        def ordered(value):
            flipped = jnp.where(bit_z == 0, value, flip(value))
            return join([flipped[0], flipped[1]], 1)

        def ordered_four(value):
            value = jnp.where(bit_x == 0, value, flip_pairs(value))
            value = jnp.where(bit_z == 0, value, turn_halves(value))
            return join([value[r] for r in range(4)], 1)

        down_grad = ordered_four(down).T
        up_grad = ordered_four(up)
        qkv_grad = jnp.stack(
            [ordered(qk[:, :, :LANE]), ordered(qk[:, :, LANE:]), ordered(vo[:, :, :LANE])]
        )
        out_grad = ordered(vo[:, :, LANE:]).T
    else:
        norm_grads = lax.psum_scatter(norm_grads, ("seq", "tp"), scatter_dimension=1, tiled=True)

        def scattered(value, tp_dim, seq_dim):
            value = lax.psum_scatter(value, "tp", scatter_dimension=tp_dim, tiled=True)
            value = lax.psum_scatter(value, "seq", scatter_dimension=seq_dim, tiled=True)
            return value.astype(F32)

        def rows_of(low_part, high_part):
            parts = [low_part[:quarter], high_part[:quarter], low_part[quarter:], high_part[quarter:]]
            return join(parts)

        both = [(j, u) for j in range(pairs) for u in range(2)]
        down = join([ffn_g[k][0][i] for k in both for i in range(2)], 1)
        up = join([rows_of(ffn_g[k][1][i], ffn_g[k][2][i]) for k in both for i in range(2)], 1)
        qk = [attn_g[j][0][h] for j, h in both]
        vo = [rows_of(attn_g[j][1][h], attn_g[j][2][h]) for j, h in both]
        down_grad = scattered(down, 1, 0).T
        up_grad = scattered(up, 1, 0)
        qkv_grad = jnp.stack(
            [
                join([g[:, :LANE] for g in qk], 1),
                join([g[:, LANE:] for g in qk], 1),
                join([g[:, :LANE] for g in vo], 1),
            ]
        )
        qkv_grad = scattered(qkv_grad, 2, 1)
        out_grad = scattered(join([g[:, LANE:] for g in vo], 1), 1, 0).T
    return (mixed, token_grad, qkv_grad, out_grad, up_grad, down_grad, norm_grads)


def solution(mesh):
    return jax.shard_map(
        body,
        mesh=mesh,
        in_specs=(
            P(("seq", "tp"), None),
            P("seq", None),
            P(None, None, "tp"),
            P("tp", None),
            P(None, "tp"),
            P("tp", None),
            P(),
            P(),
            P(),
            P(),
            P(("seq", "tp"), None),
        ),
        out_specs=(
            P(("seq", "tp"), None),
            P(("seq", "tp"), None),
            P(None, "seq", "tp"),
            P("tp", "seq"),
            P("seq", "tp"),
            P("tp", "seq"),
            P(None, ("seq", "tp")),
        ),
        check_vma=False,
    )
```

```python
import functools

import jax
import jax.numpy as jnp
from jax import lax
from jax.experimental import pallas as pl
from jax.experimental.pallas import tpu as pltpu
from jax.sharding import PartitionSpec as P

HDIM = 64
LANE = 128
BF = jnp.bfloat16
F32 = jnp.float32
SCALE = HDIM ** (-0.5)
MASKED = -1000000000.0


def dot(left, right):
    return jnp.dot(left, right, preferred_element_type=F32)


def dot_nt(left, right):
    return lax.dot_general(left, right, (((1,), (1,)), ((), ())), preferred_element_type=F32)


def everything(ref, scal):
    return ref


class Need:
    def __init__(self, shape, dtype, *parts, pinned=True):
        self.shape, self.dtype, self.parts, self.pinned = tuple(shape), dtype, parts, pinned


def need(array, pinned=True):
    return Need(array.shape, array.dtype, (array, everything, everything), pinned=pinned)


class Loads:
    def __init__(self, needs, refs, bufs, sems, scal):
        self.bufs, self.copies, self.next = bufs, [], 0
        at = 0
        for item, buf in zip(needs, bufs):
            mine = []
            for index, source, target in item.parts:
                copy = pltpu.make_async_copy(
                    source(refs[index], scal), target(buf, scal), sems.at[at]
                )
                copy.start()
                mine.append(copy)
                at += 1
            self.copies.append(mine)

    def take(self):
        self.next += 1
        return self.next - 1

    def get(self, slot):
        for copy in self.copies[slot]:
            copy.wait()
        self.copies[slot] = []
        return self.bufs[slot]

    def pop(self):
        return self.get(self.take())

    def finish(self):
        for slot in range(len(self.copies)):
            self.get(slot)


class Stores:
    def __init__(self, refs, bufs, sems):
        self.refs, self.sems, self.copies = refs, sems, []
        self.bufs = [ref if buf is None else buf for ref, buf in zip(refs, bufs)]
        self.direct = [buf is None for buf in bufs]
        self.next = 0

    def part(self, slot, value, *where):
        self.bufs[slot][where] = value

    def send(self, slot, *where):
        if self.direct[slot]:
            return
        source, target = self.bufs[slot], self.refs[slot]
        if where:
            source, target = source.at[where], target.at[where]
        copy = pltpu.make_async_copy(source, target, self.sems.at[self.next])
        self.next += 1
        copy.start()
        self.copies.append(copy)

    def put(self, slot, value):
        self.bufs[slot][...] = value
        self.send(slot)

    def finish(self):
        for copy in self.copies:
            copy.wait()


def hot(shape, dtype):
    return (shape, dtype, True)


def call(kernel, needs, outs, scal, small, name, flops, sends=None):
    arrays, parts, pinned = [], [], []
    for item in needs:
        fixed = []
        for array, source, target in item.parts:
            index = next((i for i, a in enumerate(arrays) if a is array), None)
            if index is None:
                index = len(arrays)
                arrays.append(array)
                pinned.append(item.pinned)
            fixed.append((index, source, target))
        parts.append(Need(item.shape, item.dtype, *fixed))
    copies = max(1, sum(len(item.parts) for item in parts))
    sends = max(1, len(outs) if sends is None else sends)
    here = [len(out) == 3 for out in outs]

    def run(*refs):
        refs = list(refs)
        scal_ref = refs.pop(0)
        small_refs = [refs.pop(0) for _ in small]
        in_refs = [refs.pop(0) for _ in arrays]
        out_refs = [refs.pop(0) for _ in outs]
        in_bufs = [refs.pop(0) for _ in parts]
        out_bufs = [None if stays else refs.pop(0) for stays in here]
        in_sems, out_sems = refs
        loads = Loads(parts, in_refs, in_bufs, in_sems, scal_ref)
        stores = Stores(out_refs, out_bufs, out_sems)
        kernel(scal_ref, small_refs, loads, stores)
        loads.finish()
        stores.finish()

    return pl.pallas_call(
        run,
        out_shape=[
            jax.ShapeDtypeStruct(out[0], out[1]) if stays else pltpu.HBM(out[0], out[1])
            for out, stays in zip(outs, here)
        ],
        in_specs=[pl.BlockSpec(memory_space=pltpu.SMEM)]
        + [pl.BlockSpec(memory_space=pltpu.VMEM)] * len(small)
        + [pl.BlockSpec(memory_space=pltpu.HBM if p else pl.ANY) for p in pinned],
        out_specs=[
            pl.BlockSpec(memory_space=pltpu.VMEM if stays else pltpu.HBM) for stays in here
        ],
        scratch_shapes=[pltpu.VMEM(item.shape, item.dtype) for item in parts]
        + [pltpu.VMEM(out[0], out[1]) for out, stays in zip(outs, here) if not stays]
        + [pltpu.SemaphoreType.DMA((copies,)), pltpu.SemaphoreType.DMA((sends,))],
        compiler_params=pltpu.CompilerParams(vmem_limit_bytes=32 * 1024 * 1024),
        cost_estimate=pl.CostEstimate(flops=flops, bytes_accessed=0, transcendentals=0),
        name=name,
    )(
        scal,
        *small,
        *[
            pltpu.with_memory_space_constraint(a, pltpu.HBM) if p else a
            for a, p in zip(arrays, pinned)
        ],
    )


def store_turned(scal, buf, values):
    for block in range(values.shape[1] // LANE):
        start = pl.multiple_of(scal[block] * LANE, LANE)
        buf[pl.ds(start, LANE), :] = values[:, block * LANE : (block + 1) * LANE].T


def block_of(scal, place):
    kind, value = place
    return scal[value] if kind == "table" else value


def columns(place, size, *front):
    def take(ref, scal):
        start = pl.multiple_of(block_of(scal, place) * size, size)
        return ref.at[(*front, slice(None), pl.ds(start, size))]

    return take


def lines(place, size):
    def take(ref, scal):
        start = pl.multiple_of(block_of(scal, place) * size, size)
        return ref.at[pl.ds(start, size), :]

    return take


def lanes_at(start, size):
    return lambda ref, scal: ref.at[:, pl.ds(start, size)]


def lines_at(start, size):
    return lambda ref, scal: ref.at[pl.ds(start, size), :]


def slot_at(*where):
    return lambda ref, scal: ref.at[where]


def stacked_at(index, size):
    def take(ref, scal):
        ref = ref if len(ref.shape) == 2 else ref.at[1]
        return ref.at[pl.ds(index * size, size), :]

    return take


def block_at(row, column, size):
    return lambda ref, scal: ref.at[pl.ds(row * size, size), pl.ds(column * size, size)]


def first_of(ref, scal):
    return ref if len(ref.shape) == 2 else ref.at[0]


def part_of(place):
    def find(scal):
        quarter = block_of(scal, place)
        return quarter // 2, lax.rem(quarter, 2)

    return find


def matrix_at(place, which):
    def take(ref, scal):
        half, pair = part_of(place)(scal)
        index = 1 if which else 2 * pair
        return ref.at[index, :, pl.ds(pl.multiple_of(half * LANE, LANE), LANE)]

    return take


def out_rows_at(place):
    def take(ref, scal):
        half, _ = part_of(place)(scal)
        return ref.at[pl.ds(pl.multiple_of(half * LANE, LANE), LANE), :]

    return take


def piece_lanes(place, which):
    def take(buf, scal):
        half, pair = part_of(place)(scal)
        start = pair * 4 * LANE + half * LANE + which * 2 * LANE
        return buf.at[:, pl.ds(pl.multiple_of(start, LANE), LANE)]

    return take


def attn_needs(block, pinned=True):
    if block[0] == "packed":
        pieces = block[1]
        parts = [
            (piece, lanes_at(which * LANE, LANE), piece_lanes(("table", 8 + r), which))
            for r, piece in enumerate(pieces)
            for which in range(2)
        ]
        return [Need((pieces[0].shape[0], 8 * LANE), BF, *parts, pinned=pinned)]
    _, qkv, out, index = block
    depth, width = qkv.shape[1], out.shape[1]
    place = ("block", index)
    return [
        Need(
            (depth, 6 * LANE), BF,
            *[
                (qkv, columns(place, 2 * LANE, i), lanes_at(2 * i * LANE, 2 * LANE))
                for i in range(3)
            ],
        ),
        Need((2 * LANE, width), BF, (out, lines(place, 2 * LANE), everything)),
    ]


def up_need(pieces, size, pinned=True):
    parts = []
    for number, piece in enumerate(pieces):
        target = lanes_at(number * size, size)
        if piece[0] == "packed":
            parts.append((piece[1], first_of, target))
        else:
            parts.append((piece[1], columns(piece[3], size), target))
    return Need((pieces[0][-1], len(pieces) * size), BF, *parts, pinned=pinned)


def down_need(pieces, size, pinned=True):
    parts = []
    for number, piece in enumerate(pieces):
        width = piece[-1]
        if piece[0] == "packed":
            for index in range(width // size):
                parts.append(
                    (piece[2], stacked_at(index, size), block_at(number, index, size))
                )
        else:
            parts.append((piece[2], lines(piece[3], size), lines_at(number * size, size)))
    return Need((len(pieces) * size, pieces[0][-1]), BF, *parts, pinned=pinned)


def saved_need(pieces, size):
    parts = [
        (array, lanes_at(index * size, size), lanes_at(number * size, size))
        for number, (array, index) in enumerate(pieces)
    ]
    return Need((pieces[0][0].shape[0], len(pieces) * size), BF, *parts)


def mean_of(values):
    return jnp.mean(values, axis=-1, keepdims=True)


def bias_of(seg_col, seg_row):
    return jnp.where(seg_col == seg_row, 0.0, MASKED)


def cut_kernel(places, scal, small, loads, stores):
    for slot, place in enumerate(places):
        first, second, out = loads.pop(), loads.pop(), loads.pop()
        _, pair = part_of(place)(scal)
        stores.part(slot, first[...], slice(None), slice(0, LANE))

        @pl.when(pair == 0)
        def _():
            stores.part(slot, second[...], slice(None), slice(LANE, 2 * LANE))

        @pl.when(pair == 1)
        def _():
            stores.part(slot, out[...].T, slice(None), slice(LANE, 2 * LANE))

        stores.send(slot)


def pack_kernel(size, scal, small, loads, stores):
    for slot in range(2):
        up, down = loads.pop(), loads.pop()
        stores.part(slot, up[...], 0)
        for index in range(down.shape[1] // size):
            block = down[:, index * size : (index + 1) * size]
            stores.part(slot, block, 1, pl.ds(index * size, size))
        stores.send(slot)


def turn_kernel(scal, small, loads, stores):
    store_turned(scal, stores.bufs[0], small[0][...])
    stores.send(0)


def head_parts(qkv, unit):
    query, key, value = (
        qkv[:, (2 * i + unit) * LANE : (2 * i + unit + 1) * LANE] for i in range(3)
    )
    return query * jnp.asarray(SCALE, BF), key, value


def attn_fwd_kernel(kind, first, last, scal, small, loads, stores):
    col_ref, row_ref, tokens_ref = small[:3]
    tokens = tokens_ref[...]
    bias = bias_of(col_ref[...], row_ref[...])
    lane = lax.broadcasted_iota(jnp.int32, (1, LANE), 1)
    line = lax.broadcasted_iota(jnp.int32, (LANE, 1), 0)
    weight = loads.pop()
    qkv = dot(tokens, weight[:, : 6 * LANE]).astype(BF)
    stores.put(0, qkv)
    contexts = []
    for unit in range(2):
        query, key, value = head_parts(qkv, unit)
        value_t = value.T
        parts = []
        for head in range(2):
            mine = lane >= HDIM if head else lane < HDIM
            scores = dot_nt(jnp.where(mine, key, jnp.zeros_like(key)), query) + bias
            peak = jnp.max(scores, axis=0, keepdims=True)
            raw = jnp.exp(scores - peak)
            summed = jnp.sum(raw, axis=0, keepdims=True)
            stores.part(2, peak + jnp.log(summed), pl.ds(2 * unit + head, 1), slice(None))
            prob = (raw * (1.0 / summed)).astype(BF)
            parts.append(dot(value_t, prob))
        contexts.append(jnp.where(line < HDIM, parts[0], parts[1]).astype(BF).T)
    stores.send(2)
    both = jnp.concatenate(contexts, axis=1)
    stores.put(1, both)
    if kind == "whole":
        total = dot(both, loads.pop()[...])
    else:
        total = dot_nt(both, weight[:, 6 * LANE :])
    if not first:
        total = total + small[3][...]
    at = 3
    if not last:
        stores.put(at, total)
        return
    gain_ref, shift_ref = small[-2:]
    pre = tokens.astype(F32) + total
    center = pre - mean_of(pre)
    inv = lax.rsqrt(mean_of(center * center) + 1e-12)
    hat = center * inv
    low = (hat * gain_ref[...] + shift_ref[...]).astype(BF)
    stores.put(at + 2, low)
    stores.put(at, hat)
    stores.put(at + 1, jnp.broadcast_to(inv, (hat.shape[0], LANE)))
    store_turned(scal, stores.bufs[at + 3], low)
    stores.send(at + 3)


def ffn_fwd_kernel(units, first, last, scal, small, loads, stores):
    low = small[0][...]
    total = None
    for number in range(units):
        up = dot(low, loads.pop()[...])
        phi_big = 0.5 + 0.5 * lax.erf(up * (0.5 ** 0.5))
        phi_small = jnp.exp(up * up * -0.5) * 0.3989422804014327
        act = (up * phi_big).astype(BF)
        stores.put(number * 2, act)
        stores.put(number * 2 + 1, (phi_big + up * phi_small).astype(BF))
        part = dot(act, loads.pop()[...])
        total = part if total is None else total + part
    if not first:
        total = total + small[1][...]
    at = units * 2
    if not last:
        stores.put(at, total)
        return
    hat_ref, gain1_ref, shift1_ref, gain2_ref, shift2_ref = small[-5:]
    gain2 = gain2_ref[...]
    pre = hat_ref[...] * gain1_ref[...] + shift1_ref[...] + total
    center = pre - mean_of(pre)
    inv = lax.rsqrt(mean_of(center * center) + 1e-12)
    hat = center * inv
    cot = loads.pop()[...].astype(F32)
    scaled = cot * gain2
    dpre = (scaled - mean_of(scaled) - hat * mean_of(scaled * hat)) * inv
    dffn = dpre.astype(BF)
    stores.put(at + 2, dffn)
    stores.put(at + 1, dpre)
    store_turned(scal, stores.bufs[at + 3], dffn)
    stores.send(at + 3)
    stores.put(at, (hat * gain2 + shift2_ref[...]).astype(BF))
    stores.put(at + 4, jnp.sum(cot * hat, axis=0, keepdims=True))
    stores.put(at + 5, jnp.sum(cot, axis=0, keepdims=True))


def split_rows(stores, slot, where, value):
    step = value.shape[0] // 4
    for number in range(4):
        rows = pl.ds(number // 2 * step, step)
        stores.part(slot, value[number * step : (number + 1) * step], number % 2, *where, rows)


def ffn_bwd_kernel(last, size, scal, small, loads, stores):
    dffn_ref, dffn_t_ref, low_t_ref, acc_ref = small[:4]
    wd, slope = loads.pop(), loads.pop()
    d_up = (dot_nt(dffn_ref[...], wd[...]) * slope[...].astype(F32)).astype(BF)
    down = dot(dffn_t_ref[...], loads.pop()[...]).astype(BF)
    for index in range(2):
        stores.part(0, down[:, index * size : (index + 1) * size], index)
    stores.send(0)
    up = dot(low_t_ref[...], d_up).astype(BF)
    for index in range(2):
        split_rows(stores, 1, (index,), up[:, index * size : (index + 1) * size])
    stores.send(1)
    total = acc_ref[...] + dot_nt(d_up, loads.pop()[...])
    at = 2
    if not last:
        stores.put(at, total)
        return
    hat_ref, inv_ref, gain_ref = small[4:]
    hat = hat_ref[...]
    scaled = total * gain_ref[...]
    inv = inv_ref[:, :1]
    dpre = (scaled - mean_of(scaled) - hat * mean_of(scaled * hat)) * inv
    datt = dpre.astype(BF)
    stores.put(at + 1, datt)
    stores.put(at, dpre)
    store_turned(scal, stores.bufs[at + 2], datt)
    stores.send(at + 2)
    stores.put(at + 3, jnp.sum(total * hat, axis=0, keepdims=True))
    stores.put(at + 4, jnp.sum(total, axis=0, keepdims=True))


def attn_bwd_kernel(kind, scal, small, loads, stores):
    col_ref, row_ref, datt_ref, datt_t_ref, tok_t_ref, acc_ref = small
    bias = bias_of(col_ref[...], row_ref[...])
    lane = lax.broadcasted_iota(jnp.int32, (1, LANE), 1)
    line = lax.broadcasted_iota(jnp.int32, (LANE, 1), 0)
    weight = loads.pop()
    if kind == "whole":
        dctx_all = dot_nt(datt_ref[...], loads.pop()[...]).astype(BF)
    else:
        dctx_all = dot(datt_ref[...], weight[:, 6 * LANE :]).astype(BF)
    qkv, lse = loads.pop(), loads.pop()
    grads = [[], [], []]
    for unit in range(2):
        dctx = dctx_all[:, unit * LANE : (unit + 1) * LANE]
        query, key, value = head_parts(qkv, unit)
        key_t = key.T
        parts = []
        for head in range(2):
            mine = lane >= HDIM if head else lane < HDIM
            scores = dot_nt(jnp.where(mine, key, jnp.zeros_like(key)), query) + bias
            row = 2 * unit + head
            prob = jnp.exp(scores - lse[row : row + 1, :])
            d_prob = dot_nt(jnp.where(mine, value, jnp.zeros_like(value)), dctx)
            inner = jnp.sum(prob * d_prob, axis=0, keepdims=True)
            d_scores = (prob * (d_prob - inner)).astype(BF)
            parts.append(
                (dot(key_t, d_scores), dot(d_scores, query), dot(prob.astype(BF), dctx))
            )
        d_query = (jnp.where(line < HDIM, parts[0][0], parts[1][0]) * SCALE).astype(BF).T
        grads[0].append(d_query)
        grads[1].append(jnp.where(lane < HDIM, parts[0][1], parts[1][1]).astype(BF))
        grads[2].append(jnp.where(lane < HDIM, parts[0][2], parts[1][2]).astype(BF))
    tok_t = tok_t_ref[...]
    both = jnp.concatenate(grads[0] + grads[1] + grads[2], axis=1)
    stores.put(0, dot(tok_t, both[:, : 4 * LANE]).astype(BF))
    vo = jnp.concatenate(
        [dot(tok_t, both[:, 4 * LANE :]), dot(datt_t_ref[...], loads.pop()[...])], axis=1
    )
    split_rows(stores, 1, (), vo.astype(BF))
    stores.send(1)
    stores.put(2, acc_ref[...] + dot_nt(both, weight[:, : 6 * LANE]))


def swap(value, axis, bit):
    count = lax.axis_size(axis)
    return lax.ppermute(value, axis, [(i, i ^ bit) for i in range(count)])


def add(*values):
    total = values[0].astype(F32)
    for value in values[1:]:
        total = total + value.astype(F32)
    return total.astype(BF)


def tie(values, *after):
    return list(lax.optimization_barrier((tuple(values), after))[0])


def sync(values, arrived):
    return lax.optimization_barrier((*values, *arrived))


def join(values, axis=0):
    return jnp.concatenate(values, axis=axis)


def body(
    tokens,
    segment_ids,
    qkv_weight,
    out_weight,
    up_weight,
    down_weight,
    gain_attn,
    shift_attn,
    gain_ffn,
    shift_ffn,
    cotangent,
):
    count, width = tokens.shape
    seq, tp = lax.axis_size("seq"), lax.axis_size("tp")
    me_seq, me_tp = lax.axis_index("seq"), lax.axis_index("tp")
    blocks = width // LANE
    pairs = blocks // 2
    size = up_weight.shape[1] * tp // (4 * pairs)
    fast = seq == blocks and seq == 8 and tp == 4 and qkv_weight.shape[2] == 2 * LANE
    seg = lax.dynamic_slice_in_dim(segment_ids, me_tp, 1, axis=0)
    seg_col = seg.reshape(count, 1)
    gains = [g.reshape(1, width) for g in (gain_attn, shift_attn, gain_ffn, shift_ffn)]
    absolute = jnp.arange(blocks, dtype=jnp.int32)
    half, quarter, eighth = width // 2, width // 4, width // 8
    wide = (count, width)
    work = 2 * count * width
    bit_x, bit_z = me_seq & 1, (me_seq >> 1) & 1

    def over_x(value):
        return swap(value, "seq", 1)

    def over_z(value):
        return swap(value, "seq", 2)

    def over_y(value):
        return swap(value, "tp", 2)

    def over_core(value):
        return swap(value, "tp", 1)

    if fast:
        rel = absolute ^ me_seq
        pos = ((rel >> 1) & 1) * 4 + (rel & 1) * 2 + (rel >> 2)
        mine = me_seq & 3
        scal = jnp.stack(
            [pos[i] for i in range(blocks)] + [mine ^ r for r in range(4)]
        ).astype(jnp.int32)
        table = [("table", 8 + r) for r in range(4)]
        needs = []
        for r in (0, 3):
            shape = (width, LANE)
            needs += [
                Need(shape, BF, (qkv_weight, matrix_at(table[r], which), everything))
                for which in range(2)
            ]
            needs.append(
                Need((LANE, width), BF, (out_weight, out_rows_at(table[r]), everything))
            )
        cuts = call(
            functools.partial(cut_kernel, [table[0], table[3]]), needs,
            [((width, 2 * LANE), BF)] * 2, scal, [], "cut", 1,
        )
        head_a, head_d = over_y(cuts[0]), over_y(cuts[1])
        needs = []
        for r in (0, 3):
            own = [("whole", up_weight, down_weight, table[r], width)]
            needs += [up_need(own, size), down_need(own, size)]
        packs = call(
            functools.partial(pack_kernel, size), needs,
            [((2, width, size), BF)] * 2, scal, [], "pack", 1,
        )
        ffn_a, ffn_d = over_y(packs[0]), over_y(packs[1])
        (tokens_late,) = tie([tokens], packs[1])
        near = [over_core(w) for w in (qkv_weight, out_weight, up_weight, down_weight)]
    else:
        scal = jnp.concatenate([absolute, jnp.zeros((4,), jnp.int32)])
        qkv_all = lax.all_gather(qkv_weight, "tp", axis=2, tiled=True)
        out_all = lax.all_gather(out_weight, "tp", axis=0, tiled=True)
        up_all = lax.all_gather(up_weight, "tp", axis=1, tiled=True)
        down_all = lax.all_gather(down_weight, "tp", axis=0, tiled=True)

    kept, acts = {}, {}
    early = tokens_late if fast else tokens

    def attn_fwd(j, total, last):
        needs = attn_needs(heads[j], False)
        outs = [((count, 6 * LANE), BF), ((count, 2 * LANE), BF), ((8, count), F32)]
        if last:
            outs += [
                hot(wide, F32), hot((count, LANE), F32), hot(wide, BF), hot((width, count), BF),
            ]
        else:
            outs.append(hot(wide, F32))
        first = total is None
        small = [seg_col, seg, early] + ([] if first else [total]) + (gains[:2] if last else [])
        res = call(
            functools.partial(attn_fwd_kernel, heads[j][0], first, last),
            needs, outs, scal, small, f"attn_fwd{j}", 1,
        )
        kept[j] = res[:3]
        return res[3:]

    def ffn_fwd(number, group, total, last):
        needs, outs = [], []
        for unit in group:
            pieces = [hidden[piece] for piece in unit]
            needs += [up_need(pieces, size, False), down_need(pieces, size, False)]
            outs += [((count, len(unit) * size), BF)] * 2
        first = total is None
        small = [low] + ([] if first else [total])
        if last:
            needs.append(need(cotangent))
            small += [hat, *gains]
            outs += [
                (wide, BF), hot(wide, F32), hot(wide, BF), hot((width, count), BF),
                hot((1, width), F32), hot((1, width), F32),
            ]
        else:
            outs.append(hot(wide, F32))
        res = call(
            functools.partial(ffn_fwd_kernel, len(group), first, last),
            needs, outs, scal, small, f"ffn_fwd{number}", 8 * work * size * len(group),
        )
        for index, unit in enumerate(group):
            for place, piece in enumerate(unit):
                acts[piece] = [(array, place) for array in res[index * 2 : index * 2 + 2]]
        return res[len(group) * 2 :]

    if fast:
        heads, hidden = {}, {}
        heads[0] = ("whole", qkv_weight, out_weight, 0)
        heads[1] = ("whole", *near[:2], 0)
        for r in range(4):
            hidden[0, r] = ("whole", up_weight, down_weight, table[r], width)
            hidden[1, r] = ("whole", *near[2:], table[r], width)

        def packed(r, both):
            hidden[2, r] = ("packed", both, both, width)
            other = over_core(both)
            hidden[3, r] = ("packed", other, other, width)

        (total,) = attn_fwd(0, None, False)
        (head_a,) = tie([head_a], total)
        head_b, head_c = over_x(head_a), over_z(head_a)
        other_a = over_core(head_a)
        (total,) = attn_fwd(1, total, False)
        tok_t = call(
            turn_kernel, [], [hot((width, count), BF)], scal, tie([tokens], total), "turn", 1
        )[0]
        head_b, head_c, head_d = tie([head_b, head_c, head_d], tok_t)
        pieces = [head_a, head_b, head_c, head_d]
        heads[2] = ("packed", pieces)
        heads[3] = ("packed", [other_a] + [over_core(p) for p in pieces[1:]])
        (total,) = attn_fwd(2, total, False)
        (ffn_a,) = tie([ffn_a], total)
        ffn_b, ffn_c = over_x(ffn_a), over_z(ffn_a)
        packed(0, ffn_a)
        hat, inv, low, low_t = attn_fwd(3, total, True)
        (total,) = ffn_fwd(0, [[(0, 0), (0, 1)], [(0, 2), (0, 3)]], None, False)
        (total,) = ffn_fwd(1, [[(1, 0), (1, 1)], [(1, 2), (1, 3)]], total, False)
        for r, both in zip((1, 2, 3), tie([ffn_b, ffn_c, ffn_d], total)):
            packed(r, both)
        (total,) = ffn_fwd(2, [[(2, 0), (3, 0)]], total, False)
        (total,) = ffn_fwd(3, [[(2, 1), (2, 2)], [(3, 1), (3, 2)]], total, False)
        res = ffn_fwd(4, [[(2, 3), (3, 3)]], total, True)
    else:
        heads = {j: ("whole", qkv_all, out_all, j) for j in range(pairs)}
        hidden = {
            (k // 4, k % 4): ("whole", up_all, down_all, ("block", k), width)
            for k in range(4 * pairs)
        }
        tok_t = call(
            turn_kernel, [], [hot((width, count), BF)], scal, [tokens], "turn", 1
        )[0]
        total = None
        for j in range(pairs):
            res = attn_fwd(j, total, j == pairs - 1)
            total = res[0]
        hat, inv, low, low_t = res
        total = None
        for j in range(pairs):
            res = ffn_fwd(j, [[(j, 0), (j, 1)], [(j, 2), (j, 3)]], total, j == pairs - 1)
            total = res[0]
    mixed, d_pre, d_ffn, d_ffn_t, g_gain2, g_shift2 = res

    order = [3, 2, 1, 0] if fast else list(range(pairs))
    ffn_g, attn_g, from_core = {}, {}, {}
    down_y, up_x = {}, {}
    total = d_pre
    for u in range(2):
        for j in order:
            last = j == order[-1] and u == 1
            pieces = [hidden[j, 2 * u + i] for i in range(2)]
            saved = [acts[j, 2 * u + i] for i in range(2)]
            needs = [
                down_need(pieces, size),
                saved_need([s[1] for s in saved], size),
                saved_need([s[0] for s in saved], size),
                up_need(pieces, size),
            ]
            small = [d_ffn, d_ffn_t, low_t, total]
            outs = [((2, width, size), BF), ((2, 2, half, size), BF)]
            if last:
                small += [hat, inv, gains[0]]
                outs = outs + [
                    hot(wide, F32), hot(wide, BF), hot((width, count), BF),
                    hot((1, width), F32), hot((1, width), F32),
                ]
            else:
                outs = outs + [hot(wide, F32)]
            res = call(
                functools.partial(ffn_bwd_kernel, last, size),
                needs, outs, scal, small, f"ffn_bwd{j}{u}", 1,
            )
            ffn_g[j, u], total = res[:2], res[2]
            if fast and j % 2:
                from_core[j - 1, u] = [over_core(g) for g in res[:2]]
    d_pre_one, d_att, d_att_t, g_gain1, g_shift1 = res[2:]

    norm_grads = join([g_gain1, g_shift1, g_gain2, g_shift2])

    def flip(value):
        return join([value[1:], value[:1]])

    def turn_halves(value):
        return join([value[2:], value[:2]])

    def flip_pairs(value):
        return join([value[1:2], value[:1], value[3:], value[2:3]])

    def attn_bwd(j, total):
        needs = attn_needs(heads[j]) + [need(kept[j][0]), need(kept[j][2]), need(kept[j][1])]
        res = call(
            functools.partial(attn_bwd_kernel, heads[j][0]),
            needs, [((width, 4 * LANE), BF), ((2, half, 4 * LANE), BF), hot(wide, F32)],
            scal, [seg_col, seg, d_att, d_att_t, tok_t, total], f"attn_bwd{j}", 1,
        )
        attn_g[j] = res[:2]
        if fast and j % 2:
            from_core[j - 1] = [over_core(g) for g in res[:2]]
        return res[2]

    total = d_pre_one
    if fast:
        def far_and_near(j, u, index, *where):
            return ffn_g[j, u][index][where], from_core[j, u][index][where]

        for u in range(2):
            down_y[u] = over_y(add(*far_and_near(2, u, 0)))
        first_x = over_x(
            join([add(*far_and_near(2, 0, 1, 1)), add(*far_and_near(0, 0, 1, 1))])
        )
        far_x1 = over_x(add(*far_and_near(2, 1, 1, 1)))
        near_x1 = over_x(add(*far_and_near(0, 1, 1, 1)))

        total, down_y[0], first_x = sync([total], [down_y[0], first_x])

        def down_sum(u, *where):
            return add(*far_and_near(0, u, 0, *where), down_y[u][where])

        rest, front = slice(half, None), slice(0, half)
        down_z = {0: over_z(down_sum(0, slice(None), rest))}
        far = [add(*far_and_near(2, 0, 1, 0), flip(first_x[:2]))]
        near = [add(*far_and_near(0, 0, 1, 0), flip(first_x[2:]))]
        total = attn_bwd(3, total)

        total, down_y[1], far_x1 = sync([total], [down_y[1], far_x1])
        down_z[1] = over_z(down_sum(1, slice(None), rest))
        far = join(far + [add(*far_and_near(2, 1, 1, 0), flip(far_x1))])
        far_z = over_z(far[:, quarter:])
        total = attn_bwd(2, total)

        total, near_x1, down_z[0] = sync([total], [near_x1, down_z[0]])
        near = join(near + [add(*far_and_near(0, 1, 1, 0), flip(near_x1))])
        near_z = over_z(near[:, quarter:])
        qk_y = over_y(add(attn_g[2][0], from_core[2][0]))
        vo_x = over_x(add(attn_g[2][1][1], from_core[2][1][1]))
        total = attn_bwd(1, total)

        total, down_z[1], far_z = sync([total], [down_z[1], far_z])
        down = join([add(down_sum(u, slice(None), front), down_z[1 - u]) for u in range(2)])
        down_x = over_x(down[:, quarter:])
        up_y = over_y(add(far[:, :quarter], turn_halves(far_z)))
        total = attn_bwd(0, total)
        token_grad = total

        def last_step(value):
            return value[..., :eighth, :], swap(value[..., eighth:, :], "seq", 4)

        def last_sum(kept_part, got):
            return kept_part.astype(F32) + got.astype(F32)

        vo_near_x = over_x(add(attn_g[0][1][1], from_core[0][1][1]))
        norm_grads = norm_grads + over_core(norm_grads)
        norm_y = over_y(norm_grads)
        (vo_x,) = tie([vo_x], total)
        vo_far = add(attn_g[2][1][0], from_core[2][1][0], vo_x)
        vo_z = over_z(vo_far[quarter:])
        (down_x,) = tie([down_x], vo_far)
        down = last_step(add(down[:, :quarter], flip_pairs(down_x)))
        (qk_y,) = tie([qk_y], down[0])
        qk = attn_g[0][0], from_core[0][0], qk_y
        qk_z = over_z(add(*[g[half:] for g in qk]))
        near_z, up_y = tie([near_z, up_y], qk_y)
        up = last_step(add(near[:, :quarter], turn_halves(near_z), up_y))
        vo_near_x, norm_y = tie([vo_near_x, norm_y], up[0])
        vo_near = add(attn_g[0][1][0], from_core[0][1][0], vo_near_x)
        vo_near_z = over_z(vo_near[quarter:])
        norm_grads = norm_grads + norm_y
        norm_x = over_x(norm_grads)
        (vo_z,) = tie([vo_z], vo_near)
        vo_y = over_y(add(vo_far[:quarter], vo_z))
        qk_z, norm_x = tie([qk_z, norm_x], vo_near)
        qk = add(*[g[:half] for g in qk], qk_z)
        qk_x = over_x(qk[quarter:])
        norm_grads = norm_grads + norm_x
        norm_z = over_z(norm_grads)
        vo_near_z, vo_y, norm_z = tie([vo_near_z, vo_y, norm_z], qk)
        vo = last_step(add(vo_near[:quarter], vo_near_z, vo_y))
        norm_grads = norm_grads + norm_z
        norm_grads = norm_grads + swap(norm_grads, "seq", 4)
        qk = last_step(add(qk[:quarter], qk_x))
        share = width // (seq * tp)
        norm_grads = lax.dynamic_slice_in_dim(
            norm_grads, (me_seq * tp + me_tp) * share, share, axis=1
        )

        def ordered(value):
            value = jnp.where(bit_x == 0, value, flip_pairs(value))
            value = jnp.where(bit_z == 0, value, turn_halves(value))
            return join([value[r] for r in range(4)], 1)

        down_grad = ordered(last_sum(*down)).T
        up_grad = ordered(last_sum(*up))
        qk, vo = last_sum(*qk), last_sum(*vo)
        qkv_grad = jnp.stack([qk[:, : 2 * LANE], qk[:, 2 * LANE :], vo[:, : 2 * LANE]])
        out_grad = vo[:, 2 * LANE :].T
    else:
        for j in order:
            total = attn_bwd(j, total)
        token_grad = total
        norm_grads = lax.psum_scatter(norm_grads, ("seq", "tp"), scatter_dimension=1, tiled=True)

        def scattered(value, tp_dim, seq_dim):
            value = lax.psum_scatter(value, "tp", scatter_dimension=tp_dim, tiled=True)
            value = lax.psum_scatter(value, "seq", scatter_dimension=seq_dim, tiled=True)
            return value.astype(F32)

        def rows_of(parts):
            return join([parts[i, ..., k * quarter : (k + 1) * quarter, :]
                         for k in range(2) for i in range(2)], -2)

        both = [(j, u) for j in range(pairs) for u in range(2)]
        down = join([ffn_g[k][0][i] for k in both for i in range(2)], 1)
        up = join([rows_of(ffn_g[k][1][:, i]) for k in both for i in range(2)], 1)
        qk = [attn_g[j][0] for j in range(pairs)]
        vo = [rows_of(attn_g[j][1]) for j in range(pairs)]
        down_grad = scattered(down, 1, 0).T
        up_grad = scattered(up, 1, 0)
        qkv_grad = jnp.stack(
            [
                join([g[:, : 2 * LANE] for g in qk], 1),
                join([g[:, 2 * LANE :] for g in qk], 1),
                join([g[:, : 2 * LANE] for g in vo], 1),
            ]
        )
        qkv_grad = scattered(qkv_grad, 2, 1)
        out_grad = scattered(join([g[:, 2 * LANE :] for g in vo], 1), 1, 0).T
    return (mixed, token_grad, qkv_grad, out_grad, up_grad, down_grad, norm_grads)


def solution(mesh):
    return jax.shard_map(
        body,
        mesh=mesh,
        in_specs=(
            P(("seq", "tp"), None),
            P("seq", None),
            P(None, None, "tp"),
            P("tp", None),
            P(None, "tp"),
            P("tp", None),
            P(),
            P(),
            P(),
            P(),
            P(("seq", "tp"), None),
        ),
        out_specs=(
            P(("seq", "tp"), None),
            P(("seq", "tp"), None),
            P(None, "seq", "tp"),
            P("tp", "seq"),
            P("seq", "tp"),
            P("tp", "seq"),
            P(None, ("seq", "tp")),
        ),
        check_vma=False,
    )
```

```python
import functools

import jax
import jax.numpy as jnp
from jax import lax
from jax.experimental import pallas as pl
from jax.experimental.pallas import tpu as pltpu
from jax.sharding import PartitionSpec as P

HDIM = 64
LANE = 128
BF = jnp.bfloat16
F32 = jnp.float32
SCALE = HDIM ** (-0.5)
MASKED = -1000000000.0


def dot(left, right):
    return jnp.dot(left, right, preferred_element_type=F32)


def dot_nt(left, right):
    return lax.dot_general(left, right, (((1,), (1,)), ((), ())), preferred_element_type=F32)


def everything(ref, scal):
    return ref


class Need:
    def __init__(self, shape, dtype, *parts, pinned=True):
        self.shape, self.dtype, self.parts, self.pinned = tuple(shape), dtype, parts, pinned


def need(array, pinned=True):
    return Need(array.shape, array.dtype, (array, everything, everything), pinned=pinned)


class Loads:
    def __init__(self, needs, refs, bufs, sems, scal):
        self.bufs, self.copies, self.next = bufs, [], 0
        at = 0
        for item, buf in zip(needs, bufs):
            mine = []
            for index, source, target in item.parts:
                copy = pltpu.make_async_copy(
                    source(refs[index], scal), target(buf, scal), sems.at[at]
                )
                copy.start()
                mine.append(copy)
                at += 1
            self.copies.append(mine)

    def take(self):
        self.next += 1
        return self.next - 1

    def get(self, slot):
        for copy in self.copies[slot]:
            copy.wait()
        self.copies[slot] = []
        return self.bufs[slot]

    def pop(self):
        return self.get(self.take())

    def finish(self):
        for slot in range(len(self.copies)):
            self.get(slot)


class Stores:
    def __init__(self, refs, bufs, sems):
        self.refs, self.sems, self.copies = refs, sems, []
        self.bufs = [ref if buf is None else buf for ref, buf in zip(refs, bufs)]
        self.direct = [buf is None for buf in bufs]
        self.next = 0

    def part(self, slot, value, *where):
        self.bufs[slot][where] = value

    def send(self, slot, *where):
        if self.direct[slot]:
            return
        source, target = self.bufs[slot], self.refs[slot]
        if where:
            source, target = source.at[where], target.at[where]
        copy = pltpu.make_async_copy(source, target, self.sems.at[self.next])
        self.next += 1
        copy.start()
        self.copies.append(copy)

    def put(self, slot, value):
        self.bufs[slot][...] = value
        self.send(slot)

    def finish(self):
        for copy in self.copies:
            copy.wait()


def hot(shape, dtype):
    return (shape, dtype, True)


def call(kernel, needs, outs, scal, small, name, flops, sends=None):
    arrays, parts, pinned = [], [], []
    for item in needs:
        fixed = []
        for array, source, target in item.parts:
            index = next((i for i, a in enumerate(arrays) if a is array), None)
            if index is None:
                index = len(arrays)
                arrays.append(array)
                pinned.append(item.pinned)
            fixed.append((index, source, target))
        parts.append(Need(item.shape, item.dtype, *fixed))
    copies = max(1, sum(len(item.parts) for item in parts))
    sends = max(1, len(outs) if sends is None else sends)
    here = [len(out) == 3 for out in outs]

    def run(*refs):
        refs = list(refs)
        scal_ref = refs.pop(0)
        small_refs = [refs.pop(0) for _ in small]
        in_refs = [refs.pop(0) for _ in arrays]
        out_refs = [refs.pop(0) for _ in outs]
        in_bufs = [refs.pop(0) for _ in parts]
        out_bufs = [None if stays else refs.pop(0) for stays in here]
        in_sems, out_sems = refs
        loads = Loads(parts, in_refs, in_bufs, in_sems, scal_ref)
        stores = Stores(out_refs, out_bufs, out_sems)
        kernel(scal_ref, small_refs, loads, stores)
        loads.finish()
        stores.finish()

    return pl.pallas_call(
        run,
        out_shape=[
            jax.ShapeDtypeStruct(out[0], out[1]) if stays else pltpu.HBM(out[0], out[1])
            for out, stays in zip(outs, here)
        ],
        in_specs=[pl.BlockSpec(memory_space=pltpu.SMEM)]
        + [pl.BlockSpec(memory_space=pltpu.VMEM)] * len(small)
        + [pl.BlockSpec(memory_space=pltpu.HBM if p else pl.ANY) for p in pinned],
        out_specs=[
            pl.BlockSpec(memory_space=pltpu.VMEM if stays else pltpu.HBM) for stays in here
        ],
        scratch_shapes=[pltpu.VMEM(item.shape, item.dtype) for item in parts]
        + [pltpu.VMEM(out[0], out[1]) for out, stays in zip(outs, here) if not stays]
        + [pltpu.SemaphoreType.DMA((copies,)), pltpu.SemaphoreType.DMA((sends,))],
        compiler_params=pltpu.CompilerParams(vmem_limit_bytes=32 * 1024 * 1024),
        cost_estimate=pl.CostEstimate(flops=flops, bytes_accessed=0, transcendentals=0),
        name=name,
    )(
        scal,
        *small,
        *[
            pltpu.with_memory_space_constraint(a, pltpu.HBM) if p else a
            for a, p in zip(arrays, pinned)
        ],
    )


def store_turned(scal, buf, values):
    for block in range(values.shape[1] // LANE):
        start = pl.multiple_of(scal[block] * LANE, LANE)
        buf[pl.ds(start, LANE), :] = values[:, block * LANE : (block + 1) * LANE].T


def block_of(scal, place):
    kind, value = place
    return scal[value] if kind == "table" else value


def columns(place, size, *front):
    def take(ref, scal):
        start = pl.multiple_of(block_of(scal, place) * size, size)
        return ref.at[(*front, slice(None), pl.ds(start, size))]

    return take


def lines(place, size):
    def take(ref, scal):
        start = pl.multiple_of(block_of(scal, place) * size, size)
        return ref.at[pl.ds(start, size), :]

    return take


def lanes_at(start, size):
    return lambda ref, scal: ref.at[:, pl.ds(start, size)]


def lines_at(start, size):
    return lambda ref, scal: ref.at[pl.ds(start, size), :]


def slot_at(*where):
    return lambda ref, scal: ref.at[where]


def stacked_at(index, size):
    def take(ref, scal):
        ref = ref if len(ref.shape) == 2 else ref.at[1]
        return ref.at[pl.ds(index * size, size), :]

    return take


def block_at(row, column, size):
    return lambda ref, scal: ref.at[pl.ds(row * size, size), pl.ds(column * size, size)]


def first_of(ref, scal):
    return ref if len(ref.shape) == 2 else ref.at[0]


def part_of(place):
    def find(scal):
        quarter = block_of(scal, place)
        return quarter // 2, lax.rem(quarter, 2)

    return find


def matrix_at(place, which):
    def take(ref, scal):
        half, pair = part_of(place)(scal)
        index = 1 if which else 2 * pair
        return ref.at[index, :, pl.ds(pl.multiple_of(half * LANE, LANE), LANE)]

    return take


def out_rows_at(place):
    def take(ref, scal):
        half, _ = part_of(place)(scal)
        return ref.at[pl.ds(pl.multiple_of(half * LANE, LANE), LANE), :]

    return take


def piece_lanes(place, which):
    def take(buf, scal):
        half, pair = part_of(place)(scal)
        start = pair * 4 * LANE + half * LANE + which * 2 * LANE
        return buf.at[:, pl.ds(pl.multiple_of(start, LANE), LANE)]

    return take


def attn_needs(block, pinned=True):
    if block[0] == "packed":
        pieces = block[1]
        parts = [
            (piece, lanes_at(which * LANE, LANE), piece_lanes(("table", 8 + r), which))
            for r, piece in enumerate(pieces)
            for which in range(2)
        ]
        return [Need((pieces[0].shape[0], 8 * LANE), BF, *parts, pinned=pinned)]
    _, qkv, out, index = block
    depth, width = qkv.shape[1], out.shape[1]
    place = ("block", index)
    return [
        Need(
            (depth, 6 * LANE), BF,
            *[
                (qkv, columns(place, 2 * LANE, i), lanes_at(2 * i * LANE, 2 * LANE))
                for i in range(3)
            ],
        ),
        Need((2 * LANE, width), BF, (out, lines(place, 2 * LANE), everything)),
    ]


def up_need(pieces, size, pinned=True):
    parts = []
    for number, piece in enumerate(pieces):
        target = lanes_at(number * size, size)
        if piece[0] == "packed":
            parts.append((piece[1], first_of, target))
        else:
            parts.append((piece[1], columns(piece[3], size), target))
    return Need((pieces[0][-1], len(pieces) * size), BF, *parts, pinned=pinned)


def down_need(pieces, size, pinned=True):
    parts = []
    for number, piece in enumerate(pieces):
        width = piece[-1]
        if piece[0] == "packed":
            for index in range(width // size):
                parts.append(
                    (piece[2], stacked_at(index, size), block_at(number, index, size))
                )
        else:
            parts.append((piece[2], lines(piece[3], size), lines_at(number * size, size)))
    return Need((len(pieces) * size, pieces[0][-1]), BF, *parts, pinned=pinned)


def saved_need(pieces, size):
    parts = [
        (array, lanes_at(index * size, size), lanes_at(number * size, size))
        for number, (array, index) in enumerate(pieces)
    ]
    return Need((pieces[0][0].shape[0], len(pieces) * size), BF, *parts)


def mean_of(values):
    return jnp.mean(values, axis=-1, keepdims=True)


def bias_of(seg_col, seg_row):
    return jnp.where(seg_col == seg_row, 0.0, MASKED)


def cut_kernel(places, scal, small, loads, stores):
    for slot, place in enumerate(places):
        first, second, out = loads.pop(), loads.pop(), loads.pop()
        _, pair = part_of(place)(scal)
        stores.part(slot, first[...], slice(None), slice(0, LANE))

        @pl.when(pair == 0)
        def _():
            stores.part(slot, second[...], slice(None), slice(LANE, 2 * LANE))

        @pl.when(pair == 1)
        def _():
            stores.part(slot, out[...].T, slice(None), slice(LANE, 2 * LANE))

        stores.send(slot)


def pack_kernel(size, scal, small, loads, stores):
    for slot in range(2):
        up, down = loads.pop(), loads.pop()
        stores.part(slot, up[...], 0)
        for index in range(down.shape[1] // size):
            block = down[:, index * size : (index + 1) * size]
            stores.part(slot, block, 1, pl.ds(index * size, size))
        stores.send(slot)


def turn_kernel(scal, small, loads, stores):
    store_turned(scal, stores.bufs[0], small[0][...])
    stores.send(0)


def head_parts(qkv, unit):
    query, key, value = (
        qkv[:, (2 * i + unit) * LANE : (2 * i + unit + 1) * LANE] for i in range(3)
    )
    return query * jnp.asarray(SCALE, BF), key, value


def attn_fwd_kernel(kind, first, last, scal, small, loads, stores):
    col_ref, row_ref, tokens_ref = small[:3]
    tokens = tokens_ref[...]
    bias = bias_of(col_ref[...], row_ref[...])
    lane = lax.broadcasted_iota(jnp.int32, (1, LANE), 1)
    line = lax.broadcasted_iota(jnp.int32, (LANE, 1), 0)
    weight = loads.pop()
    qkv = dot(tokens, weight[:, : 6 * LANE]).astype(BF)
    stores.put(0, qkv)
    contexts = []
    for unit in range(2):
        query, key, value = head_parts(qkv, unit)
        value_t = value.T
        parts = []
        for head in range(2):
            mine = lane >= HDIM if head else lane < HDIM
            scores = dot_nt(jnp.where(mine, key, jnp.zeros_like(key)), query) + bias
            peak = jnp.max(scores, axis=0, keepdims=True)
            raw = jnp.exp(scores - peak)
            summed = jnp.sum(raw, axis=0, keepdims=True)
            stores.part(2, peak + jnp.log(summed), pl.ds(2 * unit + head, 1), slice(None))
            prob = (raw * (1.0 / summed)).astype(BF)
            parts.append(dot(value_t, prob))
        contexts.append(jnp.where(line < HDIM, parts[0], parts[1]).astype(BF).T)
    stores.send(2)
    both = jnp.concatenate(contexts, axis=1)
    stores.put(1, both)
    if kind == "whole":
        total = dot(both, loads.pop()[...])
    else:
        total = dot_nt(both, weight[:, 6 * LANE :])
    if not first:
        total = total + small[3][...]
    at = 3
    if not last:
        stores.put(at, total)
        return
    gain_ref, shift_ref = small[-2:]
    pre = tokens.astype(F32) + total
    center = pre - mean_of(pre)
    inv = lax.rsqrt(mean_of(center * center) + 1e-12)
    hat = center * inv
    low = (hat * gain_ref[...] + shift_ref[...]).astype(BF)
    stores.put(at + 2, low)
    stores.put(at, hat)
    stores.put(at + 1, jnp.broadcast_to(inv, (hat.shape[0], LANE)))
    store_turned(scal, stores.bufs[at + 3], low)
    stores.send(at + 3)


def ffn_fwd_kernel(units, first, last, scal, small, loads, stores):
    low = small[0][...]
    total = None
    for number in range(units):
        up = dot(low, loads.pop()[...])
        phi_big = 0.5 + 0.5 * lax.erf(up * (0.5 ** 0.5))
        phi_small = jnp.exp(up * up * -0.5) * 0.3989422804014327
        act = (up * phi_big).astype(BF)
        stores.put(number * 2, act)
        stores.put(number * 2 + 1, (phi_big + up * phi_small).astype(BF))
        part = dot(act, loads.pop()[...])
        total = part if total is None else total + part
    if not first:
        total = total + small[1][...]
    at = units * 2
    if not last:
        stores.put(at, total)
        return
    hat_ref, gain1_ref, shift1_ref, gain2_ref, shift2_ref = small[-5:]
    gain2 = gain2_ref[...]
    pre = hat_ref[...] * gain1_ref[...] + shift1_ref[...] + total
    center = pre - mean_of(pre)
    inv = lax.rsqrt(mean_of(center * center) + 1e-12)
    hat = center * inv
    cot = loads.pop()[...].astype(F32)
    scaled = cot * gain2
    dpre = (scaled - mean_of(scaled) - hat * mean_of(scaled * hat)) * inv
    dffn = dpre.astype(BF)
    stores.put(at + 2, dffn)
    stores.put(at + 1, dpre)
    store_turned(scal, stores.bufs[at + 3], dffn)
    stores.send(at + 3)
    stores.put(at, (hat * gain2 + shift2_ref[...]).astype(BF))
    stores.put(at + 4, jnp.sum(cot * hat, axis=0, keepdims=True))
    stores.put(at + 5, jnp.sum(cot, axis=0, keepdims=True))


def split_rows(stores, slot, where, value):
    step = value.shape[0] // 4
    for number in range(4):
        rows = pl.ds(number // 2 * step, step)
        piece = value[number * step : (number + 1) * step]
        stores.part(slot + number % 2, piece, *where, rows)


def ffn_bwd_kernel(near, has_recv, last, size, scal, small, loads, stores):
    dffn_ref, dffn_t_ref, low_t_ref, acc_ref = small[:4]
    wd, slope = loads.pop(), loads.pop()
    d_up = (dot_nt(dffn_ref[...], wd[...]) * slope[...].astype(F32)).astype(BF)
    down = dot(dffn_t_ref[...], loads.pop()[...])
    got = loads.pop() if has_recv else None
    for index in range(2):
        value = down[:, index * size : (index + 1) * size]
        if has_recv:
            value = value + got[0, index].astype(F32)
        stores.part(0, value.astype(BF), *((index,) if near else (0, index)))
    if near:
        stores.send(0)
    up = dot(low_t_ref[...], d_up)
    for index in range(2):
        value = up[:, index * size : (index + 1) * size]
        if has_recv:
            value = value + got[1, index].astype(F32)
        if near:
            split_rows(stores, 1, (index,), value.astype(BF))
        else:
            stores.part(0, value.astype(BF), 1, index)
    if near:
        stores.send(1)
        stores.send(2)
    else:
        stores.send(0)
    total = acc_ref[...] + dot_nt(d_up, loads.pop()[...])
    at = 3 if near else 1
    if not last:
        stores.put(at, total)
        return
    hat_ref, inv_ref, gain_ref = small[4:]
    hat = hat_ref[...]
    scaled = total * gain_ref[...]
    inv = inv_ref[:, :1]
    dpre = (scaled - mean_of(scaled) - hat * mean_of(scaled * hat)) * inv
    datt = dpre.astype(BF)
    stores.put(at + 1, datt)
    stores.put(at, dpre)
    store_turned(scal, stores.bufs[at + 2], datt)
    stores.send(at + 2)
    stores.put(at + 3, jnp.sum(total * hat, axis=0, keepdims=True))
    stores.put(at + 4, jnp.sum(total, axis=0, keepdims=True))


def attn_bwd_kernel(kind, near, has_recv, scal, small, loads, stores):
    col_ref, row_ref, datt_ref, datt_t_ref, tok_t_ref, acc_ref = small
    bias = bias_of(col_ref[...], row_ref[...])
    lane = lax.broadcasted_iota(jnp.int32, (1, LANE), 1)
    line = lax.broadcasted_iota(jnp.int32, (LANE, 1), 0)
    weight = loads.pop()
    if kind == "whole":
        dctx_all = dot_nt(datt_ref[...], loads.pop()[...]).astype(BF)
    else:
        dctx_all = dot(datt_ref[...], weight[:, 6 * LANE :]).astype(BF)
    qkv, lse = loads.pop(), loads.pop()
    grads = [[], [], []]
    for unit in range(2):
        dctx = dctx_all[:, unit * LANE : (unit + 1) * LANE]
        query, key, value = head_parts(qkv, unit)
        key_t = key.T
        parts = []
        for head in range(2):
            mine = lane >= HDIM if head else lane < HDIM
            scores = dot_nt(jnp.where(mine, key, jnp.zeros_like(key)), query) + bias
            row = 2 * unit + head
            prob = jnp.exp(scores - lse[row : row + 1, :])
            d_prob = dot_nt(jnp.where(mine, value, jnp.zeros_like(value)), dctx)
            inner = jnp.sum(prob * d_prob, axis=0, keepdims=True)
            d_scores = (prob * (d_prob - inner)).astype(BF)
            parts.append(
                (dot(key_t, d_scores), dot(d_scores, query), dot(prob.astype(BF), dctx))
            )
        d_query = (jnp.where(line < HDIM, parts[0][0], parts[1][0]) * SCALE).astype(BF).T
        grads[0].append(d_query)
        grads[1].append(jnp.where(lane < HDIM, parts[0][1], parts[1][1]).astype(BF))
        grads[2].append(jnp.where(lane < HDIM, parts[0][2], parts[1][2]).astype(BF))
    tok_t = tok_t_ref[...]
    both = jnp.concatenate(grads[0] + grads[1] + grads[2], axis=1)
    ctx = loads.pop()
    got = loads.pop() if has_recv else None
    qk = dot(tok_t, both[:, : 4 * LANE])
    if has_recv:
        qk = qk + got[:, : 4 * LANE].astype(F32)
    vo = jnp.concatenate(
        [dot(tok_t, both[:, 4 * LANE :]), dot(datt_t_ref[...], ctx[...])], axis=1
    )
    if has_recv:
        vo = vo + got[:, 4 * LANE :].astype(F32)
    if near:
        stores.put(0, qk.astype(BF))
        split_rows(stores, 1, (), vo.astype(BF))
        stores.send(1)
        stores.send(2)
    else:
        stores.part(0, qk.astype(BF), slice(None), slice(0, 4 * LANE))
        stores.part(0, vo.astype(BF), slice(None), slice(4 * LANE, 8 * LANE))
        stores.send(0)
    stores.put(3 if near else 1, acc_ref[...] + dot_nt(both, weight[:, : 6 * LANE]))


def swap(value, axis, bit):
    count = lax.axis_size(axis)
    return lax.ppermute(value, axis, [(i, i ^ bit) for i in range(count)])


def add(*values):
    total = values[0].astype(F32)
    for value in values[1:]:
        total = total + value.astype(F32)
    return total.astype(BF)


def tie(values, *after):
    return list(lax.optimization_barrier((tuple(values), after))[0])


def sync(values, arrived):
    return lax.optimization_barrier((*values, *arrived))


def join(values, axis=0):
    return jnp.concatenate(values, axis=axis)


def body(
    tokens,
    segment_ids,
    qkv_weight,
    out_weight,
    up_weight,
    down_weight,
    gain_attn,
    shift_attn,
    gain_ffn,
    shift_ffn,
    cotangent,
):
    count, width = tokens.shape
    seq, tp = lax.axis_size("seq"), lax.axis_size("tp")
    me_seq, me_tp = lax.axis_index("seq"), lax.axis_index("tp")
    blocks = width // LANE
    pairs = blocks // 2
    size = up_weight.shape[1] * tp // (4 * pairs)
    fast = seq == blocks and seq == 8 and tp == 4 and qkv_weight.shape[2] == 2 * LANE
    seg = lax.dynamic_slice_in_dim(segment_ids, me_tp, 1, axis=0)
    seg_col = seg.reshape(count, 1)
    gains = [g.reshape(1, width) for g in (gain_attn, shift_attn, gain_ffn, shift_ffn)]
    absolute = jnp.arange(blocks, dtype=jnp.int32)
    half, quarter, eighth = width // 2, width // 4, width // 8
    wide = (count, width)
    work = 2 * count * width
    bit_x, bit_z = me_seq & 1, (me_seq >> 1) & 1

    def over_x(value):
        return swap(value, "seq", 1)

    def over_z(value):
        return swap(value, "seq", 2)

    def over_y(value):
        return swap(value, "tp", 2)

    def over_core(value):
        return swap(value, "tp", 1)

    if fast:
        rel = absolute ^ me_seq
        pos = ((rel >> 1) & 1) * 4 + (rel & 1) * 2 + (rel >> 2)
        mine = me_seq & 3
        scal = jnp.stack(
            [pos[i] for i in range(blocks)] + [mine ^ r for r in range(4)]
        ).astype(jnp.int32)
        table = [("table", 8 + r) for r in range(4)]
        needs = []
        for r in (0, 3):
            shape = (width, LANE)
            needs += [
                Need(shape, BF, (qkv_weight, matrix_at(table[r], which), everything))
                for which in range(2)
            ]
            needs.append(
                Need((LANE, width), BF, (out_weight, out_rows_at(table[r]), everything))
            )
        cuts = call(
            functools.partial(cut_kernel, [table[0], table[3]]), needs,
            [((width, 2 * LANE), BF)] * 2, scal, [], "cut", 1,
        )
        head_a, head_d = over_y(cuts[0]), over_y(cuts[1])
        needs = []
        for r in (0, 3):
            own = [("whole", up_weight, down_weight, table[r], width)]
            needs += [up_need(own, size), down_need(own, size)]
        packs = call(
            functools.partial(pack_kernel, size), needs,
            [((2, width, size), BF)] * 2, scal, [], "pack", 1,
        )
        ffn_a, ffn_d = over_y(packs[0]), over_y(packs[1])
        (tokens_late,) = tie([tokens], packs[1])
        near = [over_core(w) for w in (qkv_weight, out_weight)]
    else:
        scal = jnp.concatenate([absolute, jnp.zeros((4,), jnp.int32)])
        qkv_all = lax.all_gather(qkv_weight, "tp", axis=2, tiled=True)
        out_all = lax.all_gather(out_weight, "tp", axis=0, tiled=True)
        up_all = lax.all_gather(up_weight, "tp", axis=1, tiled=True)
        down_all = lax.all_gather(down_weight, "tp", axis=0, tiled=True)

    kept, acts = {}, {}
    early = tokens_late if fast else tokens

    def attn_fwd(j, total, last):
        needs = attn_needs(heads[j], False)
        outs = [((count, 6 * LANE), BF), ((count, 2 * LANE), BF), ((8, count), F32)]
        if last:
            outs += [
                hot(wide, F32), hot((count, LANE), F32), hot(wide, BF), hot((width, count), BF),
            ]
        else:
            outs.append(hot(wide, F32))
        first = total is None
        small = [seg_col, seg, early] + ([] if first else [total]) + (gains[:2] if last else [])
        res = call(
            functools.partial(attn_fwd_kernel, heads[j][0], first, last),
            needs, outs, scal, small, f"attn_fwd{j}", 1,
        )
        kept[j] = res[:3]
        return res[3:]

    def ffn_fwd(number, group, total, last):
        needs, outs = [], []
        for unit in group:
            pieces = [hidden[piece] for piece in unit]
            needs += [up_need(pieces, size, False), down_need(pieces, size, False)]
            outs += [((count, len(unit) * size), BF)] * 2
        first = total is None
        small = [low] + ([] if first else [total])
        if last:
            needs.append(need(cotangent))
            small += [hat, *gains]
            outs += [
                (wide, BF), hot(wide, F32), hot(wide, BF), hot((width, count), BF),
                hot((1, width), F32), hot((1, width), F32),
            ]
        else:
            outs.append(hot(wide, F32))
        res = call(
            functools.partial(ffn_fwd_kernel, len(group), first, last),
            needs, outs, scal, small, f"ffn_fwd{number}", 8 * work * size * len(group),
        )
        for index, unit in enumerate(group):
            for place, piece in enumerate(unit):
                acts[piece] = [(array, place) for array in res[index * 2 : index * 2 + 2]]
        return res[len(group) * 2 :]

    if fast:
        heads, hidden = {}, {}
        heads[0] = ("whole", qkv_weight, out_weight, 0)
        heads[1] = ("whole", *near[:2], 0)
        for r in range(4):
            hidden[0, r] = ("whole", up_weight, down_weight, table[r], width)

        def packed(r, both):
            hidden[2, r] = ("packed", both, both, width)
            other = over_core(both)
            hidden[3, r] = ("packed", other, other, width)

        (total,) = attn_fwd(0, None, False)
        (head_a,) = tie([head_a], total, *near)
        head_b, head_c = over_x(head_a), over_z(head_a)
        other_a = over_core(head_a)
        (total,) = attn_fwd(1, total, False)
        tok_t = call(
            turn_kernel, [], [hot((width, count), BF)], scal, tie([tokens], total), "turn", 1
        )[0]
        head_b, head_c, head_d = tie([head_b, head_c, head_d], tok_t)
        pieces = [head_a, head_b, head_c, head_d]
        heads[2] = ("packed", pieces)
        heads[3] = ("packed", [other_a] + [over_core(p) for p in pieces[1:]])
        (total,) = attn_fwd(2, total, False)
        late = [over_core(w) for w in tie([up_weight, down_weight], *heads[3][1])]
        for r in range(4):
            hidden[1, r] = ("whole", *late, table[r], width)
        hat, inv, low, low_t = attn_fwd(3, total, True)
        (ffn_a,) = tie([ffn_a], low)
        ffn_b, ffn_c = over_x(ffn_a), over_z(ffn_a)
        packed(0, ffn_a)
        (total,) = ffn_fwd(0, [[(0, 0), (0, 1)], [(0, 2), (0, 3)]], None, False)
        (total,) = ffn_fwd(1, [[(1, 0), (1, 1)], [(1, 2), (1, 3)]], total, False)
        for r, both in zip((1, 2, 3), tie([ffn_b, ffn_c, ffn_d], total)):
            packed(r, both)
        (total,) = ffn_fwd(2, [[(2, 0), (3, 0)]], total, False)
        (total,) = ffn_fwd(3, [[(2, 1), (2, 2)], [(3, 1), (3, 2)]], total, False)
        res = ffn_fwd(4, [[(2, 3), (3, 3)]], total, True)
    else:
        heads = {j: ("whole", qkv_all, out_all, j) for j in range(pairs)}
        hidden = {
            (k // 4, k % 4): ("whole", up_all, down_all, ("block", k), width)
            for k in range(4 * pairs)
        }
        tok_t = call(
            turn_kernel, [], [hot((width, count), BF)], scal, [tokens], "turn", 1
        )[0]
        total = None
        for j in range(pairs):
            res = attn_fwd(j, total, j == pairs - 1)
            total = res[0]
        hat, inv, low, low_t = res
        total = None
        for j in range(pairs):
            res = ffn_fwd(j, [[(j, 0), (j, 1)], [(j, 2), (j, 3)]], total, j == pairs - 1)
            total = res[0]
    mixed, d_pre, d_ffn, d_ffn_t, g_gain2, g_shift2 = res

    order = [3, 1, 2, 0] if fast else list(range(pairs))
    units = [(j, u) for j in order for u in range(2)]
    ffn_g, attn_g, from_core = {}, {}, {}
    down_y, far_x = {}, {}
    total = d_pre
    for j, u in units:
        last = (j, u) == units[-1]
        here = not fast or j % 2 == 0
        recv = from_core.get((j, u))
        pieces = [hidden[j, 2 * u + i] for i in range(2)]
        saved = [acts[j, 2 * u + i] for i in range(2)]
        needs = [
            down_need(pieces, size),
            saved_need([s[1] for s in saved], size),
            saved_need([s[0] for s in saved], size),
        ]
        if recv is not None:
            needs.append(need(recv, False))
        needs.append(up_need(pieces, size))
        small = [d_ffn, d_ffn_t, low_t, total]
        if here:
            outs = [((2, width, size), BF), ((2, half, size), BF), ((2, half, size), BF)]
        else:
            outs = [((2, 2, width, size), BF)]
        grads = len(outs)
        if last:
            small += [hat, inv, gains[0]]
            outs = outs + [
                hot(wide, F32), hot(wide, BF), hot((width, count), BF),
                hot((1, width), F32), hot((1, width), F32),
            ]
        else:
            outs = outs + [hot(wide, F32)]
        res = call(
            functools.partial(ffn_bwd_kernel, here, recv is not None, last, size),
            needs, outs, scal, small, f"ffn_bwd{j}{u}", 1,
        )
        ffn_g[j, u], total = res[:grads], res[grads]
        if not here:
            from_core[j - 1, u] = over_core(res[0])
        if fast and j == 2:
            down_y[u], far_x[u] = over_y(res[0]), over_x(res[2])
    d_pre_one, d_att, d_att_t, g_gain1, g_shift1 = res[grads:]

    norm_grads = join([g_gain1, g_shift1, g_gain2, g_shift2])

    def flip(value):
        return join([value[1:], value[:1]])

    def turn_halves(value):
        return join([value[2:], value[:2]])

    def flip_pairs(value):
        return join([value[1:2], value[:1], value[3:], value[2:3]])

    def attn_bwd(j, total):
        here = not fast or j % 2 == 0
        recv = from_core.get(j)
        needs = attn_needs(heads[j]) + [need(kept[j][0]), need(kept[j][2]), need(kept[j][1])]
        if recv is not None:
            needs.append(need(recv, False))
        columns_each = 4 * LANE
        if here:
            outs = [((width, columns_each), BF)] + [((half, columns_each), BF)] * 2
        else:
            outs = [((width, 2 * columns_each), BF)]
        res = call(
            functools.partial(attn_bwd_kernel, heads[j][0], here, recv is not None),
            needs, outs + [hot(wide, F32)],
            scal, [seg_col, seg, d_att, d_att_t, tok_t, total], f"attn_bwd{j}", 1,
        )
        attn_g[j] = res[:-1]
        if not here:
            from_core[j - 1] = over_core(res[0])
        return res[-1]

    total = d_pre_one
    if fast:
        near_x = over_x(join([ffn_g[0, u][2] for u in range(2)]))
        rest, front = slice(half, None), slice(0, half)

        def down_sum(u, rows):
            return add(ffn_g[0, u][0][:, rows], down_y[u][:, rows])

        total, down_y[0], far_x[0] = sync([total], [down_y[0], far_x[0]])
        down_z = {0: over_z(down_sum(0, rest))}
        total = attn_bwd(3, total)

        total, far_x[1], down_z[0], norm_grads = sync(
            [total], [far_x[1], down_z[0], norm_grads]
        )
        norm_next = over_core(norm_grads)
        far = join([add(ffn_g[2, u][1], flip(far_x[u])) for u in range(2)])
        far_z = over_z(far[:, quarter:])
        total = attn_bwd(1, total)

        total, down_y[1], near_x, far_z, norm_next = sync(
            [total], [down_y[1], near_x, far_z, norm_next]
        )
        norm_grads = norm_grads + norm_next
        norm_next = over_y(norm_grads)
        up_y = over_y(add(far[:, :quarter], turn_halves(far_z)))
        down_z[1] = over_z(down_sum(1, rest))
        near = join([add(ffn_g[0, u][1], flip(near_x[2 * u : 2 * u + 2])) for u in range(2)])
        total = attn_bwd(2, total)

        total, down_z[1], up_y, norm_next = sync([total], [down_z[1], up_y, norm_next])
        norm_grads = norm_grads + norm_next
        (near,) = tie([near], total)
        near_z = over_z(near[:, quarter:])
        down = join([add(down_sum(u, front), down_z[1 - u]) for u in range(2)])
        down_x = over_x(down[:, quarter:])
        qk_y = over_y(attn_g[2][0])
        vo_x = over_x(attn_g[2][2])
        total = attn_bwd(0, total)
        token_grad = total

        def last_sum(value, got):
            return value[..., :eighth, :].astype(F32) + got.astype(F32)

        vo_near_x = over_x(attn_g[0][2])
        qk_near, qk_y = sync([attn_g[0][0]], [qk_y])
        qk_z = over_z(add(qk_near[half:], qk_y[half:]))
        qk_y, vo_x = sync([qk_y], [vo_x])
        vo_far = add(attn_g[2][1], vo_x)
        vo_z = over_z(vo_far[quarter:])
        vo_far, down_x, near_z = sync([vo_far], [down_x, near_z])
        down = add(down[:, :quarter], flip_pairs(down_x))
        up = add(near[:, :quarter], turn_halves(near_z), up_y)
        hidden_sum = join([down, up])
        hidden_got = swap(hidden_sum[:, eighth:], "seq", 4)
        hidden_sum, vo_near_x = sync([hidden_sum], [vo_near_x])
        vo_near = add(attn_g[0][1], vo_near_x)
        vo_near_z = over_z(vo_near[quarter:])
        vo_near, norm_grads = sync([vo_near], [norm_grads])
        norm_next = over_x(norm_grads)
        vo_near, vo_z = sync([vo_near], [vo_z])
        vo_y = over_y(add(vo_far[:quarter], vo_z))
        vo_near, qk_z, norm_next = sync([vo_near], [qk_z, norm_next])
        qk = add(qk_near[:half], qk_y[:half], qk_z)
        qk_x = over_x(qk[quarter:])
        norm_grads = norm_grads + norm_next
        norm_next = over_z(norm_grads)
        qk, vo_near_z, vo_y = sync([qk], [vo_near_z, vo_y])
        vo = add(vo_near[:quarter], vo_near_z, vo_y)
        vo_got = swap(vo[eighth:], "seq", 4)
        vo, qk_x, norm_next, hidden_got = sync([vo], [qk_x, norm_next, hidden_got])
        qk = add(qk[:quarter], qk_x)
        qk_got = swap(qk[eighth:], "seq", 4)
        norm_grads = norm_grads + norm_next
        norm_grads = norm_grads + swap(norm_grads, "seq", 4)
        hidden_sum = last_sum(hidden_sum, hidden_got)
        down, up = hidden_sum[:4], hidden_sum[4:]
        vo, qk = last_sum(vo, vo_got), last_sum(qk, qk_got)
        share = width // (seq * tp)
        norm_grads = lax.dynamic_slice_in_dim(
            norm_grads, (me_seq * tp + me_tp) * share, share, axis=1
        )

        def ordered(value):
            value = jnp.where(bit_x == 0, value, flip_pairs(value))
            value = jnp.where(bit_z == 0, value, turn_halves(value))
            return join([value[r] for r in range(4)], 1)

        down_grad = ordered(down).T
        up_grad = ordered(up)
        qkv_grad = jnp.stack([qk[:, : 2 * LANE], qk[:, 2 * LANE :], vo[:, : 2 * LANE]])
        out_grad = vo[:, 2 * LANE :].T
    else:
        for j in order:
            total = attn_bwd(j, total)
        token_grad = total
        norm_grads = lax.psum_scatter(norm_grads, ("seq", "tp"), scatter_dimension=1, tiled=True)

        def scattered(value, tp_dim, seq_dim):
            value = lax.psum_scatter(value, "tp", scatter_dimension=tp_dim, tiled=True)
            value = lax.psum_scatter(value, "seq", scatter_dimension=seq_dim, tiled=True)
            return value.astype(F32)

        def rows_of(low_part, high_part):
            parts = [
                part[..., k * quarter : (k + 1) * quarter, :]
                for k in range(2)
                for part in (low_part, high_part)
            ]
            return join(parts, -2)

        both = [(j, u) for j in range(pairs) for u in range(2)]
        down = join([ffn_g[k][0][i] for k in both for i in range(2)], 1)
        up = join([rows_of(ffn_g[k][1][i], ffn_g[k][2][i]) for k in both for i in range(2)], 1)
        qk = [attn_g[j][0] for j in range(pairs)]
        vo = [rows_of(attn_g[j][1], attn_g[j][2]) for j in range(pairs)]
        down_grad = scattered(down, 1, 0).T
        up_grad = scattered(up, 1, 0)
        qkv_grad = jnp.stack(
            [
                join([g[:, : 2 * LANE] for g in qk], 1),
                join([g[:, 2 * LANE :] for g in qk], 1),
                join([g[:, : 2 * LANE] for g in vo], 1),
            ]
        )
        qkv_grad = scattered(qkv_grad, 2, 1)
        out_grad = scattered(join([g[:, 2 * LANE :] for g in vo], 1), 1, 0).T
    return (mixed, token_grad, qkv_grad, out_grad, up_grad, down_grad, norm_grads)


def solution(mesh):
    return jax.shard_map(
        body,
        mesh=mesh,
        in_specs=(
            P(("seq", "tp"), None),
            P("seq", None),
            P(None, None, "tp"),
            P("tp", None),
            P(None, "tp"),
            P("tp", None),
            P(),
            P(),
            P(),
            P(),
            P(("seq", "tp"), None),
        ),
        out_specs=(
            P(("seq", "tp"), None),
            P(("seq", "tp"), None),
            P(None, "seq", "tp"),
            P("tp", "seq"),
            P("seq", "tp"),
            P("tp", "seq"),
            P(None, ("seq", "tp")),
        ),
        check_vma=False,
    )
```

```python
import functools

import jax
import jax.numpy as jnp
from jax import lax
from jax.experimental import pallas as pl
from jax.experimental.pallas import tpu as pltpu
from jax.sharding import PartitionSpec as P

HDIM = 64
LANE = 128
BF = jnp.bfloat16
F32 = jnp.float32
SCALE = HDIM ** (-0.5)
MASKED = -1000000000.0


def dot(left, right):
    return jnp.dot(left, right, preferred_element_type=F32)


def dot_nt(left, right):
    return lax.dot_general(left, right, (((1,), (1,)), ((), ())), preferred_element_type=F32)


def everything(ref, scal):
    return ref


class Need:
    def __init__(self, shape, dtype, *parts, pinned=True):
        self.shape, self.dtype, self.parts, self.pinned = tuple(shape), dtype, parts, pinned


def need(array, pinned=True):
    return Need(array.shape, array.dtype, (array, everything, everything), pinned=pinned)


class Loads:
    def __init__(self, needs, refs, bufs, sems, scal):
        self.bufs, self.copies, self.next = bufs, [], 0
        at = 0
        for item, buf in zip(needs, bufs):
            mine = []
            for index, source, target in item.parts:
                copy = pltpu.make_async_copy(
                    source(refs[index], scal), target(buf, scal), sems.at[at]
                )
                copy.start()
                mine.append(copy)
                at += 1
            self.copies.append(mine)

    def take(self):
        self.next += 1
        return self.next - 1

    def get(self, slot):
        for copy in self.copies[slot]:
            copy.wait()
        self.copies[slot] = []
        return self.bufs[slot]

    def pop(self):
        return self.get(self.take())

    def finish(self):
        for slot in range(len(self.copies)):
            self.get(slot)


class Stores:
    def __init__(self, refs, bufs, sems):
        self.refs, self.sems, self.copies = refs, sems, []
        self.bufs = [ref if buf is None else buf for ref, buf in zip(refs, bufs)]
        self.direct = [buf is None for buf in bufs]
        self.next = 0

    def part(self, slot, value, *where):
        self.bufs[slot][where] = value

    def send(self, slot, *where):
        if self.direct[slot]:
            return
        source, target = self.bufs[slot], self.refs[slot]
        if where:
            source, target = source.at[where], target.at[where]
        copy = pltpu.make_async_copy(source, target, self.sems.at[self.next])
        self.next += 1
        copy.start()
        self.copies.append(copy)

    def put(self, slot, value):
        self.bufs[slot][...] = value
        self.send(slot)

    def finish(self):
        for copy in self.copies:
            copy.wait()


def hot(shape, dtype):
    return (shape, dtype, True)


def call(kernel, needs, outs, scal, small, name, flops, sends=None):
    arrays, parts, pinned = [], [], []
    for item in needs:
        fixed = []
        for array, source, target in item.parts:
            index = next((i for i, a in enumerate(arrays) if a is array), None)
            if index is None:
                index = len(arrays)
                arrays.append(array)
                pinned.append(item.pinned)
            fixed.append((index, source, target))
        parts.append(Need(item.shape, item.dtype, *fixed))
    copies = max(1, sum(len(item.parts) for item in parts))
    sends = max(1, len(outs) if sends is None else sends)
    here = [len(out) == 3 for out in outs]

    def run(*refs):
        refs = list(refs)
        scal_ref = refs.pop(0)
        small_refs = [refs.pop(0) for _ in small]
        in_refs = [refs.pop(0) for _ in arrays]
        out_refs = [refs.pop(0) for _ in outs]
        in_bufs = [refs.pop(0) for _ in parts]
        out_bufs = [None if stays else refs.pop(0) for stays in here]
        in_sems, out_sems = refs
        loads = Loads(parts, in_refs, in_bufs, in_sems, scal_ref)
        stores = Stores(out_refs, out_bufs, out_sems)
        kernel(scal_ref, small_refs, loads, stores)
        loads.finish()
        stores.finish()

    return pl.pallas_call(
        run,
        out_shape=[
            jax.ShapeDtypeStruct(out[0], out[1]) if stays else pltpu.HBM(out[0], out[1])
            for out, stays in zip(outs, here)
        ],
        in_specs=[pl.BlockSpec(memory_space=pltpu.SMEM)]
        + [pl.BlockSpec(memory_space=pltpu.VMEM)] * len(small)
        + [pl.BlockSpec(memory_space=pltpu.HBM if p else pl.ANY) for p in pinned],
        out_specs=[
            pl.BlockSpec(memory_space=pltpu.VMEM if stays else pltpu.HBM) for stays in here
        ],
        scratch_shapes=[pltpu.VMEM(item.shape, item.dtype) for item in parts]
        + [pltpu.VMEM(out[0], out[1]) for out, stays in zip(outs, here) if not stays]
        + [pltpu.SemaphoreType.DMA((copies,)), pltpu.SemaphoreType.DMA((sends,))],
        compiler_params=pltpu.CompilerParams(vmem_limit_bytes=40 * 1024 * 1024),
        cost_estimate=pl.CostEstimate(flops=flops, bytes_accessed=0, transcendentals=0),
        name=name,
    )(
        scal,
        *small,
        *[
            pltpu.with_memory_space_constraint(a, pltpu.HBM) if p else a
            for a, p in zip(arrays, pinned)
        ],
    )


def store_turned(scal, buf, values):
    for block in range(values.shape[1] // LANE):
        start = pl.multiple_of(scal[block] * LANE, LANE)
        buf[pl.ds(start, LANE), :] = values[:, block * LANE : (block + 1) * LANE].T


def block_of(scal, place):
    kind, value = place
    return scal[value] if kind == "table" else value


def columns(place, size, *front):
    def take(ref, scal):
        start = pl.multiple_of(block_of(scal, place) * size, size)
        return ref.at[(*front, slice(None), pl.ds(start, size))]

    return take


def lines(place, size):
    def take(ref, scal):
        start = pl.multiple_of(block_of(scal, place) * size, size)
        return ref.at[pl.ds(start, size), :]

    return take


def lanes_at(start, size):
    return lambda ref, scal: ref.at[:, pl.ds(start, size)]


def lines_at(start, size):
    return lambda ref, scal: ref.at[pl.ds(start, size), :]


def slot_at(*where):
    return lambda ref, scal: ref.at[where]


def stacked_at(index, size):
    def take(ref, scal):
        ref = ref if len(ref.shape) == 2 else ref.at[1]
        return ref.at[pl.ds(index * size, size), :]

    return take


def block_at(row, column, size):
    return lambda ref, scal: ref.at[pl.ds(row * size, size), pl.ds(column * size, size)]


def first_of(ref, scal):
    return ref if len(ref.shape) == 2 else ref.at[0]


def part_of(place):
    def find(scal):
        quarter = block_of(scal, place)
        return quarter // 2, lax.rem(quarter, 2)

    return find


def matrix_at(place, which):
    def take(ref, scal):
        half, pair = part_of(place)(scal)
        index = 1 if which else 2 * pair
        return ref.at[index, :, pl.ds(pl.multiple_of(half * LANE, LANE), LANE)]

    return take


def out_rows_at(place):
    def take(ref, scal):
        half, _ = part_of(place)(scal)
        return ref.at[pl.ds(pl.multiple_of(half * LANE, LANE), LANE), :]

    return take


def piece_lanes(place, which):
    def take(buf, scal):
        half, pair = part_of(place)(scal)
        start = pair * 4 * LANE + half * LANE + which * 2 * LANE
        return buf.at[:, pl.ds(pl.multiple_of(start, LANE), LANE)]

    return take


def attn_needs(block, pinned=True):
    if block[0] == "packed":
        pieces = block[1]
        parts = [
            (piece, lanes_at(which * LANE, LANE), piece_lanes(("table", 8 + r), which))
            for r, piece in enumerate(pieces)
            for which in range(2)
        ]
        return [Need((pieces[0].shape[0], 8 * LANE), BF, *parts, pinned=pinned)]
    _, qkv, out, index = block
    depth, width = qkv.shape[1], out.shape[1]
    place = ("block", index)
    return [
        Need(
            (depth, 6 * LANE), BF,
            *[
                (qkv, columns(place, 2 * LANE, i), lanes_at(2 * i * LANE, 2 * LANE))
                for i in range(3)
            ],
        ),
        Need((2 * LANE, width), BF, (out, lines(place, 2 * LANE), everything)),
    ]


def up_need(pieces, size, pinned=True):
    parts = []
    for number, piece in enumerate(pieces):
        target = lanes_at(number * size, size)
        if piece[0] == "packed":
            parts.append((piece[1], first_of, target))
        else:
            parts.append((piece[1], columns(piece[3], size), target))
    return Need((pieces[0][-1], len(pieces) * size), BF, *parts, pinned=pinned)


def down_need(pieces, size, pinned=True):
    parts = []
    for number, piece in enumerate(pieces):
        width = piece[-1]
        if piece[0] == "packed":
            for index in range(width // size):
                parts.append(
                    (piece[2], stacked_at(index, size), block_at(number, index, size))
                )
        else:
            parts.append((piece[2], lines(piece[3], size), lines_at(number * size, size)))
    return Need((len(pieces) * size, pieces[0][-1]), BF, *parts, pinned=pinned)


def saved_need(pieces, size):
    parts = [
        (array, lanes_at(index * size, size), lanes_at(number * size, size))
        for number, (array, index) in enumerate(pieces)
    ]
    return Need((pieces[0][0].shape[0], len(pieces) * size), BF, *parts)


def mean_of(values):
    return jnp.mean(values, axis=-1, keepdims=True)


def bias_of(seg_col, seg_row):
    return jnp.where(seg_col == seg_row, 0.0, MASKED)


def cut_kernel(places, scal, small, loads, stores):
    for slot, place in enumerate(places):
        first, second, out = loads.pop(), loads.pop(), loads.pop()
        _, pair = part_of(place)(scal)
        stores.part(slot, first[...], slice(None), slice(0, LANE))

        @pl.when(pair == 0)
        def _():
            stores.part(slot, second[...], slice(None), slice(LANE, 2 * LANE))

        @pl.when(pair == 1)
        def _():
            stores.part(slot, out[...].T, slice(None), slice(LANE, 2 * LANE))

        stores.send(slot)


def pack_kernel(size, scal, small, loads, stores):
    for slot in range(2):
        up, down = loads.pop(), loads.pop()
        stores.part(slot, up[...], 0)
        for index in range(down.shape[1] // size):
            block = down[:, index * size : (index + 1) * size]
            stores.part(slot, block, 1, pl.ds(index * size, size))
        stores.send(slot)


def turn_kernel(scal, small, loads, stores):
    store_turned(scal, stores.bufs[0], small[0][...])
    stores.send(0)


def head_parts(qkv, unit):
    query, key, value = (
        qkv[:, (2 * i + unit) * LANE : (2 * i + unit + 1) * LANE] for i in range(3)
    )
    return query * jnp.asarray(SCALE, BF), key, value


def stacked(pair, lane):
    zero = jnp.zeros_like(pair)
    return jnp.concatenate(
        [jnp.where(lane < HDIM, pair, zero), jnp.where(lane >= HDIM, pair, zero)], axis=0
    )


def attn_fwd_kernel(kind, first, last, scal, small, loads, stores):
    col_ref, row_ref, tokens_ref = small[:3]
    tokens = tokens_ref[...]
    bias = bias_of(col_ref[...], row_ref[...])
    lane = lax.broadcasted_iota(jnp.int32, (1, LANE), 1)
    length = tokens.shape[0]
    weight = loads.pop()
    qkv = dot(tokens, weight[:, : 6 * LANE]).astype(BF)
    stores.put(0, qkv)
    contexts = []
    for unit in range(2):
        query, key, value = head_parts(qkv, unit)
        scores = dot_nt(stacked(key, lane), query)
        probs = []
        for head in range(2):
            mine = scores[head * length : (head + 1) * length] + bias
            peak = jnp.max(mine, axis=0, keepdims=True)
            raw = jnp.exp(mine - peak)
            summed = jnp.sum(raw, axis=0, keepdims=True)
            stores.part(2, peak + jnp.log(summed), pl.ds(2 * unit + head, 1), slice(None))
            probs.append((raw * (1.0 / summed)).astype(BF))
        context = dot(stacked(value, lane).T, jnp.concatenate(probs, axis=0))
        contexts.append(context.astype(BF).T)
    stores.send(2)
    both = jnp.concatenate(contexts, axis=1)
    stores.put(1, both)
    if kind == "whole":
        total = dot(both, loads.pop()[...])
    else:
        total = dot_nt(both, weight[:, 6 * LANE :])
    if not first:
        total = total + small[3][...]
    at = 3
    if not last:
        stores.put(at, total)
        return
    gain_ref, shift_ref = small[-2:]
    pre = tokens.astype(F32) + total
    center = pre - mean_of(pre)
    inv = lax.rsqrt(mean_of(center * center) + 1e-12)
    hat = center * inv
    low = (hat * gain_ref[...] + shift_ref[...]).astype(BF)
    stores.put(at + 2, low)
    stores.put(at, hat)
    stores.put(at + 1, jnp.broadcast_to(inv, (hat.shape[0], LANE)))
    store_turned(scal, stores.bufs[at + 3], low)
    stores.send(at + 3)


def ffn_fwd_kernel(units, first, last, scal, small, loads, stores):
    low = small[0][...]
    total = None
    for number in range(units):
        up = dot(low, loads.pop()[...])
        phi_big = 0.5 + 0.5 * lax.erf(up * (0.5 ** 0.5))
        phi_small = jnp.exp(up * up * -0.5) * 0.3989422804014327
        act = (up * phi_big).astype(BF)
        stores.put(number * 2, act)
        stores.put(number * 2 + 1, (phi_big + up * phi_small).astype(BF))
        part = dot(act, loads.pop()[...])
        total = part if total is None else total + part
    if not first:
        total = total + small[1][...]
    at = units * 2
    if not last:
        stores.put(at, total)
        return
    hat_ref, gain1_ref, shift1_ref, gain2_ref, shift2_ref = small[-5:]
    gain2 = gain2_ref[...]
    pre = hat_ref[...] * gain1_ref[...] + shift1_ref[...] + total
    center = pre - mean_of(pre)
    inv = lax.rsqrt(mean_of(center * center) + 1e-12)
    hat = center * inv
    cot = loads.pop()[...].astype(F32)
    scaled = cot * gain2
    dpre = (scaled - mean_of(scaled) - hat * mean_of(scaled * hat)) * inv
    dffn = dpre.astype(BF)
    stores.put(at + 2, dffn)
    stores.put(at + 1, dpre)
    store_turned(scal, stores.bufs[at + 3], dffn)
    stores.send(at + 3)
    stores.put(at, (hat * gain2 + shift2_ref[...]).astype(BF))
    stores.put(at + 4, jnp.sum(cot * hat, axis=0, keepdims=True))
    stores.put(at + 5, jnp.sum(cot, axis=0, keepdims=True))


def split_rows(stores, slot, where, value, inside=False):
    step = value.shape[0] // 4
    for number in range(4):
        rows = pl.ds(number // 2 * step, step)
        piece = value[number * step : (number + 1) * step]
        if inside:
            stores.part(slot, piece, number % 2, rows)
        else:
            stores.part(slot + number % 2, piece, *where, rows)


def ffn_bwd_kernel(near, has_recv, last, size, scal, small, loads, stores):
    dffn_ref, dffn_t_ref, low_t_ref, acc_ref = small[:4]
    wd, slope = loads.pop(), loads.pop()
    d_up = (dot_nt(dffn_ref[...], wd[...]) * slope[...].astype(F32)).astype(BF)
    down = dot(dffn_t_ref[...], loads.pop()[...])
    got = [loads.pop() for _ in range(2)] if has_recv else None
    for r in range(4):
        value = down[:, r * size : (r + 1) * size]
        if has_recv:
            value = value + got[r // 2][0, r % 2].astype(F32)
        stores.part(r // 2, value.astype(BF), *((r % 2,) if near else (0, r % 2)))
    if near:
        stores.send(0)
        stores.send(1)
    up = dot(low_t_ref[...], d_up)
    for r in range(4):
        value = up[:, r * size : (r + 1) * size]
        if has_recv:
            value = value + got[r // 2][1, r % 2].astype(F32)
        if near:
            split_rows(stores, 2, (r,), value.astype(BF))
        else:
            stores.part(r // 2, value.astype(BF), 1, r % 2)
    if near:
        stores.send(2)
        stores.send(3)
    else:
        stores.send(0)
        stores.send(1)
    total = acc_ref[...] + dot_nt(d_up, loads.pop()[...])
    at = 4 if near else 2
    if not last:
        stores.put(at, total)
        return
    hat_ref, inv_ref, gain_ref = small[4:]
    hat = hat_ref[...]
    scaled = total * gain_ref[...]
    inv = inv_ref[:, :1]
    dpre = (scaled - mean_of(scaled) - hat * mean_of(scaled * hat)) * inv
    datt = dpre.astype(BF)
    stores.put(at + 1, datt)
    stores.put(at, dpre)
    store_turned(scal, stores.bufs[at + 2], datt)
    stores.send(at + 2)
    stores.put(at + 3, jnp.sum(total * hat, axis=0, keepdims=True))
    stores.put(at + 4, jnp.sum(total, axis=0, keepdims=True))


def attn_bwd_kernel(kind, near, has_recv, scal, small, loads, stores):
    col_ref, row_ref, datt_ref, datt_t_ref, tok_t_ref, acc_ref = small
    bias = bias_of(col_ref[...], row_ref[...])
    lane = lax.broadcasted_iota(jnp.int32, (1, LANE), 1)
    weight = loads.pop()
    if kind == "whole":
        dctx_all = dot_nt(datt_ref[...], loads.pop()[...]).astype(BF)
    else:
        dctx_all = dot(datt_ref[...], weight[:, 6 * LANE :]).astype(BF)
    length = dctx_all.shape[0]
    qkv, lse = loads.pop(), loads.pop()
    grads = [[], [], []]

    def chosen(value):
        return jnp.where(lane < HDIM, value[:length], value[length:]).astype(BF)

    for unit in range(2):
        dctx = dctx_all[:, unit * LANE : (unit + 1) * LANE]
        query, key, value = head_parts(qkv, unit)
        keys = stacked(key, lane)
        scores = dot_nt(keys, query)
        d_probs = dot_nt(stacked(value, lane), dctx)
        probs, d_scores = [], []
        for head in range(2):
            rows = slice(head * length, (head + 1) * length)
            row = 2 * unit + head
            prob = jnp.exp(scores[rows] + bias - lse[row : row + 1, :])
            d_prob = d_probs[rows]
            inner = jnp.sum(prob * d_prob, axis=0, keepdims=True)
            probs.append(prob.astype(BF))
            d_scores.append((prob * (d_prob - inner)).astype(BF))
        d_scores = jnp.concatenate(d_scores, axis=0)
        grads[0].append((dot(keys.T, d_scores) * SCALE).astype(BF).T)
        grads[1].append(chosen(dot(d_scores, query)))
        grads[2].append(chosen(dot(jnp.concatenate(probs, axis=0), dctx)))
    tok_t = tok_t_ref[...]
    both = jnp.concatenate(grads[0] + grads[1] + grads[2], axis=1)
    ctx = loads.pop()
    qk = dot(tok_t, both[:, : 4 * LANE])
    if has_recv:
        qk = qk + loads.pop()[...].astype(F32)
    vo = jnp.concatenate(
        [dot(tok_t, both[:, 4 * LANE :]), dot(datt_t_ref[...], ctx[...])], axis=1
    )
    if has_recv:
        vo = vo + loads.pop()[...].astype(F32)
    if near:
        split_rows(stores, 0, (0,), qk.astype(BF), True)
        stores.send(0)
        split_rows(stores, 1, (), vo.astype(BF))
        stores.send(1)
        stores.send(2)
    else:
        stores.put(0, qk.astype(BF))
        stores.put(1, vo.astype(BF))
    stores.put(3 if near else 2, acc_ref[...] + dot_nt(both, weight[:, : 6 * LANE]))


def swap(value, axis, bit):
    count = lax.axis_size(axis)
    return lax.ppermute(value, axis, [(i, i ^ bit) for i in range(count)])


def add(*values):
    total = values[0].astype(F32)
    for value in values[1:]:
        total = total + value.astype(F32)
    return total.astype(BF)


def tie(values, *after):
    return list(lax.optimization_barrier((tuple(values), after))[0])


def sync(values, arrived):
    return lax.optimization_barrier((*values, *arrived))


def join(values, axis=0):
    return jnp.concatenate(values, axis=axis)


def body(
    tokens,
    segment_ids,
    qkv_weight,
    out_weight,
    up_weight,
    down_weight,
    gain_attn,
    shift_attn,
    gain_ffn,
    shift_ffn,
    cotangent,
):
    count, width = tokens.shape
    seq, tp = lax.axis_size("seq"), lax.axis_size("tp")
    me_seq, me_tp = lax.axis_index("seq"), lax.axis_index("tp")
    blocks = width // LANE
    pairs = blocks // 2
    size = up_weight.shape[1] * tp // (4 * pairs)
    fast = seq == blocks and seq == 8 and tp == 4 and qkv_weight.shape[2] == 2 * LANE
    seg = lax.dynamic_slice_in_dim(segment_ids, me_tp, 1, axis=0)
    seg_col = seg.reshape(count, 1)
    gains = [g.reshape(1, width) for g in (gain_attn, shift_attn, gain_ffn, shift_ffn)]
    absolute = jnp.arange(blocks, dtype=jnp.int32)
    half, quarter, eighth = width // 2, width // 4, width // 8
    wide = (count, width)
    work = 2 * count * width
    bit_x, bit_z = me_seq & 1, (me_seq >> 1) & 1

    def over_x(value):
        return swap(value, "seq", 1)

    def over_z(value):
        return swap(value, "seq", 2)

    def over_y(value):
        return swap(value, "tp", 2)

    def over_core(value):
        return swap(value, "tp", 1)

    if fast:
        rel = absolute ^ me_seq
        pos = ((rel >> 1) & 1) * 4 + (rel & 1) * 2 + (rel >> 2)
        mine = me_seq & 3
        scal = jnp.stack(
            [pos[i] for i in range(blocks)] + [mine ^ r for r in range(4)]
        ).astype(jnp.int32)
        table = [("table", 8 + r) for r in range(4)]
        needs = []
        for r in (0, 3):
            shape = (width, LANE)
            needs += [
                Need(shape, BF, (qkv_weight, matrix_at(table[r], which), everything))
                for which in range(2)
            ]
            needs.append(
                Need((LANE, width), BF, (out_weight, out_rows_at(table[r]), everything))
            )
        cuts = call(
            functools.partial(cut_kernel, [table[0], table[3]]), needs,
            [((width, 2 * LANE), BF)] * 2, scal, [], "cut", 1,
        )
        head_a, head_d = over_y(cuts[0]), over_y(cuts[1])
        near = [over_core(w) for w in (qkv_weight, out_weight)]
    else:
        scal = jnp.concatenate([absolute, jnp.zeros((4,), jnp.int32)])
        qkv_all = lax.all_gather(qkv_weight, "tp", axis=2, tiled=True)
        out_all = lax.all_gather(out_weight, "tp", axis=0, tiled=True)
        up_all = lax.all_gather(up_weight, "tp", axis=1, tiled=True)
        down_all = lax.all_gather(down_weight, "tp", axis=0, tiled=True)

    kept, acts = {}, {}

    def attn_fwd(j, total, last):
        needs = attn_needs(heads[j], False)
        outs = [((count, 6 * LANE), BF), ((count, 2 * LANE), BF), ((8, count), F32)]
        if last:
            outs += [
                hot(wide, F32), hot((count, LANE), F32), hot(wide, BF), hot((width, count), BF),
            ]
        else:
            outs.append(hot(wide, F32))
        first = total is None
        small = [seg_col, seg, tokens] + ([] if first else [total]) + (gains[:2] if last else [])
        res = call(
            functools.partial(attn_fwd_kernel, heads[j][0], first, last),
            needs, outs, scal, small, f"attn_fwd{j}", 1,
        )
        kept[j] = res[:3]
        return res[3:]

    def ffn_fwd(number, group, total, last):
        needs, outs = [], []
        for unit in group:
            pieces = [hidden[piece] for piece in unit]
            needs += [up_need(pieces, size, False), down_need(pieces, size, False)]
            outs += [((count, len(unit) * size), BF)] * 2
        first = total is None
        small = [low] + ([] if first else [total])
        if last:
            needs.append(need(cotangent))
            small += [hat, *gains]
            outs += [
                (wide, BF), hot(wide, F32), hot(wide, BF), hot((width, count), BF),
                hot((1, width), F32), hot((1, width), F32),
            ]
        else:
            outs.append(hot(wide, F32))
        res = call(
            functools.partial(ffn_fwd_kernel, len(group), first, last),
            needs, outs, scal, small, f"ffn_fwd{number}", 8 * work * size * len(group),
        )
        for index, unit in enumerate(group):
            for place, piece in enumerate(unit):
                acts[piece] = [(array, place) for array in res[index * 2 : index * 2 + 2]]
        return res[len(group) * 2 :]

    if fast:
        heads, hidden = {}, {}
        heads[0] = ("whole", qkv_weight, out_weight, 0)
        heads[1] = ("whole", *near[:2], 0)
        for r in range(4):
            hidden[0, r] = ("whole", up_weight, down_weight, table[r], width)

        def packed(r, both):
            hidden[2, r] = ("packed", both, both, width)
            other = over_core(both)
            hidden[3, r] = ("packed", other, other, width)

        (total,) = attn_fwd(0, None, False)
        total, *weights = sync([total], [up_weight, down_weight])
        needs = []
        for r in (0, 3):
            own = [("whole", *weights, table[r], width)]
            needs += [up_need(own, size), down_need(own, size)]
        packs = call(
            functools.partial(pack_kernel, size), needs,
            [((2, width, size), BF)] * 2, scal, [], "pack", 1,
        )
        ffn_a, ffn_d = over_y(packs[0]), over_y(packs[1])
        (head_a,) = tie([head_a], total, *near)
        head_b, head_c = over_x(head_a), over_z(head_a)
        other_a = over_core(head_a)
        (total,) = attn_fwd(1, total, False)
        tok_t = call(
            turn_kernel, [], [hot((width, count), BF)], scal, tie([tokens], total), "turn", 1
        )[0]
        head_b, head_c, head_d = tie([head_b, head_c, head_d], tok_t)
        pieces = [head_a, head_b, head_c, head_d]
        heads[2] = ("packed", pieces)
        heads[3] = ("packed", [other_a] + [over_core(p) for p in pieces[1:]])
        (total,) = attn_fwd(2, total, False)
        total, ffn_a = sync([total], [ffn_a])
        late = [over_core(w) for w in tie([up_weight, down_weight], *heads[3][1])]
        for r in range(4):
            hidden[1, r] = ("whole", *late, table[r], width)
        hat, inv, low, low_t = attn_fwd(3, total, True)
        ffn_b, ffn_c = over_x(ffn_a), over_z(ffn_a)
        packed(0, ffn_a)
        (total,) = ffn_fwd(0, [[(0, r) for r in range(4)]], None, False)
        (total,) = ffn_fwd(1, [[(2, 0), (3, 0)]], total, False)
        (total,) = ffn_fwd(2, [[(1, r) for r in range(4)]], total, False)
        for r, both in zip((1, 2, 3), tie([ffn_b, ffn_c, ffn_d], total)):
            packed(r, both)
        (total,) = ffn_fwd(3, [[(2, r) for r in (1, 2, 3)]], total, False)
        res = ffn_fwd(4, [[(3, r) for r in (1, 2, 3)]], total, True)
    else:
        heads = {j: ("whole", qkv_all, out_all, j) for j in range(pairs)}
        hidden = {
            (k // 4, k % 4): ("whole", up_all, down_all, ("block", k), width)
            for k in range(4 * pairs)
        }
        tok_t = call(
            turn_kernel, [], [hot((width, count), BF)], scal, [tokens], "turn", 1
        )[0]
        total = None
        for j in range(pairs):
            res = attn_fwd(j, total, j == pairs - 1)
            total = res[0]
        hat, inv, low, low_t = res
        total = None
        for j in range(pairs):
            res = ffn_fwd(j, [[(j, r) for r in range(4)]], total, j == pairs - 1)
            total = res[0]
    mixed, d_pre, d_ffn, d_ffn_t, g_gain2, g_shift2 = res

    order = [3, 1, 2, 0] if fast else list(range(pairs))
    ffn_g, attn_g, from_core = {}, {}, {}
    total = d_pre
    for j in order:
        last = j == order[-1]
        here = not fast or j % 2 == 0
        recv = from_core.get(j)
        pieces = [hidden[j, r] for r in range(4)]
        saved = [acts[j, r] for r in range(4)]
        needs = [
            down_need(pieces, size),
            saved_need([s[1] for s in saved], size),
            saved_need([s[0] for s in saved], size),
        ]
        if recv is not None:
            needs += [need(g, False) for g in recv]
        needs.append(up_need(pieces, size))
        small = [d_ffn, d_ffn_t, low_t, total]
        if here:
            outs = [((2, width, size), BF)] * 2 + [((4, half, size), BF)] * 2
        else:
            outs = [((2, 2, width, size), BF)] * 2
        grads = len(outs)
        if last:
            small += [hat, inv, gains[0]]
            outs = outs + [
                hot(wide, F32), hot(wide, BF), hot((width, count), BF),
                hot((1, width), F32), hot((1, width), F32),
            ]
        else:
            outs = outs + [hot(wide, F32)]
        res = call(
            functools.partial(ffn_bwd_kernel, here, recv is not None, last, size),
            needs, outs, scal, small, f"ffn_bwd{j}", 1,
        )
        ffn_g[j], total = res[:grads], res[grads]
        if not here:
            from_core[j - 1] = [over_core(g) for g in res[:grads]]
        if fast and j == 2:
            down_y = [over_y(g) for g in res[:2]]
            far_x = over_x(res[3])
    d_pre_one, d_att, d_att_t, g_gain1, g_shift1 = res[grads:]

    norm_grads = join([g_gain1, g_shift1, g_gain2, g_shift2])

    def flip(value):
        return join([value[1:], value[:1]])

    def turn_halves(value):
        return join([value[2:], value[:2]])

    def flip_pairs(value):
        return join([value[1:2], value[:1], value[3:], value[2:3]])

    def attn_bwd(j, total):
        here = not fast or j % 2 == 0
        recv = from_core.get(("attn", j))
        needs = attn_needs(heads[j]) + [need(kept[j][0]), need(kept[j][2]), need(kept[j][1])]
        if recv is not None:
            needs += [need(g, False) for g in recv]
        each = 4 * LANE
        if here:
            outs = [((2, half, each), BF), ((half, each), BF), ((half, each), BF)]
        else:
            outs = [((width, each), BF)] * 2
        res = call(
            functools.partial(attn_bwd_kernel, heads[j][0], here, recv is not None),
            needs, outs + [hot(wide, F32)],
            scal, [seg_col, seg, d_att, d_att_t, tok_t, total], f"attn_bwd{j}", 1,
        )
        attn_g[j] = res[:-1]
        if not here:
            from_core["attn", j - 1] = [over_core(g) for g in res[:-1]]
        return res[-1]

    total = d_pre_one
    if fast:
        near_x = over_x(ffn_g[0][3])
        rest, front = slice(half, None), slice(0, half)

        def down_sum(u, rows):
            return add(ffn_g[0][u][:, rows], down_y[u][:, rows])

        total, down_y[0], far_x = sync([total], [down_y[0], far_x])
        down_z = {0: over_z(down_sum(0, rest))}
        far = add(ffn_g[2][2], flip_pairs(far_x))
        far_z = over_z(far[:, quarter:])
        total = attn_bwd(3, total)
        total = attn_bwd(1, total)

        total, down_z[0], norm_grads, down_y[1], near_x = sync(
            [total], [down_z[0], norm_grads, down_y[1], near_x]
        )
        norm_next = over_core(norm_grads)
        total = attn_bwd(2, total)

        total, far_z, norm_next = sync([total], [far_z, norm_next])
        norm_grads = norm_grads + norm_next
        down_z[1] = over_z(down_sum(1, rest))
        up_y = over_y(add(far[:, :quarter], turn_halves(far_z)))
        vo_x = over_x(attn_g[2][2])
        qk_y = over_y(attn_g[2][0])
        near = add(ffn_g[0][2], flip_pairs(near_x))
        near_z = over_z(near[:, quarter:])
        total = attn_bwd(0, total)
        token_grad = total

        def last_sum(value, got):
            return value[..., :eighth, :].astype(F32) + got.astype(F32)

        vo_near_x = over_x(attn_g[0][2])
        vo_lo, down_z[1] = sync([attn_g[0][1]], [down_z[1]])
        down = join([add(down_sum(u, front), down_z[1 - u]) for u in range(2)])
        down_x = over_x(down[:, quarter:])
        down, vo_x, up_y = sync([down], [vo_x, up_y])
        vo_y = over_y(add(attn_g[2][1], vo_x))
        down, near_z, vo_near_x = sync([down], [near_z, vo_near_x])
        up = add(near[:, :quarter], turn_halves(near_z), up_y)
        up_got = swap(up[:, eighth:], "seq", 4)
        qk_near, qk_y, norm_grads = sync([attn_g[0][0]], [qk_y, norm_grads])
        qk_x = over_x(add(qk_near[1], qk_y[1]))
        norm_next = over_y(norm_grads)
        qk_y, down_x = sync([qk_y], [down_x])
        down = add(down[:, :quarter], flip_pairs(down_x))
        down_got = swap(down[:, eighth:], "seq", 4)
        qk_y, vo_y, norm_next = sync([qk_y], [vo_y, norm_next])
        vo = add(vo_lo, vo_near_x, vo_y)
        vo_z = over_z(vo[quarter:])
        norm_grads = norm_grads + norm_next
        norm_next = over_x(norm_grads)
        vo, qk_x = sync([vo], [qk_x])
        qk = add(qk_near[0], qk_y[0], qk_x)
        qk_z = over_z(qk[quarter:])
        qk, vo_z, norm_next, up_got = sync([qk], [vo_z, norm_next, up_got])
        vo = add(vo[:quarter], vo_z)
        vo_got = swap(vo[eighth:], "seq", 4)
        norm_grads = norm_grads + norm_next
        norm_next = over_z(norm_grads)
        vo, qk_z, norm_next, down_got = sync([vo], [qk_z, norm_next, down_got])
        qk = add(qk[:quarter], qk_z)
        qk_got = swap(qk[eighth:], "seq", 4)
        norm_grads = norm_grads + norm_next
        norm_grads = norm_grads + swap(norm_grads, "seq", 4)
        down, up = last_sum(down, down_got), last_sum(up, up_got)
        vo, qk = last_sum(vo, vo_got), last_sum(qk, qk_got)
        share = width // (seq * tp)
        norm_grads = lax.dynamic_slice_in_dim(
            norm_grads, (me_seq * tp + me_tp) * share, share, axis=1
        )

        def ordered(value):
            value = jnp.where(bit_x == 0, value, flip_pairs(value))
            value = jnp.where(bit_z == 0, value, turn_halves(value))
            return join([value[r] for r in range(4)], 1)

        down_grad = ordered(down).T
        up_grad = ordered(up)
        qkv_grad = jnp.stack([qk[:, : 2 * LANE], qk[:, 2 * LANE :], vo[:, : 2 * LANE]])
        out_grad = vo[:, 2 * LANE :].T
    else:
        for j in order:
            total = attn_bwd(j, total)
        token_grad = total
        norm_grads = lax.psum_scatter(norm_grads, ("seq", "tp"), scatter_dimension=1, tiled=True)

        def scattered(value, tp_dim, seq_dim):
            value = lax.psum_scatter(value, "tp", scatter_dimension=tp_dim, tiled=True)
            value = lax.psum_scatter(value, "seq", scatter_dimension=seq_dim, tiled=True)
            return value.astype(F32)

        def rows_of(low_part, high_part):
            parts = [
                part[..., k * quarter : (k + 1) * quarter, :]
                for k in range(2)
                for part in (low_part, high_part)
            ]
            return join(parts, -2)

        down = join([ffn_g[j][u][i] for j in range(pairs) for u in range(2) for i in range(2)], 1)
        up = join(
            [rows_of(ffn_g[j][2][r], ffn_g[j][3][r]) for j in range(pairs) for r in range(4)], 1
        )
        qk = [rows_of(attn_g[j][0][0], attn_g[j][0][1]) for j in range(pairs)]
        vo = [rows_of(attn_g[j][1], attn_g[j][2]) for j in range(pairs)]
        down_grad = scattered(down, 1, 0).T
        up_grad = scattered(up, 1, 0)
        qkv_grad = jnp.stack(
            [
                join([g[:, : 2 * LANE] for g in qk], 1),
                join([g[:, 2 * LANE :] for g in qk], 1),
                join([g[:, : 2 * LANE] for g in vo], 1),
            ]
        )
        qkv_grad = scattered(qkv_grad, 2, 1)
        out_grad = scattered(join([g[:, 2 * LANE :] for g in vo], 1), 1, 0).T
    return (mixed, token_grad, qkv_grad, out_grad, up_grad, down_grad, norm_grads)


def solution(mesh):
    return jax.shard_map(
        body,
        mesh=mesh,
        in_specs=(
            P(("seq", "tp"), None),
            P("seq", None),
            P(None, None, "tp"),
            P("tp", None),
            P(None, "tp"),
            P("tp", None),
            P(),
            P(),
            P(),
            P(),
            P(("seq", "tp"), None),
        ),
        out_specs=(
            P(("seq", "tp"), None),
            P(("seq", "tp"), None),
            P(None, "seq", "tp"),
            P("tp", "seq"),
            P("seq", "tp"),
            P("tp", "seq"),
            P(None, ("seq", "tp")),
        ),
        check_vma=False,
    )
```

```python
import functools

import jax
import jax.numpy as jnp
from jax import lax
from jax.experimental import pallas as pl
from jax.experimental.pallas import tpu as pltpu
from jax.sharding import PartitionSpec as P

HDIM = 64
LANE = 128
BF = jnp.bfloat16
F32 = jnp.float32
SCALE = HDIM ** (-0.5)
MASKED = -1000000000.0
VMEM_MIB = (("attn_fwd", 16), ("ffn_fwd", 20), ("ffn_bwd", 28), ("attn_bwd", 18), ("pack", 12))


def dot(left, right):
    return jnp.dot(left, right, preferred_element_type=F32)


def dot_nt(left, right):
    return lax.dot_general(left, right, (((1,), (1,)), ((), ())), preferred_element_type=F32)


def everything(ref, scal):
    return ref


class Need:
    def __init__(self, shape, dtype, *parts, pinned=True):
        self.shape, self.dtype, self.parts, self.pinned = tuple(shape), dtype, parts, pinned


def need(array, pinned=True):
    return Need(array.shape, array.dtype, (array, everything, everything), pinned=pinned)


class Loads:
    def __init__(self, needs, refs, bufs, sems, scal):
        self.bufs, self.copies, self.next = bufs, [], 0
        at = 0
        for item, buf in zip(needs, bufs):
            mine = []
            for index, source, target in item.parts:
                copy = pltpu.make_async_copy(
                    source(refs[index], scal), target(buf, scal), sems.at[at]
                )
                copy.start()
                mine.append(copy)
                at += 1
            self.copies.append(mine)

    def take(self):
        self.next += 1
        return self.next - 1

    def get(self, slot):
        for copy in self.copies[slot]:
            copy.wait()
        self.copies[slot] = []
        return self.bufs[slot]

    def pop(self):
        return self.get(self.take())

    def finish(self):
        for slot in range(len(self.copies)):
            self.get(slot)


class Stores:
    def __init__(self, refs, bufs, sems):
        self.refs, self.sems, self.copies = refs, sems, []
        self.bufs = [ref if buf is None else buf for ref, buf in zip(refs, bufs)]
        self.direct = [buf is None for buf in bufs]
        self.next = 0

    def part(self, slot, value, *where):
        self.bufs[slot][where] = value

    def send(self, slot, *where):
        if self.direct[slot]:
            return
        source, target = self.bufs[slot], self.refs[slot]
        if where:
            source, target = source.at[where], target.at[where]
        copy = pltpu.make_async_copy(source, target, self.sems.at[self.next])
        self.next += 1
        copy.start()
        self.copies.append(copy)

    def put(self, slot, value):
        self.bufs[slot][...] = value
        self.send(slot)

    def finish(self):
        for copy in self.copies:
            copy.wait()


def hot(shape, dtype):
    return (shape, dtype, True)


def vmem_of(name):
    for start, size in VMEM_MIB:
        if name.startswith(start):
            return size
    return 16


def call(kernel, needs, outs, scal, small, name, flops, sends=None):
    arrays, parts, pinned = [], [], []
    for item in needs:
        fixed = []
        for array, source, target in item.parts:
            index = next((i for i, a in enumerate(arrays) if a is array), None)
            if index is None:
                index = len(arrays)
                arrays.append(array)
                pinned.append(item.pinned)
            fixed.append((index, source, target))
        parts.append(Need(item.shape, item.dtype, *fixed))
    copies = max(1, sum(len(item.parts) for item in parts))
    sends = max(1, len(outs) if sends is None else sends)
    here = [len(out) == 3 for out in outs]

    def run(*refs):
        refs = list(refs)
        scal_ref = refs.pop(0)
        small_refs = [refs.pop(0) for _ in small]
        in_refs = [refs.pop(0) for _ in arrays]
        out_refs = [refs.pop(0) for _ in outs]
        in_bufs = [refs.pop(0) for _ in parts]
        out_bufs = [None if stays else refs.pop(0) for stays in here]
        in_sems, out_sems = refs
        loads = Loads(parts, in_refs, in_bufs, in_sems, scal_ref)
        stores = Stores(out_refs, out_bufs, out_sems)
        kernel(scal_ref, small_refs, loads, stores)
        loads.finish()
        stores.finish()

    return pl.pallas_call(
        run,
        out_shape=[
            jax.ShapeDtypeStruct(out[0], out[1]) if stays else pltpu.HBM(out[0], out[1])
            for out, stays in zip(outs, here)
        ],
        in_specs=[pl.BlockSpec(memory_space=pltpu.SMEM)]
        + [pl.BlockSpec(memory_space=pltpu.VMEM)] * len(small)
        + [pl.BlockSpec(memory_space=pltpu.HBM if p else pl.ANY) for p in pinned],
        out_specs=[
            pl.BlockSpec(memory_space=pltpu.VMEM if stays else pltpu.HBM) for stays in here
        ],
        scratch_shapes=[pltpu.VMEM(item.shape, item.dtype) for item in parts]
        + [pltpu.VMEM(out[0], out[1]) for out, stays in zip(outs, here) if not stays]
        + [pltpu.SemaphoreType.DMA((copies,)), pltpu.SemaphoreType.DMA((sends,))],
        compiler_params=pltpu.CompilerParams(vmem_limit_bytes=vmem_of(name) * 1024 * 1024),
        cost_estimate=pl.CostEstimate(flops=flops, bytes_accessed=0, transcendentals=0),
        name=name,
    )(
        scal,
        *small,
        *[
            pltpu.with_memory_space_constraint(a, pltpu.HBM) if p else a
            for a, p in zip(arrays, pinned)
        ],
    )


def store_turned(scal, buf, values):
    for block in range(values.shape[1] // LANE):
        start = pl.multiple_of(scal[block] * LANE, LANE)
        buf[pl.ds(start, LANE), :] = values[:, block * LANE : (block + 1) * LANE].T


def block_of(scal, place):
    kind, value = place
    return scal[value] if kind == "table" else value


def columns(place, size, *front):
    def take(ref, scal):
        start = pl.multiple_of(block_of(scal, place) * size, size)
        return ref.at[(*front, slice(None), pl.ds(start, size))]

    return take


def lines(place, size):
    def take(ref, scal):
        start = pl.multiple_of(block_of(scal, place) * size, size)
        return ref.at[pl.ds(start, size), :]

    return take


def lanes_at(start, size):
    return lambda ref, scal: ref.at[:, pl.ds(start, size)]


def lines_at(start, size):
    return lambda ref, scal: ref.at[pl.ds(start, size), :]


def slot_at(*where):
    return lambda ref, scal: ref.at[where]


def stacked_at(index, size):
    def take(ref, scal):
        ref = ref if len(ref.shape) == 2 else ref.at[1]
        return ref.at[pl.ds(index * size, size), :]

    return take


def block_at(row, column, size):
    return lambda ref, scal: ref.at[pl.ds(row * size, size), pl.ds(column * size, size)]


def first_of(ref, scal):
    return ref if len(ref.shape) == 2 else ref.at[0]


def part_of(place):
    def find(scal):
        quarter = block_of(scal, place)
        return quarter // 2, lax.rem(quarter, 2)

    return find


def matrix_at(place, which):
    def take(ref, scal):
        half, pair = part_of(place)(scal)
        index = 1 if which else 2 * pair
        return ref.at[index, :, pl.ds(pl.multiple_of(half * LANE, LANE), LANE)]

    return take


def out_rows_at(place):
    def take(ref, scal):
        half, _ = part_of(place)(scal)
        return ref.at[pl.ds(pl.multiple_of(half * LANE, LANE), LANE), :]

    return take


def piece_lanes(place, which):
    def take(buf, scal):
        half, pair = part_of(place)(scal)
        start = pair * 4 * LANE + half * LANE + which * 2 * LANE
        return buf.at[:, pl.ds(pl.multiple_of(start, LANE), LANE)]

    return take


def attn_needs(block, pinned=True):
    if block[0] == "packed":
        pieces = block[1]
        parts = [
            (piece, lanes_at(which * LANE, LANE), piece_lanes(("table", 8 + r), which))
            for r, piece in enumerate(pieces)
            for which in range(2)
        ]
        return [Need((pieces[0].shape[0], 8 * LANE), BF, *parts, pinned=pinned)]
    _, qkv, out, index = block
    depth, width = qkv.shape[1], out.shape[1]
    place = ("block", index)
    return [
        Need(
            (depth, 6 * LANE), BF,
            *[
                (qkv, columns(place, 2 * LANE, i), lanes_at(2 * i * LANE, 2 * LANE))
                for i in range(3)
            ],
        ),
        Need((2 * LANE, width), BF, (out, lines(place, 2 * LANE), everything)),
    ]


def up_need(pieces, size, pinned=True):
    parts = []
    for number, piece in enumerate(pieces):
        target = lanes_at(number * size, size)
        if piece[0] == "packed":
            parts.append((piece[1], first_of, target))
        else:
            parts.append((piece[1], columns(piece[3], size), target))
    return Need((pieces[0][-1], len(pieces) * size), BF, *parts, pinned=pinned)


def down_need(pieces, size, pinned=True):
    parts = []
    for number, piece in enumerate(pieces):
        width = piece[-1]
        if piece[0] == "packed":
            for index in range(width // size):
                parts.append(
                    (piece[2], stacked_at(index, size), block_at(number, index, size))
                )
        else:
            parts.append((piece[2], lines(piece[3], size), lines_at(number * size, size)))
    return Need((len(pieces) * size, pieces[0][-1]), BF, *parts, pinned=pinned)


def saved_need(pieces, size):
    parts = [
        (array, lanes_at(index * size, size), lanes_at(number * size, size))
        for number, (array, index) in enumerate(pieces)
    ]
    return Need((pieces[0][0].shape[0], len(pieces) * size), BF, *parts)


def mean_of(values):
    return jnp.mean(values, axis=-1, keepdims=True)


def bias_of(seg_col, seg_row):
    return jnp.where(seg_col == seg_row, 0.0, MASKED)


def cut_kernel(places, scal, small, loads, stores):
    for slot, place in enumerate(places):
        first, second, out = loads.pop(), loads.pop(), loads.pop()
        _, pair = part_of(place)(scal)
        stores.part(slot, first[...], slice(None), slice(0, LANE))

        @pl.when(pair == 0)
        def _():
            stores.part(slot, second[...], slice(None), slice(LANE, 2 * LANE))

        @pl.when(pair == 1)
        def _():
            stores.part(slot, out[...].T, slice(None), slice(LANE, 2 * LANE))

        stores.send(slot)


def pack_kernel(size, scal, small, loads, stores):
    for slot in range(2):
        up, down = loads.pop(), loads.pop()
        stores.part(slot, up[...], 0)
        for index in range(down.shape[1] // size):
            block = down[:, index * size : (index + 1) * size]
            stores.part(slot, block, 1, pl.ds(index * size, size))
        stores.send(slot)


def turn_kernel(scal, small, loads, stores):
    store_turned(scal, stores.bufs[0], small[0][...])
    stores.send(0)


def head_parts(qkv, unit):
    query, key, value = (
        qkv[:, (2 * i + unit) * LANE : (2 * i + unit + 1) * LANE] for i in range(3)
    )
    return query * jnp.asarray(SCALE, BF), key, value


def stacked(pair, lane):
    zero = jnp.zeros_like(pair)
    return jnp.concatenate(
        [jnp.where(lane < HDIM, pair, zero), jnp.where(lane >= HDIM, pair, zero)], axis=0
    )


def attn_fwd_kernel(kind, first, last, scal, small, loads, stores):
    col_ref, row_ref, tokens_ref = small[:3]
    tokens = tokens_ref[...]
    bias = bias_of(col_ref[...], row_ref[...])
    lane = lax.broadcasted_iota(jnp.int32, (1, LANE), 1)
    length = tokens.shape[0]
    weight = loads.pop()
    qkv = dot(tokens, weight[:, : 6 * LANE]).astype(BF)
    stores.put(0, qkv)
    contexts = []
    for unit in range(2):
        query, key, value = head_parts(qkv, unit)
        scores = dot_nt(stacked(key, lane), query)
        probs = []
        for head in range(2):
            mine = scores[head * length : (head + 1) * length] + bias
            peak = jnp.max(mine, axis=0, keepdims=True)
            raw = jnp.exp(mine - peak)
            summed = jnp.sum(raw, axis=0, keepdims=True)
            stores.part(2, peak + jnp.log(summed), pl.ds(2 * unit + head, 1), slice(None))
            probs.append((raw * (1.0 / summed)).astype(BF))
        context = dot(stacked(value, lane).T, jnp.concatenate(probs, axis=0))
        contexts.append(context.astype(BF).T)
    stores.send(2)
    both = jnp.concatenate(contexts, axis=1)
    stores.put(1, both)
    if kind == "whole":
        total = dot(both, loads.pop()[...])
    else:
        total = dot_nt(both, weight[:, 6 * LANE :])
    if not first:
        total = total + small[3][...]
    at = 3
    if not last:
        stores.put(at, total)
        return
    gain_ref, shift_ref = small[-2:]
    pre = tokens.astype(F32) + total
    center = pre - mean_of(pre)
    inv = lax.rsqrt(mean_of(center * center) + 1e-12)
    hat = center * inv
    low = (hat * gain_ref[...] + shift_ref[...]).astype(BF)
    stores.put(at + 2, low)
    stores.put(at, hat)
    stores.put(at + 1, jnp.broadcast_to(inv, (hat.shape[0], LANE)))
    store_turned(scal, stores.bufs[at + 3], low)
    stores.send(at + 3)


def ffn_fwd_kernel(units, first, last, scal, small, loads, stores):
    low = small[0][...]
    total = None
    for number in range(units):
        up = dot(low, loads.pop()[...])
        phi_big = 0.5 + 0.5 * lax.erf(up * (0.5 ** 0.5))
        phi_small = jnp.exp(up * up * -0.5) * 0.3989422804014327
        act = (up * phi_big).astype(BF)
        stores.put(number * 2, act)
        stores.put(number * 2 + 1, (phi_big + up * phi_small).astype(BF))
        part = dot(act, loads.pop()[...])
        total = part if total is None else total + part
    if not first:
        total = total + small[1][...]
    at = units * 2
    if not last:
        stores.put(at, total)
        return
    hat_ref, gain1_ref, shift1_ref, gain2_ref, shift2_ref = small[-5:]
    gain2 = gain2_ref[...]
    pre = hat_ref[...] * gain1_ref[...] + shift1_ref[...] + total
    center = pre - mean_of(pre)
    inv = lax.rsqrt(mean_of(center * center) + 1e-12)
    hat = center * inv
    cot = loads.pop()[...].astype(F32)
    scaled = cot * gain2
    dpre = (scaled - mean_of(scaled) - hat * mean_of(scaled * hat)) * inv
    dffn = dpre.astype(BF)
    stores.put(at + 2, dffn)
    stores.put(at + 1, dpre)
    store_turned(scal, stores.bufs[at + 3], dffn)
    stores.send(at + 3)
    stores.put(at, (hat * gain2 + shift2_ref[...]).astype(BF))
    stores.put(at + 4, jnp.sum(cot * hat, axis=0, keepdims=True))
    stores.put(at + 5, jnp.sum(cot, axis=0, keepdims=True))


def split_rows(stores, slot, where, value, inside=False):
    step = value.shape[0] // 4
    for number in range(4):
        rows = pl.ds(number // 2 * step, step)
        piece = value[number * step : (number + 1) * step]
        if inside:
            stores.part(slot, piece, number % 2, rows)
        else:
            stores.part(slot + number % 2, piece, *where, rows)


def ffn_bwd_kernel(near, has_recv, last, size, scal, small, loads, stores):
    dffn_ref, dffn_t_ref, low_t_ref, acc_ref = small[:4]
    down = dot(dffn_t_ref[...], loads.pop()[...])
    got = [loads.pop() for _ in range(2)] if has_recv else None
    for r in range(4):
        value = down[:, r * size : (r + 1) * size]
        if has_recv:
            value = value + got[r // 2][0, r % 2].astype(F32)
        stores.part(r // 2, value.astype(BF), *((r % 2,) if near else (0, r % 2)))
    if near:
        stores.send(0)
        stores.send(1)
    wd, slope = loads.pop(), loads.pop()
    d_up = (dot_nt(dffn_ref[...], wd[...]) * slope[...].astype(F32)).astype(BF)
    up = dot(low_t_ref[...], d_up)
    for r in range(4):
        value = up[:, r * size : (r + 1) * size]
        if has_recv:
            value = value + got[r // 2][1, r % 2].astype(F32)
        if near:
            split_rows(stores, 2, (r,), value.astype(BF))
        else:
            stores.part(r // 2, value.astype(BF), 1, r % 2)
    if near:
        stores.send(2)
        stores.send(3)
    else:
        stores.send(0)
        stores.send(1)
    total = acc_ref[...] + dot_nt(d_up, loads.pop()[...])
    at = 4 if near else 2
    if not last:
        stores.put(at, total)
        return
    hat_ref, inv_ref, gain_ref = small[4:]
    hat = hat_ref[...]
    scaled = total * gain_ref[...]
    inv = inv_ref[:, :1]
    dpre = (scaled - mean_of(scaled) - hat * mean_of(scaled * hat)) * inv
    datt = dpre.astype(BF)
    stores.put(at + 1, datt)
    stores.put(at, dpre)
    store_turned(scal, stores.bufs[at + 2], datt)
    stores.send(at + 2)
    stores.put(at + 3, jnp.sum(total * hat, axis=0, keepdims=True))
    stores.put(at + 4, jnp.sum(total, axis=0, keepdims=True))


def attn_bwd_kernel(kind, near, has_recv, scal, small, loads, stores):
    col_ref, row_ref, datt_ref, datt_t_ref, tok_t_ref = small
    bias = bias_of(col_ref[...], row_ref[...])
    lane = lax.broadcasted_iota(jnp.int32, (1, LANE), 1)
    qkv, lse = loads.pop(), loads.pop()
    pairs, keys, probs = [], [], []
    length = bias.shape[0]
    for unit in range(2):
        query, key, value = head_parts(qkv, unit)
        keys.append(stacked(key, lane))
        scores = dot_nt(keys[unit], query)
        pairs.append((query, value))
        for head in range(2):
            row = 2 * unit + head
            mine = scores[head * length : (head + 1) * length] + bias
            probs.append(jnp.exp(mine - lse[row : row + 1, :]))
    weight = loads.pop()
    if kind == "whole":
        dctx_all = dot_nt(datt_ref[...], loads.pop()[...]).astype(BF)
    else:
        dctx_all = dot(datt_ref[...], weight[:, 6 * LANE :]).astype(BF)
    grads = [[], [], []]

    def chosen(value):
        return jnp.where(lane < HDIM, value[:length], value[length:]).astype(BF)

    for unit in range(2):
        dctx = dctx_all[:, unit * LANE : (unit + 1) * LANE]
        query, value = pairs[unit]
        d_probs = dot_nt(stacked(value, lane), dctx)
        d_scores = []
        for head in range(2):
            prob = probs[2 * unit + head]
            d_prob = d_probs[head * length : (head + 1) * length]
            inner = jnp.sum(prob * d_prob, axis=0, keepdims=True)
            d_scores.append((prob * (d_prob - inner)).astype(BF))
        d_scores = jnp.concatenate(d_scores, axis=0)
        low_probs = jnp.concatenate([p.astype(BF) for p in probs[2 * unit : 2 * unit + 2]], axis=0)
        grads[0].append((dot(keys[unit].T, d_scores) * SCALE).astype(BF).T)
        grads[1].append(chosen(dot(d_scores, query)))
        grads[2].append(chosen(dot(low_probs, dctx)))
    tok_t = tok_t_ref[...]
    both = jnp.concatenate(grads[0] + grads[1] + grads[2], axis=1)
    ctx = loads.pop()
    qk = dot(tok_t, both[:, : 4 * LANE])
    if has_recv:
        qk = qk + loads.pop()[...].astype(F32)
    vo = jnp.concatenate(
        [dot(tok_t, both[:, 4 * LANE :]), dot(datt_t_ref[...], ctx[...])], axis=1
    )
    if has_recv:
        vo = vo + loads.pop()[...].astype(F32)
    if near:
        split_rows(stores, 0, (0,), qk.astype(BF), True)
        stores.send(0)
        split_rows(stores, 1, (), vo.astype(BF))
        stores.send(1)
        stores.send(2)
    else:
        stores.put(0, qk.astype(BF))
        stores.put(1, vo.astype(BF))
    stores.put(3 if near else 2, loads.pop()[...] + dot_nt(both, weight[:, : 6 * LANE]))


def swap(value, axis, bit):
    count = lax.axis_size(axis)
    return lax.ppermute(value, axis, [(i, i ^ bit) for i in range(count)])


def add(*values):
    total = values[0].astype(F32)
    for value in values[1:]:
        total = total + value.astype(F32)
    return total.astype(BF)


def tie(values, *after):
    return list(lax.optimization_barrier((tuple(values), after))[0])


def sync(values, arrived):
    return lax.optimization_barrier((*values, *arrived))


def join(values, axis=0):
    return jnp.concatenate(values, axis=axis)


def body(
    tokens,
    segment_ids,
    qkv_weight,
    out_weight,
    up_weight,
    down_weight,
    gain_attn,
    shift_attn,
    gain_ffn,
    shift_ffn,
    cotangent,
):
    count, width = tokens.shape
    seq, tp = lax.axis_size("seq"), lax.axis_size("tp")
    me_seq, me_tp = lax.axis_index("seq"), lax.axis_index("tp")
    blocks = width // LANE
    pairs = blocks // 2
    size = up_weight.shape[1] * tp // (4 * pairs)
    fast = seq == blocks and seq == 8 and tp == 4 and qkv_weight.shape[2] == 2 * LANE
    seg = lax.dynamic_slice_in_dim(segment_ids, me_tp, 1, axis=0)
    seg_col = seg.reshape(count, 1)
    gains = [g.reshape(1, width) for g in (gain_attn, shift_attn, gain_ffn, shift_ffn)]
    absolute = jnp.arange(blocks, dtype=jnp.int32)
    half, quarter, eighth = width // 2, width // 4, width // 8
    wide = (count, width)
    work = 2 * count * width
    bit_x, bit_z = me_seq & 1, (me_seq >> 1) & 1

    def over_x(value):
        return swap(value, "seq", 1)

    def over_z(value):
        return swap(value, "seq", 2)

    def over_y(value):
        return swap(value, "tp", 2)

    def over_core(value):
        return swap(value, "tp", 1)

    if fast:
        rel = absolute ^ me_seq
        pos = ((rel >> 1) & 1) * 4 + (rel & 1) * 2 + (rel >> 2)
        mine = me_seq & 3
        scal = jnp.stack(
            [pos[i] for i in range(blocks)] + [mine ^ r for r in range(4)]
        ).astype(jnp.int32)
        table = [("table", 8 + r) for r in range(4)]
        needs = []
        for r in (0, 3):
            shape = (width, LANE)
            needs += [
                Need(shape, BF, (qkv_weight, matrix_at(table[r], which), everything))
                for which in range(2)
            ]
            needs.append(
                Need((LANE, width), BF, (out_weight, out_rows_at(table[r]), everything))
            )
        cuts = call(
            functools.partial(cut_kernel, [table[0], table[3]]), needs,
            [((width, 2 * LANE), BF)] * 2, scal, [], "cut", 1,
        )
        head_a, head_d = over_y(cuts[0]), over_y(cuts[1])
        near = [over_core(w) for w in (qkv_weight, out_weight)]
    else:
        scal = jnp.concatenate([absolute, jnp.zeros((4,), jnp.int32)])
        qkv_all = lax.all_gather(qkv_weight, "tp", axis=2, tiled=True)
        out_all = lax.all_gather(out_weight, "tp", axis=0, tiled=True)
        up_all = lax.all_gather(up_weight, "tp", axis=1, tiled=True)
        down_all = lax.all_gather(down_weight, "tp", axis=0, tiled=True)

    kept, acts = {}, {}

    def attn_fwd(j, total, last):
        needs = attn_needs(heads[j], False)
        outs = [((count, 6 * LANE), BF), ((count, 2 * LANE), BF), ((8, count), F32)]
        if last:
            outs += [
                hot(wide, F32), hot((count, LANE), F32), hot(wide, BF), hot((width, count), BF),
            ]
        else:
            outs.append(hot(wide, F32))
        first = total is None
        small = [seg_col, seg, tokens] + ([] if first else [total]) + (gains[:2] if last else [])
        res = call(
            functools.partial(attn_fwd_kernel, heads[j][0], first, last),
            needs, outs, scal, small, f"attn_fwd{j}", 1,
        )
        kept[j] = res[:3]
        return res[3:]

    def ffn_fwd(number, group, total, last):
        needs, outs = [], []
        for unit in group:
            pieces = [hidden[piece] for piece in unit]
            needs += [up_need(pieces, size, False), down_need(pieces, size, False)]
            outs += [((count, len(unit) * size), BF)] * 2
        first = total is None
        small = [low] + ([] if first else [total])
        if last:
            needs.append(need(cotangent))
            small += [hat, *gains]
            outs += [
                (wide, BF), hot(wide, F32), hot(wide, BF), hot((width, count), BF),
                hot((1, width), F32), hot((1, width), F32),
            ]
        else:
            outs.append(hot(wide, F32))
        res = call(
            functools.partial(ffn_fwd_kernel, len(group), first, last),
            needs, outs, scal, small, f"ffn_fwd{number}", 8 * work * size * len(group),
        )
        for index, unit in enumerate(group):
            for place, piece in enumerate(unit):
                acts[piece] = [(array, place) for array in res[index * 2 : index * 2 + 2]]
        return res[len(group) * 2 :]

    if fast:
        heads, hidden = {}, {}
        heads[0] = ("whole", qkv_weight, out_weight, 0)
        heads[1] = ("whole", *near[:2], 0)
        for r in range(4):
            hidden[0, r] = ("whole", up_weight, down_weight, table[r], width)

        def packed(r, both):
            hidden[2, r] = ("packed", both, both, width)
            other = over_core(both)
            hidden[3, r] = ("packed", other, other, width)

        (total,) = attn_fwd(0, None, False)
        total, *weights = sync([total], [up_weight, down_weight])
        needs = []
        for r in (0, 3):
            own = [("whole", *weights, table[r], width)]
            needs += [up_need(own, size), down_need(own, size)]
        packs = call(
            functools.partial(pack_kernel, size), needs,
            [((2, width, size), BF)] * 2, scal, [], "pack", 1,
        )
        ffn_a, ffn_d = over_y(packs[0]), over_y(packs[1])
        (head_a,) = tie([head_a], total, *near)
        head_b, head_c = over_x(head_a), over_z(head_a)
        other_a = over_core(head_a)
        (total,) = attn_fwd(1, total, False)
        tok_t = call(
            turn_kernel, [], [hot((width, count), BF)], scal, tie([tokens], total), "turn", 1
        )[0]
        head_b, head_c, head_d = tie([head_b, head_c, head_d], tok_t)
        pieces = [head_a, head_b, head_c, head_d]
        heads[2] = ("packed", pieces)
        heads[3] = ("packed", [other_a] + [over_core(p) for p in pieces[1:]])
        (total,) = attn_fwd(2, total, False)
        total, ffn_a = sync([total], [ffn_a])
        late = [over_core(w) for w in tie([up_weight, down_weight], *heads[3][1])]
        for r in range(4):
            hidden[1, r] = ("whole", *late, table[r], width)
        hat, inv, low, low_t = attn_fwd(3, total, True)
        ffn_b, ffn_c = over_x(ffn_a), over_z(ffn_a)
        packed(0, ffn_a)
        (total,) = ffn_fwd(0, [[(0, r) for r in range(4)]], None, False)
        (total,) = ffn_fwd(1, [[(2, 0), (3, 0)]], total, False)
        (total,) = ffn_fwd(2, [[(1, r) for r in range(4)]], total, False)
        for r, both in zip((1, 2, 3), tie([ffn_b, ffn_c, ffn_d], total)):
            packed(r, both)
        (total,) = ffn_fwd(3, [[(2, r) for r in (1, 2, 3)]], total, False)
        res = ffn_fwd(4, [[(3, r) for r in (1, 2, 3)]], total, True)
    else:
        heads = {j: ("whole", qkv_all, out_all, j) for j in range(pairs)}
        hidden = {
            (k // 4, k % 4): ("whole", up_all, down_all, ("block", k), width)
            for k in range(4 * pairs)
        }
        tok_t = call(
            turn_kernel, [], [hot((width, count), BF)], scal, [tokens], "turn", 1
        )[0]
        total = None
        for j in range(pairs):
            res = attn_fwd(j, total, j == pairs - 1)
            total = res[0]
        hat, inv, low, low_t = res
        total = None
        for j in range(pairs):
            res = ffn_fwd(j, [[(j, r) for r in range(4)]], total, j == pairs - 1)
            total = res[0]
    mixed, d_pre, d_ffn, d_ffn_t, g_gain2, g_shift2 = res

    order = [3, 1, 2, 0] if fast else list(range(pairs))
    ffn_g, attn_g, from_core = {}, {}, {}
    total = d_pre
    for j in order:
        last = j == order[-1]
        here = not fast or j % 2 == 0
        recv = from_core.get(j)
        pieces = [hidden[j, r] for r in range(4)]
        saved = [acts[j, r] for r in range(4)]
        needs = [saved_need([s[0] for s in saved], size)]
        if recv is not None:
            needs += [need(g, False) for g in recv]
        needs += [
            down_need(pieces, size),
            saved_need([s[1] for s in saved], size),
            up_need(pieces, size),
        ]
        small = [d_ffn, d_ffn_t, low_t, total]
        if here:
            outs = [((2, width, size), BF)] * 2 + [((4, half, size), BF)] * 2
        else:
            outs = [((2, 2, width, size), BF)] * 2
        grads = len(outs)
        if last:
            small += [hat, inv, gains[0]]
            outs = outs + [
                (wide, F32), hot(wide, BF), hot((width, count), BF),
                hot((1, width), F32), hot((1, width), F32),
            ]
        else:
            outs = outs + [hot(wide, F32)]
        res = call(
            functools.partial(ffn_bwd_kernel, here, recv is not None, last, size),
            needs, outs, scal, small, f"ffn_bwd{j}", 1,
        )
        ffn_g[j], total = res[:grads], res[grads]
        if not here:
            from_core[j - 1] = [over_core(g) for g in res[:grads]]
        if fast and j == 2:
            down_y = [over_y(g) for g in res[:2]]
            far_x = over_x(res[3])
    d_pre_one, d_att, d_att_t, g_gain1, g_shift1 = res[grads:]

    norm_grads = join([g_gain1, g_shift1, g_gain2, g_shift2])

    def flip(value):
        return join([value[1:], value[:1]])

    def turn_halves(value):
        return join([value[2:], value[:2]])

    def flip_pairs(value):
        return join([value[1:2], value[:1], value[3:], value[2:3]])

    def attn_bwd(j, total):
        here = not fast or j % 2 == 0
        recv = from_core.get(("attn", j))
        needs = [need(kept[j][0]), need(kept[j][2]), *attn_needs(heads[j]), need(kept[j][1])]
        if recv is not None:
            needs += [need(g) for g in recv]
        needs.append(need(total))
        each = 4 * LANE
        if here:
            outs = [((2, half, each), BF), ((half, each), BF), ((half, each), BF)]
        else:
            outs = [((width, each), BF)] * 2
        res = call(
            functools.partial(attn_bwd_kernel, heads[j][0], here, recv is not None),
            needs, outs + [(wide, F32)],
            scal, [seg_col, seg, d_att, d_att_t, tok_t], f"attn_bwd{j}", 1,
        )
        attn_g[j] = res[:-1]
        if not here:
            from_core["attn", j - 1] = [over_core(g) for g in res[:-1]]
        return res[-1]

    total = d_pre_one
    if fast:
        near_x = over_x(ffn_g[0][3])
        rest, front = slice(half, None), slice(0, half)

        def down_sum(u, rows):
            return add(ffn_g[0][u][:, rows], down_y[u][:, rows])

        total = attn_bwd(3, total)

        total, down_y[0], far_x = sync([total], [down_y[0], far_x])
        far = add(ffn_g[2][2], flip_pairs(far_x))
        first_z = over_z(
            join([down_sum(0, rest).reshape(4, quarter, size), far[:, quarter:]])
        )
        total = attn_bwd(1, total)
        total = attn_bwd(2, total)

        total, first_z, down_y[1], near_x = sync([total], [first_z, down_y[1], near_x])
        near = add(ffn_g[0][2], flip_pairs(near_x))
        second_z = over_z(
            join([down_sum(1, rest).reshape(4, quarter, size), near[:, quarter:]])
        )
        up_y = over_y(add(far[:, :quarter], turn_halves(first_z[4:])))
        vo_x = over_x(attn_g[2][2])
        qk_y = over_y(attn_g[2][0])
        total = attn_bwd(0, total)
        token_grad = total

        def last_sum(value, got):
            return value[..., :eighth, :].astype(F32) + got.astype(F32)

        vo_near_x = over_x(attn_g[0][2])
        vo_lo, vo_x = sync([attn_g[0][1]], [vo_x])
        vo_y = over_y(add(attn_g[2][1], vo_x))
        qk_near, qk_y = sync([attn_g[0][0]], [qk_y])
        qk_x = over_x(add(qk_near[1], qk_y[1]))
        qk_y, second_z = sync([qk_y], [second_z])
        got = [z[:4].reshape(2, half, size) for z in (first_z, second_z)]
        down = join([add(down_sum(u, front), got[1 - u]) for u in range(2)])
        down_x = over_x(down[:, quarter:])
        norm_next = over_core(norm_grads)
        down, vo_near_x, up_y, norm_next = sync([down], [vo_near_x, up_y, norm_next])
        up = add(near[:, :quarter], turn_halves(second_z[4:]), up_y)
        up_got = swap(up[:, eighth:], "seq", 4)
        norm_grads = norm_grads + norm_next
        norm_next = over_y(norm_grads)
        up, vo_y, norm_next = sync([up], [vo_y, norm_next])
        vo = add(vo_lo, vo_near_x, vo_y)
        vo_z = over_z(vo[quarter:])
        norm_grads = norm_grads + norm_next
        norm_next = over_x(norm_grads)
        vo, qk_x = sync([vo], [qk_x])
        qk = add(qk_near[0], qk_y[0], qk_x)
        qk_z = over_z(qk[quarter:])
        qk, down_x, norm_next = sync([qk], [down_x, norm_next])
        down = add(down[:, :quarter], flip_pairs(down_x))
        down_got = swap(down[:, eighth:], "seq", 4)
        norm_grads = norm_grads + norm_next
        norm_next = over_z(norm_grads)
        down, vo_z = sync([down], [vo_z])
        vo = add(vo[:quarter], vo_z)
        vo_got = swap(vo[eighth:], "seq", 4)
        vo, qk_z, norm_next = sync([vo], [qk_z, norm_next])
        qk = add(qk[:quarter], qk_z)
        qk_got = swap(qk[eighth:], "seq", 4)
        norm_grads = norm_grads + norm_next
        norm_grads = norm_grads + swap(norm_grads, "seq", 4)
        qk, up_got, down_got = sync([qk], [up_got, down_got])
        down, up = last_sum(down, down_got), last_sum(up, up_got)
        vo, qk = last_sum(vo, vo_got), last_sum(qk, qk_got)
        share = width // (seq * tp)
        norm_grads = lax.dynamic_slice_in_dim(
            norm_grads, (me_seq * tp + me_tp) * share, share, axis=1
        )

        def ordered(value):
            value = jnp.where(bit_x == 0, value, flip_pairs(value))
            value = jnp.where(bit_z == 0, value, turn_halves(value))
            return join([value[r] for r in range(4)], 1)

        down_grad = ordered(down).T
        up_grad = ordered(up)
        qkv_grad = jnp.stack([qk[:, : 2 * LANE], qk[:, 2 * LANE :], vo[:, : 2 * LANE]])
        out_grad = vo[:, 2 * LANE :].T
    else:
        for j in order:
            total = attn_bwd(j, total)
        token_grad = total
        norm_grads = lax.psum_scatter(norm_grads, ("seq", "tp"), scatter_dimension=1, tiled=True)

        def scattered(value, tp_dim, seq_dim):
            value = lax.psum_scatter(value, "tp", scatter_dimension=tp_dim, tiled=True)
            value = lax.psum_scatter(value, "seq", scatter_dimension=seq_dim, tiled=True)
            return value.astype(F32)

        def rows_of(low_part, high_part):
            parts = [
                part[..., k * quarter : (k + 1) * quarter, :]
                for k in range(2)
                for part in (low_part, high_part)
            ]
            return join(parts, -2)

        down = join([ffn_g[j][u][i] for j in range(pairs) for u in range(2) for i in range(2)], 1)
        up = join(
            [rows_of(ffn_g[j][2][r], ffn_g[j][3][r]) for j in range(pairs) for r in range(4)], 1
        )
        qk = [rows_of(attn_g[j][0][0], attn_g[j][0][1]) for j in range(pairs)]
        vo = [rows_of(attn_g[j][1], attn_g[j][2]) for j in range(pairs)]
        down_grad = scattered(down, 1, 0).T
        up_grad = scattered(up, 1, 0)
        qkv_grad = jnp.stack(
            [
                join([g[:, : 2 * LANE] for g in qk], 1),
                join([g[:, 2 * LANE :] for g in qk], 1),
                join([g[:, : 2 * LANE] for g in vo], 1),
            ]
        )
        qkv_grad = scattered(qkv_grad, 2, 1)
        out_grad = scattered(join([g[:, 2 * LANE :] for g in vo], 1), 1, 0).T
    return (mixed, token_grad, qkv_grad, out_grad, up_grad, down_grad, norm_grads)


def solution(mesh):
    return jax.shard_map(
        body,
        mesh=mesh,
        in_specs=(
            P(("seq", "tp"), None),
            P("seq", None),
            P(None, None, "tp"),
            P("tp", None),
            P(None, "tp"),
            P("tp", None),
            P(),
            P(),
            P(),
            P(),
            P(("seq", "tp"), None),
        ),
        out_specs=(
            P(("seq", "tp"), None),
            P(("seq", "tp"), None),
            P(None, "seq", "tp"),
            P("tp", "seq"),
            P("seq", "tp"),
            P("tp", "seq"),
            P(None, ("seq", "tp")),
        ),
        check_vma=False,
    )
```

```python
import functools

import jax
import jax.numpy as jnp
from jax import lax
from jax.experimental import pallas as pl
from jax.experimental.pallas import tpu as pltpu
from jax.sharding import PartitionSpec as P

HDIM = 64
LANE = 128
BF = jnp.bfloat16
F32 = jnp.float32
SCALE = HDIM ** (-0.5)
MASKED = -1000000000.0
VMEM_MIB = (("attn_fwd", 16), ("ffn_fwd", 20), ("ffn_bwd", 28), ("attn_bwd", 18), ("pack", 12))


def dot(left, right):
    return jnp.dot(left, right, preferred_element_type=F32)


def dot_nt(left, right):
    return lax.dot_general(left, right, (((1,), (1,)), ((), ())), preferred_element_type=F32)


def everything(ref, scal):
    return ref


class Need:
    def __init__(self, shape, dtype, *parts, pinned=True):
        self.shape, self.dtype, self.parts, self.pinned = tuple(shape), dtype, parts, pinned


def need(array, pinned=True):
    return Need(array.shape, array.dtype, (array, everything, everything), pinned=pinned)


class Loads:
    def __init__(self, needs, refs, bufs, sems, scal):
        self.bufs, self.copies, self.next = bufs, [], 0
        at = 0
        for item, buf in zip(needs, bufs):
            mine = []
            for index, source, target in item.parts:
                copy = pltpu.make_async_copy(
                    source(refs[index], scal), target(buf, scal), sems.at[at]
                )
                copy.start()
                mine.append(copy)
                at += 1
            self.copies.append(mine)

    def take(self):
        self.next += 1
        return self.next - 1

    def get(self, slot):
        for copy in self.copies[slot]:
            copy.wait()
        self.copies[slot] = []
        return self.bufs[slot]

    def pop(self):
        return self.get(self.take())

    def finish(self):
        for slot in range(len(self.copies)):
            self.get(slot)


class Stores:
    def __init__(self, refs, bufs, sems):
        self.refs, self.sems, self.copies = refs, sems, []
        self.bufs = [ref if buf is None else buf for ref, buf in zip(refs, bufs)]
        self.direct = [buf is None for buf in bufs]
        self.next = 0

    def part(self, slot, value, *where):
        self.bufs[slot][where] = value

    def send(self, slot, *where):
        if self.direct[slot]:
            return
        source, target = self.bufs[slot], self.refs[slot]
        if where:
            source, target = source.at[where], target.at[where]
        copy = pltpu.make_async_copy(source, target, self.sems.at[self.next])
        self.next += 1
        copy.start()
        self.copies.append(copy)

    def put(self, slot, value):
        self.bufs[slot][...] = value
        self.send(slot)

    def finish(self):
        for copy in self.copies:
            copy.wait()


def hot(shape, dtype):
    return (shape, dtype, True)


def vmem_of(name):
    for start, size in VMEM_MIB:
        if name.startswith(start):
            return size
    return 16


def call(kernel, needs, outs, scal, small, name, flops, sends=None):
    arrays, parts, pinned = [], [], []
    for item in needs:
        fixed = []
        for array, source, target in item.parts:
            index = next((i for i, a in enumerate(arrays) if a is array), None)
            if index is None:
                index = len(arrays)
                arrays.append(array)
                pinned.append(item.pinned)
            fixed.append((index, source, target))
        parts.append(Need(item.shape, item.dtype, *fixed))
    copies = max(1, sum(len(item.parts) for item in parts))
    sends = max(1, len(outs) if sends is None else sends)
    here = [len(out) == 3 for out in outs]

    def run(*refs):
        refs = list(refs)
        scal_ref = refs.pop(0)
        small_refs = [refs.pop(0) for _ in small]
        in_refs = [refs.pop(0) for _ in arrays]
        out_refs = [refs.pop(0) for _ in outs]
        in_bufs = [refs.pop(0) for _ in parts]
        out_bufs = [None if stays else refs.pop(0) for stays in here]
        in_sems, out_sems = refs
        loads = Loads(parts, in_refs, in_bufs, in_sems, scal_ref)
        stores = Stores(out_refs, out_bufs, out_sems)
        kernel(scal_ref, small_refs, loads, stores)
        loads.finish()
        stores.finish()

    return pl.pallas_call(
        run,
        out_shape=[
            jax.ShapeDtypeStruct(out[0], out[1]) if stays else pltpu.HBM(out[0], out[1])
            for out, stays in zip(outs, here)
        ],
        in_specs=[pl.BlockSpec(memory_space=pltpu.SMEM)]
        + [pl.BlockSpec(memory_space=pltpu.VMEM)] * len(small)
        + [pl.BlockSpec(memory_space=pltpu.HBM if p else pl.ANY) for p in pinned],
        out_specs=[
            pl.BlockSpec(memory_space=pltpu.VMEM if stays else pltpu.HBM) for stays in here
        ],
        scratch_shapes=[pltpu.VMEM(item.shape, item.dtype) for item in parts]
        + [pltpu.VMEM(out[0], out[1]) for out, stays in zip(outs, here) if not stays]
        + [pltpu.SemaphoreType.DMA((copies,)), pltpu.SemaphoreType.DMA((sends,))],
        compiler_params=pltpu.CompilerParams(vmem_limit_bytes=vmem_of(name) * 1024 * 1024),
        cost_estimate=pl.CostEstimate(flops=flops, bytes_accessed=0, transcendentals=0),
        name=name,
    )(
        scal,
        *small,
        *[
            pltpu.with_memory_space_constraint(a, pltpu.HBM) if p else a
            for a, p in zip(arrays, pinned)
        ],
    )


def store_turned(scal, buf, values):
    for block in range(values.shape[1] // LANE):
        start = pl.multiple_of(scal[block] * LANE, LANE)
        buf[pl.ds(start, LANE), :] = values[:, block * LANE : (block + 1) * LANE].T


def block_of(scal, place):
    kind, value = place
    return scal[value] if kind == "table" else value


def columns(place, size, *front):
    def take(ref, scal):
        start = pl.multiple_of(block_of(scal, place) * size, size)
        return ref.at[(*front, slice(None), pl.ds(start, size))]

    return take


def lines(place, size):
    def take(ref, scal):
        start = pl.multiple_of(block_of(scal, place) * size, size)
        return ref.at[pl.ds(start, size), :]

    return take


def lanes_at(start, size):
    return lambda ref, scal: ref.at[:, pl.ds(start, size)]


def lines_at(start, size):
    return lambda ref, scal: ref.at[pl.ds(start, size), :]


def slot_at(*where):
    return lambda ref, scal: ref.at[where]


def stacked_at(index, size):
    def take(ref, scal):
        ref = ref if len(ref.shape) == 2 else ref.at[1]
        return ref.at[pl.ds(index * size, size), :]

    return take


def block_at(row, column, size):
    return lambda ref, scal: ref.at[pl.ds(row * size, size), pl.ds(column * size, size)]


def first_of(ref, scal):
    return ref if len(ref.shape) == 2 else ref.at[0]


def part_of(place):
    def find(scal):
        quarter = block_of(scal, place)
        return quarter // 2, lax.rem(quarter, 2)

    return find


def matrix_at(place, which):
    def take(ref, scal):
        half, pair = part_of(place)(scal)
        index = 1 if which else 2 * pair
        return ref.at[index, :, pl.ds(pl.multiple_of(half * LANE, LANE), LANE)]

    return take


def out_rows_at(place):
    def take(ref, scal):
        half, _ = part_of(place)(scal)
        return ref.at[pl.ds(pl.multiple_of(half * LANE, LANE), LANE), :]

    return take


def piece_lanes(place, which, block, rows):
    def take(buf, scal):
        half, pair = part_of(place)(scal)
        start = pair * 4 * LANE + half * LANE + which * 2 * LANE
        return buf.at[pl.ds(block * rows, rows), pl.ds(pl.multiple_of(start, LANE), LANE)]

    return take


def attn_needs(block, pinned=True):
    if block[0] == "packed":
        pieces = block[1]
        parts = []
        for r, piece in enumerate(pieces):
            for half, array in enumerate(piece):
                parts += [
                    (
                        array,
                        lanes_at(which * LANE, LANE),
                        piece_lanes(("table", 8 + r), which, half, array.shape[0]),
                    )
                    for which in range(2)
                ]
        return [Need((pieces[0][0].shape[0], 8 * LANE), BF, *parts, pinned=pinned)]
    _, qkv, out, index = block
    depth, width = qkv.shape[1], out.shape[1]
    place = ("block", index)
    return [
        Need(
            (depth, 6 * LANE), BF,
            *[
                (qkv, columns(place, 2 * LANE, i), lanes_at(2 * i * LANE, 2 * LANE))
                for i in range(3)
            ],
        ),
        Need((2 * LANE, width), BF, (out, lines(place, 2 * LANE), everything)),
    ]


def up_need(pieces, size, pinned=True):
    parts = []
    for number, piece in enumerate(pieces):
        target = lanes_at(number * size, size)
        if piece[0] == "packed":
            parts.append((piece[1], first_of, target))
        else:
            parts.append((piece[1], columns(piece[3], size), target))
    return Need((pieces[0][-1], len(pieces) * size), BF, *parts, pinned=pinned)


def down_need(pieces, size, pinned=True):
    parts = []
    for number, piece in enumerate(pieces):
        width = piece[-1]
        if piece[0] == "packed":
            for index in range(width // size):
                parts.append(
                    (piece[2], stacked_at(index, size), block_at(number, index, size))
                )
        else:
            parts.append((piece[2], lines(piece[3], size), lines_at(number * size, size)))
    return Need((len(pieces) * size, pieces[0][-1]), BF, *parts, pinned=pinned)


def saved_need(pieces, size):
    parts = [
        (array, lanes_at(index * size, size), lanes_at(number * size, size))
        for number, (array, index) in enumerate(pieces)
    ]
    return Need((pieces[0][0].shape[0], len(pieces) * size), BF, *parts)


def mean_of(values):
    return jnp.mean(values, axis=-1, keepdims=True)


def bias_of(seg_col, seg_row):
    return jnp.where(seg_col == seg_row, 0.0, MASKED)


def cut_kernel(places, scal, small, loads, stores):
    for slot, place in enumerate(places):
        first, second, out = loads.pop(), loads.pop(), loads.pop()
        _, pair = part_of(place)(scal)
        stores.part(slot, first[...], slice(None), slice(0, LANE))

        @pl.when(pair == 0)
        def _():
            stores.part(slot, second[...], slice(None), slice(LANE, 2 * LANE))

        @pl.when(pair == 1)
        def _():
            stores.part(slot, out[...].T, slice(None), slice(LANE, 2 * LANE))

        stores.send(slot)


def pack_kernel(size, scal, small, loads, stores):
    for slot in range(2):
        up, down = loads.pop(), loads.pop()
        stores.part(slot, up[...], 0)
        for index in range(down.shape[1] // size):
            block = down[:, index * size : (index + 1) * size]
            stores.part(slot, block, 1, pl.ds(index * size, size))
        stores.send(slot)


def turn_kernel(scal, small, loads, stores):
    store_turned(scal, stores.bufs[0], small[0][...])
    stores.send(0)


def head_parts(qkv, unit):
    query, key, value = (
        qkv[:, (2 * i + unit) * LANE : (2 * i + unit + 1) * LANE] for i in range(3)
    )
    return query * jnp.asarray(SCALE, BF), key, value


def stacked(pair, lane):
    zero = jnp.zeros_like(pair)
    return jnp.concatenate(
        [jnp.where(lane < HDIM, pair, zero), jnp.where(lane >= HDIM, pair, zero)], axis=0
    )


def attn_fwd_kernel(kind, first, last, scal, small, loads, stores):
    col_ref, row_ref, tokens_ref = small[:3]
    tokens = tokens_ref[...]
    bias = bias_of(col_ref[...], row_ref[...])
    lane = lax.broadcasted_iota(jnp.int32, (1, LANE), 1)
    length = tokens.shape[0]
    weight = loads.pop()
    qkv = dot(tokens, weight[:, : 6 * LANE]).astype(BF)
    stores.put(0, qkv)
    contexts = []
    for unit in range(2):
        query, key, value = head_parts(qkv, unit)
        scores = dot_nt(stacked(key, lane), query)
        probs = []
        for head in range(2):
            mine = scores[head * length : (head + 1) * length] + bias
            peak = jnp.max(mine, axis=0, keepdims=True)
            raw = jnp.exp(mine - peak)
            summed = jnp.sum(raw, axis=0, keepdims=True)
            stores.part(2, peak + jnp.log(summed), pl.ds(2 * unit + head, 1), slice(None))
            probs.append((raw * (1.0 / summed)).astype(BF))
        context = dot(stacked(value, lane).T, jnp.concatenate(probs, axis=0))
        contexts.append(context.astype(BF).T)
    stores.send(2)
    both = jnp.concatenate(contexts, axis=1)
    stores.put(1, both)
    if kind == "whole":
        total = dot(both, loads.pop()[...])
    else:
        total = dot_nt(both, weight[:, 6 * LANE :])
    if not first:
        total = total + small[3][...]
    at = 3
    if not last:
        stores.put(at, total)
        return
    gain_ref, shift_ref = small[-2:]
    pre = tokens.astype(F32) + total
    center = pre - mean_of(pre)
    inv = lax.rsqrt(mean_of(center * center) + 1e-12)
    hat = center * inv
    low = (hat * gain_ref[...] + shift_ref[...]).astype(BF)
    stores.put(at + 2, low)
    stores.put(at, hat)
    stores.put(at + 1, jnp.broadcast_to(inv, (hat.shape[0], LANE)))
    store_turned(scal, stores.bufs[at + 3], low)
    stores.send(at + 3)


def ffn_fwd_kernel(units, first, last, scal, small, loads, stores):
    low = small[0][...]
    total = None
    for number in range(units):
        up = dot(low, loads.pop()[...])
        phi_big = 0.5 + 0.5 * lax.erf(up * (0.5 ** 0.5))
        phi_small = jnp.exp(up * up * -0.5) * 0.3989422804014327
        act = (up * phi_big).astype(BF)
        stores.put(number * 2, act)
        stores.put(number * 2 + 1, (phi_big + up * phi_small).astype(BF))
        part = dot(act, loads.pop()[...])
        total = part if total is None else total + part
    if not first:
        total = total + small[1][...]
    at = units * 2
    if not last:
        stores.put(at, total)
        return
    hat_ref, gain1_ref, shift1_ref, gain2_ref, shift2_ref = small[-5:]
    gain2 = gain2_ref[...]
    pre = hat_ref[...] * gain1_ref[...] + shift1_ref[...] + total
    center = pre - mean_of(pre)
    inv = lax.rsqrt(mean_of(center * center) + 1e-12)
    hat = center * inv
    cot = loads.pop()[...].astype(F32)
    scaled = cot * gain2
    dpre = (scaled - mean_of(scaled) - hat * mean_of(scaled * hat)) * inv
    dffn = dpre.astype(BF)
    stores.put(at + 2, dffn)
    stores.put(at + 1, dpre)
    store_turned(scal, stores.bufs[at + 3], dffn)
    stores.send(at + 3)
    stores.put(at, (hat * gain2 + shift2_ref[...]).astype(BF))
    stores.put(at + 4, jnp.sum(cot * hat, axis=0, keepdims=True))
    stores.put(at + 5, jnp.sum(cot, axis=0, keepdims=True))


def split_rows(stores, slot, where, value, inside=False):
    step = value.shape[0] // 4
    for number in range(4):
        rows = pl.ds(number // 2 * step, step)
        piece = value[number * step : (number + 1) * step]
        if inside:
            stores.part(slot, piece, number % 2, rows)
        else:
            stores.part(slot + number % 2, piece, *where, rows)


def ffn_bwd_kernel(near, has_recv, last, size, scal, small, loads, stores):
    dffn_ref, dffn_t_ref, low_t_ref, acc_ref = small[:4]
    down = dot(dffn_t_ref[...], loads.pop()[...])
    got = [loads.pop() for _ in range(2)] if has_recv else None
    for r in range(4):
        value = down[:, r * size : (r + 1) * size]
        if has_recv:
            value = value + got[r // 2][0, r % 2].astype(F32)
        stores.part(r // 2, value.astype(BF), *((r % 2,) if near else (0, r % 2)))
    if near:
        stores.send(0)
        stores.send(1)
    wd, slope = loads.pop(), loads.pop()
    d_up = (dot_nt(dffn_ref[...], wd[...]) * slope[...].astype(F32)).astype(BF)
    up = dot(low_t_ref[...], d_up)
    for r in range(4):
        value = up[:, r * size : (r + 1) * size]
        if has_recv:
            value = value + got[r // 2][1, r % 2].astype(F32)
        if near:
            split_rows(stores, 2, (r,), value.astype(BF))
        else:
            stores.part(r // 2, value.astype(BF), 1, r % 2)
    if near:
        stores.send(2)
        stores.send(3)
    else:
        stores.send(0)
        stores.send(1)
    total = acc_ref[...] + dot_nt(d_up, loads.pop()[...])
    at = 4 if near else 2
    if not last:
        stores.put(at, total)
        return
    hat_ref, inv_ref, gain_ref = small[4:]
    hat = hat_ref[...]
    scaled = total * gain_ref[...]
    inv = inv_ref[:, :1]
    dpre = (scaled - mean_of(scaled) - hat * mean_of(scaled * hat)) * inv
    datt = dpre.astype(BF)
    stores.put(at + 1, datt)
    stores.put(at, dpre)
    store_turned(scal, stores.bufs[at + 2], datt)
    stores.send(at + 2)
    stores.put(at + 3, jnp.sum(total * hat, axis=0, keepdims=True))
    stores.put(at + 4, jnp.sum(total, axis=0, keepdims=True))


def attn_bwd_kernel(kind, near, has_recv, scal, small, loads, stores):
    col_ref, row_ref, datt_ref, datt_t_ref, tok_t_ref = small
    bias = bias_of(col_ref[...], row_ref[...])
    lane = lax.broadcasted_iota(jnp.int32, (1, LANE), 1)
    qkv, lse = loads.pop(), loads.pop()
    pairs, keys, probs = [], [], []
    length = bias.shape[0]
    for unit in range(2):
        query, key, value = head_parts(qkv, unit)
        keys.append(stacked(key, lane))
        scores = dot_nt(keys[unit], query)
        pairs.append((query, value))
        for head in range(2):
            row = 2 * unit + head
            mine = scores[head * length : (head + 1) * length] + bias
            probs.append(jnp.exp(mine - lse[row : row + 1, :]))
    weight = loads.pop()
    if kind == "whole":
        dctx_all = dot_nt(datt_ref[...], loads.pop()[...]).astype(BF)
    else:
        dctx_all = dot(datt_ref[...], weight[:, 6 * LANE :]).astype(BF)
    grads = [[], [], []]

    def chosen(value):
        return jnp.where(lane < HDIM, value[:length], value[length:]).astype(BF)

    for unit in range(2):
        dctx = dctx_all[:, unit * LANE : (unit + 1) * LANE]
        query, value = pairs[unit]
        d_probs = dot_nt(stacked(value, lane), dctx)
        d_scores = []
        for head in range(2):
            prob = probs[2 * unit + head]
            d_prob = d_probs[head * length : (head + 1) * length]
            inner = jnp.sum(prob * d_prob, axis=0, keepdims=True)
            d_scores.append((prob * (d_prob - inner)).astype(BF))
        d_scores = jnp.concatenate(d_scores, axis=0)
        low_probs = jnp.concatenate([p.astype(BF) for p in probs[2 * unit : 2 * unit + 2]], axis=0)
        grads[0].append((dot(keys[unit].T, d_scores) * SCALE).astype(BF).T)
        grads[1].append(chosen(dot(d_scores, query)))
        grads[2].append(chosen(dot(low_probs, dctx)))
    tok_t = tok_t_ref[...]
    both = jnp.concatenate(grads[0] + grads[1] + grads[2], axis=1)
    ctx = loads.pop()
    qk = dot(tok_t, both[:, : 4 * LANE])
    if has_recv:
        qk = qk + loads.pop()[...].astype(F32)
    vo = jnp.concatenate(
        [dot(tok_t, both[:, 4 * LANE :]), dot(datt_t_ref[...], ctx[...])], axis=1
    )
    if has_recv:
        vo = vo + loads.pop()[...].astype(F32)
    if near:
        split_rows(stores, 0, (0,), qk.astype(BF), True)
        stores.send(0)
        split_rows(stores, 1, (), vo.astype(BF))
        stores.send(1)
        stores.send(2)
    else:
        stores.put(0, qk.astype(BF))
        stores.put(1, vo.astype(BF))
    stores.put(3 if near else 2, loads.pop()[...] + dot_nt(both, weight[:, : 6 * LANE]))


def swap(value, axis, bit):
    count = lax.axis_size(axis)
    return lax.ppermute(value, axis, [(i, i ^ bit) for i in range(count)])


def add(*values):
    total = values[0].astype(F32)
    for value in values[1:]:
        total = total + value.astype(F32)
    return total.astype(BF)


def tie(values, *after):
    return list(lax.optimization_barrier((tuple(values), after))[0])


def sync(values, arrived):
    return lax.optimization_barrier((*values, *arrived))


def join(values, axis=0):
    return jnp.concatenate(values, axis=axis)


def body(
    tokens,
    segment_ids,
    qkv_weight,
    out_weight,
    up_weight,
    down_weight,
    gain_attn,
    shift_attn,
    gain_ffn,
    shift_ffn,
    cotangent,
):
    count, width = tokens.shape
    seq, tp = lax.axis_size("seq"), lax.axis_size("tp")
    me_seq, me_tp = lax.axis_index("seq"), lax.axis_index("tp")
    blocks = width // LANE
    pairs = blocks // 2
    size = up_weight.shape[1] * tp // (4 * pairs)
    fast = seq == blocks and seq == 8 and tp == 4 and qkv_weight.shape[2] == 2 * LANE
    seg = lax.dynamic_slice_in_dim(segment_ids, me_tp, 1, axis=0)
    seg_col = seg.reshape(count, 1)
    gains = [g.reshape(1, width) for g in (gain_attn, shift_attn, gain_ffn, shift_ffn)]
    absolute = jnp.arange(blocks, dtype=jnp.int32)
    half, quarter, eighth = width // 2, width // 4, width // 8
    wide = (count, width)
    work = 2 * count * width
    bit_x, bit_z = me_seq & 1, (me_seq >> 1) & 1

    def over_x(value):
        return swap(value, "seq", 1)

    def over_z(value):
        return swap(value, "seq", 2)

    def over_y(value):
        return swap(value, "tp", 2)

    def over_core(value):
        return swap(value, "tp", 1)

    if fast:
        rel = absolute ^ me_seq
        pos = ((rel >> 1) & 1) * 4 + (rel & 1) * 2 + (rel >> 2)
        mine = me_seq & 3
        scal = jnp.stack(
            [pos[i] for i in range(blocks)] + [mine ^ r for r in range(4)]
        ).astype(jnp.int32)
        table = [("table", 8 + r) for r in range(4)]
        needs = [
            Need((width, LANE), BF, (qkv_weight, matrix_at(table[0], which), everything))
            for which in range(2)
        ]
        needs.append(Need((LANE, width), BF, (out_weight, out_rows_at(table[0]), everything)))
        cuts = call(
            functools.partial(cut_kernel, [table[0]]), needs,
            [((width, 2 * LANE), BF)], scal, [], "cut", 1,
        )
        head_a = over_y(cuts[0])
        weights = tie([up_weight, down_weight], cuts[0])
        needs = []
        for r in (0, 3):
            own = [("whole", *weights, table[r], width)]
            needs += [up_need(own, size), down_need(own, size)]
        packs = call(
            functools.partial(pack_kernel, size), needs,
            [((2, width, size), BF)] * 2, scal, [], "pack", 1,
        )
        ffn_a, ffn_d = over_y(packs[0]), over_y(packs[1])
        (early,) = tie([tokens], packs[1])
        near = [over_core(w) for w in (qkv_weight, out_weight, up_weight, down_weight)]
    else:
        scal = jnp.concatenate([absolute, jnp.zeros((4,), jnp.int32)])
        qkv_all = lax.all_gather(qkv_weight, "tp", axis=2, tiled=True)
        out_all = lax.all_gather(out_weight, "tp", axis=0, tiled=True)
        up_all = lax.all_gather(up_weight, "tp", axis=1, tiled=True)
        down_all = lax.all_gather(down_weight, "tp", axis=0, tiled=True)

    kept, acts = {}, {}
    early = early if fast else tokens

    def attn_fwd(j, total, last):
        needs = attn_needs(heads[j], False)
        outs = [((count, 6 * LANE), BF), ((count, 2 * LANE), BF), ((8, count), F32)]
        if last:
            outs += [
                hot(wide, F32), hot((count, LANE), F32), hot(wide, BF), hot((width, count), BF),
            ]
        else:
            outs.append(hot(wide, F32))
        first = total is None
        small = [seg_col, seg, early] + ([] if first else [total]) + (gains[:2] if last else [])
        res = call(
            functools.partial(attn_fwd_kernel, heads[j][0], first, last),
            needs, outs, scal, small, f"attn_fwd{j}", 1,
        )
        kept[j] = res[:3]
        return res[3:]

    def ffn_fwd(number, group, total, last):
        needs, outs = [], []
        for unit in group:
            pieces = [hidden[piece] for piece in unit]
            needs += [up_need(pieces, size, False), down_need(pieces, size, False)]
            outs += [((count, len(unit) * size), BF)] * 2
        first = total is None
        small = [low] + ([] if first else [total])
        if last:
            needs.append(need(cotangent))
            small += [hat, *gains]
            outs += [
                (wide, BF), hot(wide, F32), hot(wide, BF), hot((width, count), BF),
                hot((1, width), F32), hot((1, width), F32),
            ]
        else:
            outs.append(hot(wide, F32))
        res = call(
            functools.partial(ffn_fwd_kernel, len(group), first, last),
            needs, outs, scal, small, f"ffn_fwd{number}", 8 * work * size * len(group),
        )
        for index, unit in enumerate(group):
            for place, piece in enumerate(unit):
                acts[piece] = [(array, place) for array in res[index * 2 : index * 2 + 2]]
        return res[len(group) * 2 :]

    if fast:
        heads, hidden = {}, {}
        heads[0] = ("whole", qkv_weight, out_weight, 0)
        heads[1] = ("whole", *near[:2], 0)
        for r in range(4):
            hidden[0, r] = ("whole", up_weight, down_weight, table[r], width)
            hidden[1, r] = ("whole", *near[2:], table[r], width)

        def packed(r, both):
            hidden[2, r] = ("packed", both, both, width)
            other = over_core(both)
            hidden[3, r] = ("packed", other, other, width)

        (total,) = attn_fwd(0, None, False)
        (head_a,) = tie([head_a], total, *near)
        head_b, head_c = over_x(head_a), over_z(head_a)
        other_a = over_core(head_a)
        (total,) = attn_fwd(1, total, False)
        tok_t = call(
            turn_kernel, [], [hot((width, count), BF)], scal, tie([tokens], total), "turn", 1
        )[0]
        head_b, head_c = tie([head_b, head_c], tok_t)
        head_d = [over_x(head_c[:half]), over_z(head_b[half:])]
        pieces = [[head_a], [head_b], [head_c], head_d]
        heads[2] = ("packed", pieces)
        others = [[over_core(g) for g in p] for p in pieces[1:]]
        heads[3] = ("packed", [[other_a], *others])
        total, ffn_a = sync([total], [ffn_a])
        (total,) = attn_fwd(2, total, False)
        hat, inv, low, low_t = attn_fwd(3, total, True)
        ffn_b, ffn_c = over_x(ffn_a), over_z(ffn_a)
        packed(0, ffn_a)
        (total,) = ffn_fwd(0, [[(0, r) for r in range(4)]], None, False)
        (total,) = ffn_fwd(1, [[(2, 0), (3, 0)]], total, False)
        (total,) = ffn_fwd(2, [[(1, r) for r in range(4)]], total, False)
        for r, both in zip((1, 2, 3), tie([ffn_b, ffn_c, ffn_d], total)):
            packed(r, both)
        (total,) = ffn_fwd(3, [[(2, r) for r in (1, 2, 3)]], total, False)
        res = ffn_fwd(4, [[(3, r) for r in (1, 2, 3)]], total, True)
    else:
        heads = {j: ("whole", qkv_all, out_all, j) for j in range(pairs)}
        hidden = {
            (k // 4, k % 4): ("whole", up_all, down_all, ("block", k), width)
            for k in range(4 * pairs)
        }
        tok_t = call(
            turn_kernel, [], [hot((width, count), BF)], scal, [tokens], "turn", 1
        )[0]
        total = None
        for j in range(pairs):
            res = attn_fwd(j, total, j == pairs - 1)
            total = res[0]
        hat, inv, low, low_t = res
        total = None
        for j in range(pairs):
            res = ffn_fwd(j, [[(j, r) for r in range(4)]], total, j == pairs - 1)
            total = res[0]
    mixed, d_pre, d_ffn, d_ffn_t, g_gain2, g_shift2 = res

    order = [3, 1, 2, 0] if fast else list(range(pairs))
    ffn_g, attn_g, from_core = {}, {}, {}
    total = d_pre
    for j in order:
        last = j == order[-1]
        here = not fast or j % 2 == 0
        recv = from_core.get(j)
        pieces = [hidden[j, r] for r in range(4)]
        saved = [acts[j, r] for r in range(4)]
        needs = [saved_need([s[0] for s in saved], size)]
        if recv is not None:
            needs += [need(g, False) for g in recv]
        needs += [
            down_need(pieces, size),
            saved_need([s[1] for s in saved], size),
            up_need(pieces, size),
        ]
        small = [d_ffn, d_ffn_t, low_t, total]
        if here:
            outs = [((2, width, size), BF)] * 2 + [((4, half, size), BF)] * 2
        else:
            outs = [((2, 2, width, size), BF)] * 2
        grads = len(outs)
        if last:
            small += [hat, inv, gains[0]]
            outs = outs + [
                (wide, F32), hot(wide, BF), hot((width, count), BF),
                hot((1, width), F32), hot((1, width), F32),
            ]
        else:
            outs = outs + [hot(wide, F32)]
        res = call(
            functools.partial(ffn_bwd_kernel, here, recv is not None, last, size),
            needs, outs, scal, small, f"ffn_bwd{j}", 1,
        )
        ffn_g[j], total = res[:grads], res[grads]
        if not here:
            from_core[j - 1] = [over_core(g) for g in res[:grads]]
        if fast and j == 2:
            down_y = [over_y(g) for g in res[:2]]
            far_x = over_x(res[3])
    d_pre_one, d_att, d_att_t, g_gain1, g_shift1 = res[grads:]

    norm_grads = join([g_gain1, g_shift1, g_gain2, g_shift2])

    def flip(value):
        return join([value[1:], value[:1]])

    def turn_halves(value):
        return join([value[2:], value[:2]])

    def flip_pairs(value):
        return join([value[1:2], value[:1], value[3:], value[2:3]])

    def attn_bwd(j, total):
        here = not fast or j % 2 == 0
        recv = from_core.get(("attn", j))
        needs = [need(kept[j][0]), need(kept[j][2]), *attn_needs(heads[j]), need(kept[j][1])]
        if recv is not None:
            needs += [need(g) for g in recv]
        needs.append(need(total))
        each = 4 * LANE
        if here:
            outs = [((2, half, each), BF), ((half, each), BF), ((half, each), BF)]
        else:
            outs = [((width, each), BF)] * 2
        res = call(
            functools.partial(attn_bwd_kernel, heads[j][0], here, recv is not None),
            needs, outs + [(wide, F32)],
            scal, [seg_col, seg, d_att, d_att_t, tok_t], f"attn_bwd{j}", 1,
        )
        attn_g[j] = res[:-1]
        if not here:
            from_core["attn", j - 1] = [over_core(g) for g in res[:-1]]
        return res[-1]

    total = d_pre_one
    if fast:
        near_x = over_x(ffn_g[0][3])
        rest, front = slice(half, None), slice(0, half)

        def down_sum(u, rows):
            return add(ffn_g[0][u][:, rows], down_y[u][:, rows])

        total = attn_bwd(3, total)

        total, down_y[0], far_x = sync([total], [down_y[0], far_x])
        far = add(ffn_g[2][2], flip_pairs(far_x))
        first_z = over_z(
            join([down_sum(0, rest).reshape(4, quarter, size), far[:, quarter:]])
        )
        total = attn_bwd(1, total)
        total = attn_bwd(2, total)

        total, first_z, down_y[1], near_x = sync([total], [first_z, down_y[1], near_x])
        near = add(ffn_g[0][2], flip_pairs(near_x))
        second_z = over_z(
            join([down_sum(1, rest).reshape(4, quarter, size), near[:, quarter:]])
        )
        up_y = over_y(add(far[:, :quarter], turn_halves(first_z[4:])))
        vo_x = over_x(attn_g[2][2])
        qk_y = over_y(attn_g[2][0])
        total = attn_bwd(0, total)
        token_grad = total

        def last_sum(value, got):
            return value[..., :eighth, :].astype(F32) + got.astype(F32)

        vo_near_x = over_x(attn_g[0][2])
        vo_lo, vo_x = sync([attn_g[0][1]], [vo_x])
        vo_y = over_y(add(attn_g[2][1], vo_x))
        qk_near, qk_y = sync([attn_g[0][0]], [qk_y])
        qk_x = over_x(add(qk_near[1], qk_y[1]))
        qk_y, second_z = sync([qk_y], [second_z])
        got = [z[:4].reshape(2, half, size) for z in (first_z, second_z)]
        down = join([add(down_sum(u, front), got[1 - u]) for u in range(2)])
        down_x = over_x(down[:, quarter:])
        norm_next = over_core(norm_grads)
        down, vo_near_x, up_y, norm_next = sync([down], [vo_near_x, up_y, norm_next])
        up = add(near[:, :quarter], turn_halves(second_z[4:]), up_y)
        up_got = swap(up[:, eighth:], "seq", 4)
        norm_grads = norm_grads + norm_next
        norm_next = over_y(norm_grads)
        up, vo_y, norm_next = sync([up], [vo_y, norm_next])
        vo = add(vo_lo, vo_near_x, vo_y)
        vo_z = over_z(vo[quarter:])
        norm_grads = norm_grads + norm_next
        norm_next = over_x(norm_grads)
        vo, qk_x = sync([vo], [qk_x])
        qk = add(qk_near[0], qk_y[0], qk_x)
        qk_z = over_z(qk[quarter:])
        qk, down_x, norm_next = sync([qk], [down_x, norm_next])
        down = add(down[:, :quarter], flip_pairs(down_x))
        down_got = swap(down[:, eighth:], "seq", 4)
        norm_grads = norm_grads + norm_next
        norm_next = over_z(norm_grads)
        down, vo_z = sync([down], [vo_z])
        vo = add(vo[:quarter], vo_z)
        vo_got = swap(vo[eighth:], "seq", 4)
        vo, qk_z, norm_next = sync([vo], [qk_z, norm_next])
        qk = add(qk[:quarter], qk_z)
        qk_got = swap(qk[eighth:], "seq", 4)
        norm_grads = norm_grads + norm_next
        norm_grads = norm_grads + swap(norm_grads, "seq", 4)
        qk, up_got, down_got = sync([qk], [up_got, down_got])
        down, up = last_sum(down, down_got), last_sum(up, up_got)
        vo, qk = last_sum(vo, vo_got), last_sum(qk, qk_got)
        share = width // (seq * tp)
        norm_grads = lax.dynamic_slice_in_dim(
            norm_grads, (me_seq * tp + me_tp) * share, share, axis=1
        )

        def ordered(value):
            value = jnp.where(bit_x == 0, value, flip_pairs(value))
            value = jnp.where(bit_z == 0, value, turn_halves(value))
            return join([value[r] for r in range(4)], 1)

        down_grad = ordered(down).T
        up_grad = ordered(up)
        qkv_grad = jnp.stack([qk[:, : 2 * LANE], qk[:, 2 * LANE :], vo[:, : 2 * LANE]])
        out_grad = vo[:, 2 * LANE :].T
    else:
        for j in order:
            total = attn_bwd(j, total)
        token_grad = total
        norm_grads = lax.psum_scatter(norm_grads, ("seq", "tp"), scatter_dimension=1, tiled=True)

        def scattered(value, tp_dim, seq_dim):
            value = lax.psum_scatter(value, "tp", scatter_dimension=tp_dim, tiled=True)
            value = lax.psum_scatter(value, "seq", scatter_dimension=seq_dim, tiled=True)
            return value.astype(F32)

        def rows_of(low_part, high_part):
            parts = [
                part[..., k * quarter : (k + 1) * quarter, :]
                for k in range(2)
                for part in (low_part, high_part)
            ]
            return join(parts, -2)

        down = join([ffn_g[j][u][i] for j in range(pairs) for u in range(2) for i in range(2)], 1)
        up = join(
            [rows_of(ffn_g[j][2][r], ffn_g[j][3][r]) for j in range(pairs) for r in range(4)], 1
        )
        qk = [rows_of(attn_g[j][0][0], attn_g[j][0][1]) for j in range(pairs)]
        vo = [rows_of(attn_g[j][1], attn_g[j][2]) for j in range(pairs)]
        down_grad = scattered(down, 1, 0).T
        up_grad = scattered(up, 1, 0)
        qkv_grad = jnp.stack(
            [
                join([g[:, : 2 * LANE] for g in qk], 1),
                join([g[:, 2 * LANE :] for g in qk], 1),
                join([g[:, : 2 * LANE] for g in vo], 1),
            ]
        )
        qkv_grad = scattered(qkv_grad, 2, 1)
        out_grad = scattered(join([g[:, 2 * LANE :] for g in vo], 1), 1, 0).T
    return (mixed, token_grad, qkv_grad, out_grad, up_grad, down_grad, norm_grads)


def solution(mesh):
    return jax.shard_map(
        body,
        mesh=mesh,
        in_specs=(
            P(("seq", "tp"), None),
            P("seq", None),
            P(None, None, "tp"),
            P("tp", None),
            P(None, "tp"),
            P("tp", None),
            P(),
            P(),
            P(),
            P(),
            P(("seq", "tp"), None),
        ),
        out_specs=(
            P(("seq", "tp"), None),
            P(("seq", "tp"), None),
            P(None, "seq", "tp"),
            P("tp", "seq"),
            P("seq", "tp"),
            P("tp", "seq"),
            P(None, ("seq", "tp")),
        ),
        check_vma=False,
    )
```

```python
import functools

import jax
import jax.numpy as jnp
from jax import lax
from jax.experimental import pallas as pl
from jax.experimental.pallas import tpu as pltpu
from jax.sharding import PartitionSpec as P

HDIM = 64
LANE = 128
BF = jnp.bfloat16
F32 = jnp.float32
SCALE = HDIM ** (-0.5)
MASKED = -1000000000.0
VMEM_MIB = (("attn_fwd", 16), ("ffn_fwd", 20), ("ffn_bwd", 28), ("attn_bwd", 18), ("pack", 12), ("token", 24))


def dot(left, right):
    return jnp.dot(left, right, preferred_element_type=F32)


def dot_nt(left, right):
    return lax.dot_general(left, right, (((1,), (1,)), ((), ())), preferred_element_type=F32)


def everything(ref, scal):
    return ref


class Need:
    def __init__(self, shape, dtype, *parts, pinned=True):
        self.shape, self.dtype, self.parts, self.pinned = tuple(shape), dtype, parts, pinned


def need(array, pinned=True):
    return Need(array.shape, array.dtype, (array, everything, everything), pinned=pinned)


class Loads:
    def __init__(self, needs, refs, bufs, sems, scal):
        self.bufs, self.copies, self.next = bufs, [], 0
        at = 0
        for item, buf in zip(needs, bufs):
            mine = []
            for index, source, target in item.parts:
                copy = pltpu.make_async_copy(
                    source(refs[index], scal), target(buf, scal), sems.at[at]
                )
                copy.start()
                mine.append(copy)
                at += 1
            self.copies.append(mine)

    def take(self):
        self.next += 1
        return self.next - 1

    def get(self, slot):
        for copy in self.copies[slot]:
            copy.wait()
        self.copies[slot] = []
        return self.bufs[slot]

    def pop(self):
        return self.get(self.take())

    def finish(self):
        for slot in range(len(self.copies)):
            self.get(slot)


class Stores:
    def __init__(self, refs, bufs, sems):
        self.refs, self.sems, self.copies = refs, sems, []
        self.bufs = [ref if buf is None else buf for ref, buf in zip(refs, bufs)]
        self.direct = [buf is None for buf in bufs]
        self.next = 0

    def part(self, slot, value, *where):
        self.bufs[slot][where] = value

    def send(self, slot, *where):
        if self.direct[slot]:
            return
        source, target = self.bufs[slot], self.refs[slot]
        if where:
            source, target = source.at[where], target.at[where]
        copy = pltpu.make_async_copy(source, target, self.sems.at[self.next])
        self.next += 1
        copy.start()
        self.copies.append(copy)

    def put(self, slot, value):
        self.bufs[slot][...] = value
        self.send(slot)

    def finish(self):
        for copy in self.copies:
            copy.wait()


def hot(shape, dtype):
    return (shape, dtype, True)


def vmem_of(name):
    for start, size in VMEM_MIB:
        if name.startswith(start):
            return size
    return 16


def call(kernel, needs, outs, scal, small, name, flops, sends=None):
    arrays, parts, pinned = [], [], []
    for item in needs:
        fixed = []
        for array, source, target in item.parts:
            index = next((i for i, a in enumerate(arrays) if a is array), None)
            if index is None:
                index = len(arrays)
                arrays.append(array)
                pinned.append(item.pinned)
            fixed.append((index, source, target))
        parts.append(Need(item.shape, item.dtype, *fixed))
    copies = max(1, sum(len(item.parts) for item in parts))
    sends = max(1, len(outs) if sends is None else sends)
    here = [len(out) == 3 for out in outs]

    def run(*refs):
        refs = list(refs)
        scal_ref = refs.pop(0)
        small_refs = [refs.pop(0) for _ in small]
        in_refs = [refs.pop(0) for _ in arrays]
        out_refs = [refs.pop(0) for _ in outs]
        in_bufs = [refs.pop(0) for _ in parts]
        out_bufs = [None if stays else refs.pop(0) for stays in here]
        in_sems, out_sems = refs
        loads = Loads(parts, in_refs, in_bufs, in_sems, scal_ref)
        stores = Stores(out_refs, out_bufs, out_sems)
        kernel(scal_ref, small_refs, loads, stores)
        loads.finish()
        stores.finish()

    return pl.pallas_call(
        run,
        out_shape=[
            jax.ShapeDtypeStruct(out[0], out[1]) if stays else pltpu.HBM(out[0], out[1])
            for out, stays in zip(outs, here)
        ],
        in_specs=[pl.BlockSpec(memory_space=pltpu.SMEM)]
        + [pl.BlockSpec(memory_space=pltpu.VMEM)] * len(small)
        + [pl.BlockSpec(memory_space=pltpu.HBM if p else pl.ANY) for p in pinned],
        out_specs=[
            pl.BlockSpec(memory_space=pltpu.VMEM if stays else pltpu.HBM) for stays in here
        ],
        scratch_shapes=[pltpu.VMEM(item.shape, item.dtype) for item in parts]
        + [pltpu.VMEM(out[0], out[1]) for out, stays in zip(outs, here) if not stays]
        + [pltpu.SemaphoreType.DMA((copies,)), pltpu.SemaphoreType.DMA((sends,))],
        compiler_params=pltpu.CompilerParams(vmem_limit_bytes=vmem_of(name) * 1024 * 1024),
        cost_estimate=pl.CostEstimate(flops=flops, bytes_accessed=0, transcendentals=0),
        name=name,
    )(
        scal,
        *small,
        *[
            pltpu.with_memory_space_constraint(a, pltpu.HBM) if p else a
            for a, p in zip(arrays, pinned)
        ],
    )


def store_turned(scal, buf, values):
    for block in range(values.shape[1] // LANE):
        start = pl.multiple_of(scal[block] * LANE, LANE)
        buf[pl.ds(start, LANE), :] = values[:, block * LANE : (block + 1) * LANE].T


def block_of(scal, place):
    kind, value = place
    return scal[value] if kind == "table" else value


def columns(place, size, *front):
    def take(ref, scal):
        start = pl.multiple_of(block_of(scal, place) * size, size)
        return ref.at[(*front, slice(None), pl.ds(start, size))]

    return take


def lines(place, size):
    def take(ref, scal):
        start = pl.multiple_of(block_of(scal, place) * size, size)
        return ref.at[pl.ds(start, size), :]

    return take


def lanes_at(start, size):
    return lambda ref, scal: ref.at[:, pl.ds(start, size)]


def lines_at(start, size):
    return lambda ref, scal: ref.at[pl.ds(start, size), :]


def slot_at(*where):
    return lambda ref, scal: ref.at[where]


def stacked_at(index, size):
    def take(ref, scal):
        ref = ref if len(ref.shape) == 2 else ref.at[1]
        return ref.at[pl.ds(index * size, size), :]

    return take


def block_at(row, column, size):
    return lambda ref, scal: ref.at[pl.ds(row * size, size), pl.ds(column * size, size)]


def first_of(ref, scal):
    return ref if len(ref.shape) == 2 else ref.at[0]


def part_of(place):
    def find(scal):
        quarter = block_of(scal, place)
        return quarter // 2, lax.rem(quarter, 2)

    return find


def matrix_at(place, which):
    def take(ref, scal):
        half, pair = part_of(place)(scal)
        index = 1 if which else 2 * pair
        return ref.at[index, :, pl.ds(pl.multiple_of(half * LANE, LANE), LANE)]

    return take


def out_rows_at(place):
    def take(ref, scal):
        half, _ = part_of(place)(scal)
        return ref.at[pl.ds(pl.multiple_of(half * LANE, LANE), LANE), :]

    return take


def piece_lanes(place, which, block, rows):
    def take(buf, scal):
        half, pair = part_of(place)(scal)
        start = pair * 4 * LANE + half * LANE + which * 2 * LANE
        return buf.at[pl.ds(block * rows, rows), pl.ds(pl.multiple_of(start, LANE), LANE)]

    return take


def attn_needs(block, pinned=True, out_only=False):
    if block[0] == "packed":
        pieces = block[1]
        parts = []
        for r, piece in enumerate(pieces):
            for half, array in enumerate(piece):
                parts += [
                    (
                        array,
                        lanes_at(which * LANE, LANE),
                        piece_lanes(("table", 8 + r), which, half, array.shape[0]),
                    )
                    for which in range(1 if out_only else 0, 2)
                ]
        return [Need((pieces[0][0].shape[0], 8 * LANE), BF, *parts, pinned=pinned)]
    _, qkv, out, index = block
    depth, width = qkv.shape[1], out.shape[1]
    place = ("block", index)
    if out_only:
        return [Need((2 * LANE, width), BF, (out, lines(place, 2 * LANE), everything))]
    return [
        Need(
            (depth, 6 * LANE), BF,
            *[
                (qkv, columns(place, 2 * LANE, i), lanes_at(2 * i * LANE, 2 * LANE))
                for i in range(3)
            ],
        ),
        Need((2 * LANE, width), BF, (out, lines(place, 2 * LANE), everything)),
    ]


def up_need(pieces, size, pinned=True):
    parts = []
    for number, piece in enumerate(pieces):
        target = lanes_at(number * size, size)
        if piece[0] == "packed":
            parts.append((piece[1], first_of, target))
        else:
            parts.append((piece[1], columns(piece[3], size), target))
    return Need((pieces[0][-1], len(pieces) * size), BF, *parts, pinned=pinned)


def down_need(pieces, size, pinned=True):
    parts = []
    for number, piece in enumerate(pieces):
        width = piece[-1]
        if piece[0] == "packed":
            for index in range(width // size):
                parts.append(
                    (piece[2], stacked_at(index, size), block_at(number, index, size))
                )
        else:
            parts.append((piece[2], lines(piece[3], size), lines_at(number * size, size)))
    return Need((len(pieces) * size, pieces[0][-1]), BF, *parts, pinned=pinned)


def saved_need(pieces, size):
    parts = [
        (array, lanes_at(index * size, size), lanes_at(number * size, size))
        for number, (array, index) in enumerate(pieces)
    ]
    return Need((pieces[0][0].shape[0], len(pieces) * size), BF, *parts)


def mean_of(values):
    return jnp.mean(values, axis=-1, keepdims=True)


def bias_of(seg_col, seg_row):
    return jnp.where(seg_col == seg_row, 0.0, MASKED)


def cut_kernel(places, scal, small, loads, stores):
    for slot, place in enumerate(places):
        first, second, out = loads.pop(), loads.pop(), loads.pop()
        _, pair = part_of(place)(scal)
        stores.part(slot, first[...], slice(None), slice(0, LANE))

        @pl.when(pair == 0)
        def _():
            stores.part(slot, second[...], slice(None), slice(LANE, 2 * LANE))

        @pl.when(pair == 1)
        def _():
            stores.part(slot, out[...].T, slice(None), slice(LANE, 2 * LANE))

        stores.send(slot)


def pack_kernel(size, scal, small, loads, stores):
    for slot in range(2):
        up, down = loads.pop(), loads.pop()
        stores.part(slot, up[...], 0)
        for index in range(down.shape[1] // size):
            block = down[:, index * size : (index + 1) * size]
            stores.part(slot, block, 1, pl.ds(index * size, size))
        stores.send(slot)


def turn_kernel(scal, small, loads, stores):
    store_turned(scal, stores.bufs[0], small[0][...])
    stores.send(0)


def head_parts(qkv, unit):
    query, key, value = (
        qkv[:, (2 * i + unit) * LANE : (2 * i + unit + 1) * LANE] for i in range(3)
    )
    return query * jnp.asarray(SCALE, BF), key, value


def stacked(pair, lane):
    zero = jnp.zeros_like(pair)
    return jnp.concatenate(
        [jnp.where(lane < HDIM, pair, zero), jnp.where(lane >= HDIM, pair, zero)], axis=0
    )


def attn_fwd_kernel(kind, first, last, scal, small, loads, stores):
    col_ref, row_ref, tokens_ref = small[:3]
    tokens = tokens_ref[...]
    bias = bias_of(col_ref[...], row_ref[...])
    lane = lax.broadcasted_iota(jnp.int32, (1, LANE), 1)
    length = tokens.shape[0]
    weight = loads.pop()
    qkv = dot(tokens, weight[:, : 6 * LANE]).astype(BF)
    stores.put(0, qkv)
    contexts = []
    for unit in range(2):
        query, key, value = head_parts(qkv, unit)
        scores = dot_nt(stacked(key, lane), query)
        probs = []
        for head in range(2):
            mine = scores[head * length : (head + 1) * length] + bias
            peak = jnp.max(mine, axis=0, keepdims=True)
            raw = jnp.exp(mine - peak)
            summed = jnp.sum(raw, axis=0, keepdims=True)
            stores.part(2, peak + jnp.log(summed), pl.ds(2 * unit + head, 1), slice(None))
            probs.append((raw * (1.0 / summed)).astype(BF))
        context = dot(stacked(value, lane).T, jnp.concatenate(probs, axis=0))
        contexts.append(context.astype(BF).T)
    stores.send(2)
    both = jnp.concatenate(contexts, axis=1)
    stores.put(1, both)
    if kind == "whole":
        total = dot(both, loads.pop()[...])
    else:
        total = dot_nt(both, weight[:, 6 * LANE :])
    if not first:
        total = total + small[3][...]
    at = 3
    if not last:
        stores.put(at, total)
        return
    gain_ref, shift_ref = small[-2:]
    pre = tokens.astype(F32) + total
    center = pre - mean_of(pre)
    inv = lax.rsqrt(mean_of(center * center) + 1e-12)
    hat = center * inv
    low = (hat * gain_ref[...] + shift_ref[...]).astype(BF)
    stores.put(at + 2, low)
    stores.put(at, hat)
    stores.put(at + 1, jnp.broadcast_to(inv, (hat.shape[0], LANE)))
    store_turned(scal, stores.bufs[at + 3], low)
    stores.send(at + 3)


def ffn_fwd_kernel(units, first, last, scal, small, loads, stores):
    low = small[0][...]
    total = None
    for number in range(units):
        up = dot(low, loads.pop()[...])
        phi_big = 0.5 + 0.5 * lax.erf(up * (0.5 ** 0.5))
        phi_small = jnp.exp(up * up * -0.5) * 0.3989422804014327
        act = (up * phi_big).astype(BF)
        stores.put(number * 2, act)
        stores.put(number * 2 + 1, (phi_big + up * phi_small).astype(BF))
        part = dot(act, loads.pop()[...])
        total = part if total is None else total + part
    if not first:
        total = total + small[1][...]
    at = units * 2
    if not last:
        stores.put(at, total)
        return
    hat_ref, gain1_ref, shift1_ref, gain2_ref, shift2_ref = small[-5:]
    gain2 = gain2_ref[...]
    pre = hat_ref[...] * gain1_ref[...] + shift1_ref[...] + total
    center = pre - mean_of(pre)
    inv = lax.rsqrt(mean_of(center * center) + 1e-12)
    hat = center * inv
    cot = loads.pop()[...].astype(F32)
    scaled = cot * gain2
    dpre = (scaled - mean_of(scaled) - hat * mean_of(scaled * hat)) * inv
    dffn = dpre.astype(BF)
    stores.put(at + 2, dffn)
    stores.put(at + 1, dpre)
    store_turned(scal, stores.bufs[at + 3], dffn)
    stores.send(at + 3)
    stores.put(at, (hat * gain2 + shift2_ref[...]).astype(BF))
    stores.put(at + 4, jnp.sum(cot * hat, axis=0, keepdims=True))
    stores.put(at + 5, jnp.sum(cot, axis=0, keepdims=True))


def split_rows(stores, slot, where, value, inside=False):
    step = value.shape[0] // 4
    for number in range(4):
        rows = pl.ds(number // 2 * step, step)
        piece = value[number * step : (number + 1) * step]
        if inside:
            stores.part(slot, piece, number % 2, rows)
        else:
            stores.part(slot + number % 2, piece, *where, rows)


def ffn_bwd_kernel(near, has_recv, last, size, scal, small, loads, stores):
    dffn_ref, dffn_t_ref, low_t_ref, acc_ref = small[:4]
    down = dot(dffn_t_ref[...], loads.pop()[...])
    got = [loads.pop() for _ in range(2)] if has_recv else None
    for r in range(4):
        value = down[:, r * size : (r + 1) * size]
        if has_recv:
            value = value + got[r // 2][0, r % 2].astype(F32)
        stores.part(r // 2, value.astype(BF), *((r % 2,) if near else (0, r % 2)))
    if near:
        stores.send(0)
        stores.send(1)
    wd, slope = loads.pop(), loads.pop()
    d_up = (dot_nt(dffn_ref[...], wd[...]) * slope[...].astype(F32)).astype(BF)
    up = dot(low_t_ref[...], d_up)
    for r in range(4):
        value = up[:, r * size : (r + 1) * size]
        if has_recv:
            value = value + got[r // 2][1, r % 2].astype(F32)
        if near:
            split_rows(stores, 2, (r,), value.astype(BF))
        else:
            stores.part(r // 2, value.astype(BF), 1, r % 2)
    if near:
        stores.send(2)
        stores.send(3)
    else:
        stores.send(0)
        stores.send(1)
    total = acc_ref[...] + dot_nt(d_up, loads.pop()[...])
    at = 4 if near else 2
    if not last:
        stores.put(at, total)
        return
    hat_ref, inv_ref, gain_ref = small[4:]
    hat = hat_ref[...]
    scaled = total * gain_ref[...]
    inv = inv_ref[:, :1]
    dpre = (scaled - mean_of(scaled) - hat * mean_of(scaled * hat)) * inv
    datt = dpre.astype(BF)
    stores.put(at + 1, datt)
    stores.put(at, dpre)
    store_turned(scal, stores.bufs[at + 2], datt)
    stores.send(at + 2)
    stores.put(at + 3, jnp.sum(total * hat, axis=0, keepdims=True))
    stores.put(at + 4, jnp.sum(total, axis=0, keepdims=True))


def attn_bwd_kernel(kind, near, has_recv, scal, small, loads, stores):
    col_ref, row_ref, datt_ref, datt_t_ref, tok_t_ref = small
    bias = bias_of(col_ref[...], row_ref[...])
    lane = lax.broadcasted_iota(jnp.int32, (1, LANE), 1)
    qkv, lse = loads.pop(), loads.pop()
    pairs, keys, probs = [], [], []
    length = bias.shape[0]
    for unit in range(2):
        query, key, value = head_parts(qkv, unit)
        keys.append(stacked(key, lane))
        scores = dot_nt(keys[unit], query)
        pairs.append((query, value))
        for head in range(2):
            row = 2 * unit + head
            mine = scores[head * length : (head + 1) * length] + bias
            probs.append(jnp.exp(mine - lse[row : row + 1, :]))
    weight = loads.pop()
    if kind == "whole":
        dctx_all = dot_nt(datt_ref[...], weight[...]).astype(BF)
    else:
        dctx_all = dot(datt_ref[...], weight[:, 6 * LANE :]).astype(BF)
    grads = [[], [], []]

    def chosen(value):
        return jnp.where(lane < HDIM, value[:length], value[length:]).astype(BF)

    for unit in range(2):
        dctx = dctx_all[:, unit * LANE : (unit + 1) * LANE]
        query, value = pairs[unit]
        d_probs = dot_nt(stacked(value, lane), dctx)
        d_scores = []
        for head in range(2):
            prob = probs[2 * unit + head]
            d_prob = d_probs[head * length : (head + 1) * length]
            inner = jnp.sum(prob * d_prob, axis=0, keepdims=True)
            d_scores.append((prob * (d_prob - inner)).astype(BF))
        d_scores = jnp.concatenate(d_scores, axis=0)
        low_probs = jnp.concatenate([p.astype(BF) for p in probs[2 * unit : 2 * unit + 2]], axis=0)
        grads[0].append((dot(keys[unit].T, d_scores) * SCALE).astype(BF).T)
        grads[1].append(chosen(dot(d_scores, query)))
        grads[2].append(chosen(dot(low_probs, dctx)))
    tok_t = tok_t_ref[...]
    both = jnp.concatenate(grads[0] + grads[1] + grads[2], axis=1)
    stores.put(3 if near else 2, both)
    ctx = loads.pop()
    qk = dot(tok_t, both[:, : 4 * LANE])
    if has_recv:
        qk = qk + loads.pop()[...].astype(F32)
    vo = jnp.concatenate(
        [dot(tok_t, both[:, 4 * LANE :]), dot(datt_t_ref[...], ctx[...])], axis=1
    )
    if has_recv:
        vo = vo + loads.pop()[...].astype(F32)
    if near:
        split_rows(stores, 0, (0,), qk.astype(BF), True)
        stores.send(0)
        split_rows(stores, 1, (), vo.astype(BF))
        stores.send(1)
        stores.send(2)
    else:
        stores.put(0, qk.astype(BF))
        stores.put(1, vo.astype(BF))


def token_kernel(kinds, scal, small, loads, stores):
    total = None
    for kind in kinds:
        both, weight = loads.pop(), loads.pop()
        if kind == "whole":
            loads.pop()
        part = dot_nt(both[...], weight[:, : 6 * LANE])
        total = part if total is None else total + part
    stores.put(0, total + loads.pop()[...])


def swap(value, axis, bit):
    count = lax.axis_size(axis)
    return lax.ppermute(value, axis, [(i, i ^ bit) for i in range(count)])


def add(*values):
    total = values[0].astype(F32)
    for value in values[1:]:
        total = total + value.astype(F32)
    return total.astype(BF)


def tie(values, *after):
    return list(lax.optimization_barrier((tuple(values), after))[0])


def sync(values, arrived):
    return lax.optimization_barrier((*values, *arrived))


def join(values, axis=0):
    return jnp.concatenate(values, axis=axis)


def body(
    tokens,
    segment_ids,
    qkv_weight,
    out_weight,
    up_weight,
    down_weight,
    gain_attn,
    shift_attn,
    gain_ffn,
    shift_ffn,
    cotangent,
):
    count, width = tokens.shape
    seq, tp = lax.axis_size("seq"), lax.axis_size("tp")
    me_seq, me_tp = lax.axis_index("seq"), lax.axis_index("tp")
    blocks = width // LANE
    pairs = blocks // 2
    size = up_weight.shape[1] * tp // (4 * pairs)
    fast = seq == blocks and seq == 8 and tp == 4 and qkv_weight.shape[2] == 2 * LANE
    seg = lax.dynamic_slice_in_dim(segment_ids, me_tp, 1, axis=0)
    seg_col = seg.reshape(count, 1)
    gains = [g.reshape(1, width) for g in (gain_attn, shift_attn, gain_ffn, shift_ffn)]
    absolute = jnp.arange(blocks, dtype=jnp.int32)
    half, quarter, eighth = width // 2, width // 4, width // 8
    wide = (count, width)
    work = 2 * count * width
    bit_x, bit_z = me_seq & 1, (me_seq >> 1) & 1

    def over_x(value):
        return swap(value, "seq", 1)

    def over_z(value):
        return swap(value, "seq", 2)

    def over_y(value):
        return swap(value, "tp", 2)

    def over_core(value):
        return swap(value, "tp", 1)

    if fast:
        rel = absolute ^ me_seq
        pos = ((rel >> 1) & 1) * 4 + (rel & 1) * 2 + (rel >> 2)
        mine = me_seq & 3
        scal = jnp.stack(
            [pos[i] for i in range(blocks)] + [mine ^ r for r in range(4)]
        ).astype(jnp.int32)
        table = [("table", 8 + r) for r in range(4)]
        needs = [
            Need((width, LANE), BF, (qkv_weight, matrix_at(table[0], which), everything))
            for which in range(2)
        ]
        needs.append(Need((LANE, width), BF, (out_weight, out_rows_at(table[0]), everything)))
        cuts = call(
            functools.partial(cut_kernel, [table[0]]), needs,
            [((width, 2 * LANE), BF)], scal, [], "cut", 1,
        )
        head_a = over_y(cuts[0])
        weights = tie([up_weight, down_weight], cuts[0])
        needs = []
        for r in (0, 3):
            own = [("whole", *weights, table[r], width)]
            needs += [up_need(own, size), down_need(own, size)]
        packs = call(
            functools.partial(pack_kernel, size), needs,
            [((2, width, size), BF)] * 2, scal, [], "pack", 1,
        )
        ffn_a, ffn_d = over_y(packs[0]), over_y(packs[1])
        (early,) = tie([tokens], packs[1])
        near = [over_core(w) for w in (qkv_weight, out_weight, up_weight, down_weight)]
    else:
        scal = jnp.concatenate([absolute, jnp.zeros((4,), jnp.int32)])
        qkv_all = lax.all_gather(qkv_weight, "tp", axis=2, tiled=True)
        out_all = lax.all_gather(out_weight, "tp", axis=0, tiled=True)
        up_all = lax.all_gather(up_weight, "tp", axis=1, tiled=True)
        down_all = lax.all_gather(down_weight, "tp", axis=0, tiled=True)

    kept, acts = {}, {}
    early = early if fast else tokens

    def attn_fwd(j, total, last):
        needs = attn_needs(heads[j], False)
        outs = [((count, 6 * LANE), BF), ((count, 2 * LANE), BF), ((8, count), F32)]
        if last:
            outs += [
                hot(wide, F32), hot((count, LANE), F32), hot(wide, BF), hot((width, count), BF),
            ]
        else:
            outs.append(hot(wide, F32))
        first = total is None
        small = [seg_col, seg, early] + ([] if first else [total]) + (gains[:2] if last else [])
        res = call(
            functools.partial(attn_fwd_kernel, heads[j][0], first, last),
            needs, outs, scal, small, f"attn_fwd{j}", 1,
        )
        kept[j] = res[:3]
        return res[3:]

    def ffn_fwd(number, group, total, last):
        needs, outs = [], []
        for unit in group:
            pieces = [hidden[piece] for piece in unit]
            needs += [up_need(pieces, size, False), down_need(pieces, size, False)]
            outs += [((count, len(unit) * size), BF)] * 2
        first = total is None
        small = [low] + ([] if first else [total])
        if last:
            needs.append(need(cotangent))
            small += [hat, *gains]
            outs += [
                (wide, BF), hot(wide, F32), hot(wide, BF), hot((width, count), BF),
                hot((1, width), F32), hot((1, width), F32),
            ]
        else:
            outs.append(hot(wide, F32))
        res = call(
            functools.partial(ffn_fwd_kernel, len(group), first, last),
            needs, outs, scal, small, f"ffn_fwd{number}", 8 * work * size * len(group),
        )
        for index, unit in enumerate(group):
            for place, piece in enumerate(unit):
                acts[piece] = [(array, place) for array in res[index * 2 : index * 2 + 2]]
        return res[len(group) * 2 :]

    if fast:
        heads, hidden = {}, {}
        heads[0] = ("whole", qkv_weight, out_weight, 0)
        heads[1] = ("whole", *near[:2], 0)
        for r in range(4):
            hidden[0, r] = ("whole", up_weight, down_weight, table[r], width)
            hidden[1, r] = ("whole", *near[2:], table[r], width)

        def packed(r, both):
            hidden[2, r] = ("packed", both, both, width)
            other = over_core(both)
            hidden[3, r] = ("packed", other, other, width)

        (total,) = attn_fwd(0, None, False)
        (head_a,) = tie([head_a], total, *near)
        head_b, head_c = over_x(head_a), over_z(head_a)
        other_a = over_core(head_a)
        (total,) = attn_fwd(1, total, False)
        tok_t = call(
            turn_kernel, [], [hot((width, count), BF)], scal, tie([tokens], total), "turn", 1
        )[0]
        head_b, head_c = tie([head_b, head_c], tok_t)
        head_d = [over_x(head_c[:half]), over_z(head_b[half:])]
        pieces = [[head_a], [head_b], [head_c], head_d]
        heads[2] = ("packed", pieces)
        others = [[over_core(g) for g in p] for p in pieces[1:]]
        heads[3] = ("packed", [[other_a], *others])
        total, ffn_a = sync([total], [ffn_a])
        (total,) = attn_fwd(2, total, False)
        hat, inv, low, low_t = attn_fwd(3, total, True)
        ffn_b, ffn_c = over_x(ffn_a), over_z(ffn_a)
        packed(0, ffn_a)
        (total,) = ffn_fwd(0, [[(0, r) for r in range(4)]], None, False)
        (total,) = ffn_fwd(1, [[(2, 0), (3, 0)]], total, False)
        (total,) = ffn_fwd(2, [[(1, r) for r in range(4)]], total, False)
        for r, both in zip((1, 2, 3), tie([ffn_b, ffn_c, ffn_d], total)):
            packed(r, both)
        (total,) = ffn_fwd(3, [[(2, r) for r in (1, 2, 3)]], total, False)
        res = ffn_fwd(4, [[(3, r) for r in (1, 2, 3)]], total, True)
    else:
        heads = {j: ("whole", qkv_all, out_all, j) for j in range(pairs)}
        hidden = {
            (k // 4, k % 4): ("whole", up_all, down_all, ("block", k), width)
            for k in range(4 * pairs)
        }
        tok_t = call(
            turn_kernel, [], [hot((width, count), BF)], scal, [tokens], "turn", 1
        )[0]
        total = None
        for j in range(pairs):
            res = attn_fwd(j, total, j == pairs - 1)
            total = res[0]
        hat, inv, low, low_t = res
        total = None
        for j in range(pairs):
            res = ffn_fwd(j, [[(j, r) for r in range(4)]], total, j == pairs - 1)
            total = res[0]
    mixed, d_pre, d_ffn, d_ffn_t, g_gain2, g_shift2 = res

    order = [3, 1, 2, 0] if fast else list(range(pairs))
    ffn_g, attn_g, from_core = {}, {}, {}
    total = d_pre
    for j in order:
        last = j == order[-1]
        here = not fast or j % 2 == 0
        recv = from_core.get(j)
        pieces = [hidden[j, r] for r in range(4)]
        saved = [acts[j, r] for r in range(4)]
        needs = [saved_need([s[0] for s in saved], size)]
        if recv is not None:
            needs += [need(g, False) for g in recv]
        needs += [
            down_need(pieces, size),
            saved_need([s[1] for s in saved], size),
            up_need(pieces, size),
        ]
        small = [d_ffn, d_ffn_t, low_t, total]
        if here:
            outs = [((2, width, size), BF)] * 2 + [((4, half, size), BF)] * 2
        else:
            outs = [((2, 2, width, size), BF)] * 2
        grads = len(outs)
        if last:
            small += [hat, inv, gains[0]]
            outs = outs + [
                (wide, F32), hot(wide, BF), hot((width, count), BF),
                hot((1, width), F32), hot((1, width), F32),
            ]
        else:
            outs = outs + [hot(wide, F32)]
        res = call(
            functools.partial(ffn_bwd_kernel, here, recv is not None, last, size),
            needs, outs, scal, small, f"ffn_bwd{j}", 1,
        )
        ffn_g[j], total = res[:grads], res[grads]
        if not here:
            from_core[j - 1] = [over_core(g) for g in res[:grads]]
        if fast and j == 2:
            down_y = [over_y(g) for g in res[:2]]
            far_x = over_x(res[3])
    d_pre_one, d_att, d_att_t, g_gain1, g_shift1 = res[grads:]

    norm_grads = join([g_gain1, g_shift1, g_gain2, g_shift2])

    def flip(value):
        return join([value[1:], value[:1]])

    def turn_halves(value):
        return join([value[2:], value[:2]])

    def flip_pairs(value):
        return join([value[1:2], value[:1], value[3:], value[2:3]])

    def attn_bwd(j, total):
        here = not fast or j % 2 == 0
        recv = from_core.get(("attn", j))
        needs = [need(kept[j][0]), need(kept[j][2]), *attn_needs(heads[j], True, True)]
        needs.append(need(kept[j][1]))
        if recv is not None:
            needs += [need(g) for g in recv]
        each = 4 * LANE
        if here:
            outs = [((2, half, each), BF), ((half, each), BF), ((half, each), BF)]
        else:
            outs = [((width, each), BF)] * 2
        res = call(
            functools.partial(attn_bwd_kernel, heads[j][0], here, recv is not None),
            needs, outs + [((count, 6 * LANE), BF)],
            scal, [seg_col, seg, total, d_att_t, tok_t], f"attn_bwd{j}", 1,
        )
        attn_g[j] = res[:-1]
        if not here:
            from_core["attn", j - 1] = [over_core(g) for g in res[:-1]]
        d_qkv[j] = res[-1]
        return tie([d_att], res[-1])[0]

    def token_gradient():
        needs = []
        for j in order:
            needs += [need(d_qkv[j]), *attn_needs(heads[j])]
        needs.append(need(d_pre_one))
        return call(
            functools.partial(token_kernel, [heads[j][0] for j in order]),
            needs, [(wide, F32)], scal, [], "token", 1,
        )[0]

    d_qkv = {}

    total = d_att
    if fast:
        near_x = over_x(ffn_g[0][3])
        rest, front = slice(half, None), slice(0, half)

        def down_sum(u, rows):
            return add(ffn_g[0][u][:, rows], down_y[u][:, rows])

        total = attn_bwd(3, total)

        total, down_y[0], far_x = sync([total], [down_y[0], far_x])
        far = add(ffn_g[2][2], flip_pairs(far_x))
        first_z = over_z(
            join([down_sum(0, rest).reshape(4, quarter, size), far[:, quarter:]])
        )
        total = attn_bwd(1, total)
        total = attn_bwd(2, total)

        total, first_z, down_y[1], near_x = sync([total], [first_z, down_y[1], near_x])
        near = add(ffn_g[0][2], flip_pairs(near_x))
        second_z = over_z(
            join([down_sum(1, rest).reshape(4, quarter, size), near[:, quarter:]])
        )
        up_y = over_y(add(far[:, :quarter], turn_halves(first_z[4:])))
        vo_x = over_x(attn_g[2][2])
        qk_y = over_y(attn_g[2][0])
        total = attn_bwd(0, total)
        token_grad = token_gradient()

        def last_sum(value, got):
            return value[..., :eighth, :].astype(F32) + got.astype(F32)

        vo_near_x = over_x(attn_g[0][2])
        vo_lo, vo_x = sync([attn_g[0][1]], [vo_x])
        vo_y = over_y(add(attn_g[2][1], vo_x))
        qk_near, qk_y = sync([attn_g[0][0]], [qk_y])
        qk_y, vo_near_x = sync([qk_y], [vo_near_x])
        qk_y, second_z, token_grad = sync([qk_y], [second_z, token_grad])
        got = [z[:4].reshape(2, half, size) for z in (first_z, second_z)]
        down = join([add(down_sum(u, front), got[1 - u]) for u in range(2)])
        down_x = over_x(down[:, quarter:])
        qk_x = over_x(tie([add(qk_near[1], qk_y[1])], down)[0])
        down, up_y, norm_grads = sync([down], [up_y, norm_grads])
        up = add(near[:, :quarter], turn_halves(second_z[4:]), up_y)
        up_got = swap(up[:, eighth:], "seq", 4)
        norm_next = over_core(norm_grads)
        up, down_x, norm_next = sync([up], [down_x, norm_next])
        down = add(down[:, :quarter], flip_pairs(down_x))
        down_got = swap(down[:, eighth:], "seq", 4)
        norm_grads = norm_grads + norm_next
        norm_next = over_y(norm_grads)
        down, vo_y = sync([down], [vo_y])
        vo = add(vo_lo, vo_near_x, vo_y)
        vo_z = over_z(vo[quarter:])
        vo, norm_next = sync([vo], [norm_next])
        norm_grads = norm_grads + norm_next
        norm_next = over_x(norm_grads)
        vo, qk_x, norm_next = sync([vo], [qk_x, norm_next])
        qk = add(qk_near[0], qk_y[0], qk_x)
        qk_z = over_z(qk[quarter:])
        norm_grads = norm_grads + norm_next
        norm_next = over_z(norm_grads)
        qk, vo_z = sync([qk], [vo_z])
        vo = add(vo[:quarter], vo_z)
        vo_got = swap(vo[eighth:], "seq", 4)
        vo, qk_z, norm_next = sync([vo], [qk_z, norm_next])
        qk = add(qk[:quarter], qk_z)
        qk_got = swap(qk[eighth:], "seq", 4)
        norm_grads = norm_grads + norm_next
        norm_grads = norm_grads + swap(norm_grads, "seq", 4)
        down, up = last_sum(down, down_got), last_sum(up, up_got)
        vo, qk = last_sum(vo, vo_got), last_sum(qk, qk_got)
        share = width // (seq * tp)
        norm_grads = lax.dynamic_slice_in_dim(
            norm_grads, (me_seq * tp + me_tp) * share, share, axis=1
        )

        def ordered(value):
            value = jnp.where(bit_x == 0, value, flip_pairs(value))
            value = jnp.where(bit_z == 0, value, turn_halves(value))
            return join([value[r] for r in range(4)], 1)

        down_grad = ordered(down).T
        up_grad = ordered(up)
        qkv_grad = jnp.stack([qk[:, : 2 * LANE], qk[:, 2 * LANE :], vo[:, : 2 * LANE]])
        out_grad = vo[:, 2 * LANE :].T
    else:
        for j in order:
            total = attn_bwd(j, total)
        token_grad = token_gradient()
        norm_grads = lax.psum_scatter(norm_grads, ("seq", "tp"), scatter_dimension=1, tiled=True)

        def scattered(value, tp_dim, seq_dim):
            value = lax.psum_scatter(value, "tp", scatter_dimension=tp_dim, tiled=True)
            value = lax.psum_scatter(value, "seq", scatter_dimension=seq_dim, tiled=True)
            return value.astype(F32)

        def rows_of(low_part, high_part):
            parts = [
                part[..., k * quarter : (k + 1) * quarter, :]
                for k in range(2)
                for part in (low_part, high_part)
            ]
            return join(parts, -2)

        down = join([ffn_g[j][u][i] for j in range(pairs) for u in range(2) for i in range(2)], 1)
        up = join(
            [rows_of(ffn_g[j][2][r], ffn_g[j][3][r]) for j in range(pairs) for r in range(4)], 1
        )
        qk = [rows_of(attn_g[j][0][0], attn_g[j][0][1]) for j in range(pairs)]
        vo = [rows_of(attn_g[j][1], attn_g[j][2]) for j in range(pairs)]
        down_grad = scattered(down, 1, 0).T
        up_grad = scattered(up, 1, 0)
        qkv_grad = jnp.stack(
            [
                join([g[:, : 2 * LANE] for g in qk], 1),
                join([g[:, 2 * LANE :] for g in qk], 1),
                join([g[:, : 2 * LANE] for g in vo], 1),
            ]
        )
        qkv_grad = scattered(qkv_grad, 2, 1)
        out_grad = scattered(join([g[:, 2 * LANE :] for g in vo], 1), 1, 0).T
    return (mixed, token_grad, qkv_grad, out_grad, up_grad, down_grad, norm_grads)


def solution(mesh):
    return jax.shard_map(
        body,
        mesh=mesh,
        in_specs=(
            P(("seq", "tp"), None),
            P("seq", None),
            P(None, None, "tp"),
            P("tp", None),
            P(None, "tp"),
            P("tp", None),
            P(),
            P(),
            P(),
            P(),
            P(("seq", "tp"), None),
        ),
        out_specs=(
            P(("seq", "tp"), None),
            P(("seq", "tp"), None),
            P(None, "seq", "tp"),
            P("tp", "seq"),
            P("seq", "tp"),
            P("tp", "seq"),
            P(None, ("seq", "tp")),
        ),
        check_vma=False,
    )
```
